32 devices in a mesh: section: 2 (over core), dp: 16 (over z, y, x).
Axes of the slice: x: 2, y: 2, z: 4, core: 2. Of those that a mesh axis runs over, the one named last changes fastest.
Arguments:
- tokens: bfloat16 [32, 512, 384], P('dp'), may hold values from -6 to 6
- sample_ids: int32 [32, 512], P('dp'), may hold values from 0 to 3, never falling along the last dimension, each value on 1 to 256 neighbouring positions
- cotangent: bfloat16 [32, 512, 384], P('dp'), may hold values from -6 to 6
- first_gain: float32 [2, 384], P('section'), may hold values from 0.5 to 1.5
- query_weight: bfloat16 [2, 384, 384], P('section'), may hold values from -0.3125 to 0.3125
- key_weight: bfloat16 [2, 384, 384], P('section'), may hold values from -0.3125 to 0.3125
- value_weight: bfloat16 [2, 384, 384], P('section'), may hold values from -0.3125 to 0.3125
- output_weight: bfloat16 [2, 384, 384], P('section'), may hold values from -2.5 to 2.5
- second_gain: float32 [2, 384], P('section'), may hold values from 0.5 to 1.5
- gate_weight: bfloat16 [2, 384, 1024], P('section'), may hold values from -0.3125 to 0.3125
- up_weight: bfloat16 [2, 384, 1024], P('section'), may hold values from -0.3125 to 0.3125
- down_weight: bfloat16 [2, 1024, 384], P('section'), may hold values from -0.1875 to 0.1875
Outputs:
- layer_outputs: bfloat16 [2, 32, 512, 384], P('section', 'dp')
- input_grads: float32 [2, 32, 512, 384], P('section', 'dp')
- first_gain_grad: float32 [2, 384], P('section')
- query_grad: float32 [2, 384, 384], P('section')
- key_grad: float32 [2, 384, 384], P('section')
- value_grad: float32 [2, 384, 384], P('section')
- output_grad: float32 [2, 384, 384], P('section')
- second_gain_grad: float32 [2, 384], P('section')
- gate_grad: float32 [2, 384, 1024], P('section')
- up_grad: float32 [2, 384, 1024], P('section')
- down_grad: float32 [2, 1024, 384], P('section')
The draws below stay inside these ranges and needn't reach their ends.
Inputs may be any that keep to these rules, and one draw needn't show every extreme that they name: `sample_ids`: within each row the ids never fall; a token attends only to tokens of its own row with the same id; each id covers 1 to 256 positions of a row and one covers exactly 256.
All inputs are finite; a program needn't handle non-finite values.
Results may differ from the reference program's by a relative error of at most 0.02.
Values may be sent and summed in bfloat16 or wider, within the bound.
A program may use at most 128 MiB of HBM per device.

```python
import math
import jax
import jax.numpy as jnp
import numpy as np
from jax import lax

DIM = 384
HEADS = 6
HEAD_DIM = 64
FF = 1024
SEQ = 512
ROWS = 32


def block_levels(rng, shape, cuts, least, top_value):
    def one(axis_at, parts):
        draws = jax.random.uniform(jax.random.fold_in(jax.random.fold_in(rng, 6), axis_at), (parts,), jnp.float32, least / len(cuts), top_value / len(cuts))
        return jnp.repeat(jnp.exp(draws), shape[axis_at] // parts).reshape((-1,) + (1,) * (len(shape) - axis_at - 1))

    factor_of = one(*cuts[0])
    for cut in cuts[1:]:
        factor_of = factor_of * one(*cut)
    return factor_of


def split_up(number_of, total, most, slope):
    weights = [(1 << 20) // math.isqrt(standing ** slope) + 1 for standing in range(2, number_of + 1)]
    surplus, holding = total - most - (number_of - 1), [1] * (number_of - 1)
    while surplus > 0:
        candidates = [i for i in range(number_of - 1) if holding[i] < most]
        pool, budget = sum([weights[i] for i in candidates]), surplus
        for i in candidates:
            addition = min(most - holding[i], max(1, budget * weights[i] // pool), surplus)
            holding[i] = holding[i] + addition
            surplus = surplus - addition
    return np.array([most] + holding)


def ragged_sizes(key, number_of, total, bound, lean):
    if number_of == 2:
        one = jax.random.randint(key, (), max(1, total - bound), min(bound, total - 1) + 1)
        return jnp.stack([one, total - one])
    lengths = jnp.asarray(split_up(number_of, total, bound, lean), jnp.int32)
    twos = (number_of - 1) // 2
    source_of, taker = lengths[1:1 + 2 * twos:2], lengths[2:2 + 2 * twos:2]
    margin = jnp.minimum(source_of - 1, bound - taker)
    passed = jax.random.randint(jax.random.fold_in(key, 1), (twos,), 0, 1 << 20) % (margin + 1)
    lengths = lengths.at[1:1 + 2 * twos:2].set(source_of - passed).at[2:2 + 2 * twos:2].set(taker + passed)
    return lengths[jax.random.permutation(jax.random.fold_in(key, 2), number_of)]


def scatter_about(key, extent, scale, bound, cuts=(), dtype=jnp.bfloat16):
    result = scale * jax.random.normal(key, extent, jnp.float32)
    if cuts:
        result = result * block_levels(key, extent, cuts, -0.22, 0.18)
    return jnp.clip(result, -bound, bound).astype(dtype)


def setup_inputs(seed: int = 0) -> dict:
    streams_of = jax.random.split(jax.random.key(seed), 13)
    tokens = scatter_about(streams_of[0], (ROWS, SEQ, DIM), 1.0, 6.0, ((0, 16),))
    sample_ids = jax.vmap(lambda own: jnp.searchsorted(jnp.cumsum(ragged_sizes(own, 4, SEQ, SEQ // 2, 2)), jnp.arange(SEQ), side="right"))(jax.random.split(streams_of[1], ROWS)).reshape((ROWS, SEQ)).astype(jnp.int32)
    cotangent = scatter_about(streams_of[2], (ROWS, SEQ, DIM), 1.0, 6.0, ((0, 16),))
    first_gain = jnp.clip(1.0 + 0.1 * jax.random.normal(streams_of[3], (2, DIM), jnp.float32), 0.5, 1.5)
    query_weight = scatter_about(streams_of[4], (2, DIM, DIM), DIM ** -0.5, 0.3125, ((0, 2),))
    key_weight = scatter_about(streams_of[5], (2, DIM, DIM), DIM ** -0.5, 0.3125, ((0, 2),))
    value_weight = scatter_about(streams_of[6], (2, DIM, DIM), DIM ** -0.5, 0.3125, ((0, 2),))
    output_weight = scatter_about(streams_of[7], (2, DIM, DIM), (max(DIM // 64, 1)) ** -0.5, 2.5, ((0, 2),))
    second_gain = jnp.clip(1.0 + 0.1 * jax.random.normal(streams_of[8], (2, DIM), jnp.float32), 0.5, 1.5)
    gate_weight = scatter_about(streams_of[9], (2, DIM, FF), DIM ** -0.5, 0.3125, ((0, 2),))
    up_weight = scatter_about(streams_of[10], (2, DIM, FF), DIM ** -0.5, 0.3125, ((0, 2),))
    down_weight = scatter_about(streams_of[11], (2, FF, DIM), FF ** -0.5, 0.1875, ((0, 2),))
    return {"tokens": tokens, "sample_ids": sample_ids, "cotangent": cotangent, "first_gain": first_gain, "query_weight": query_weight, "key_weight": key_weight, "value_weight": value_weight, "output_weight": output_weight, "second_gain": second_gain, "gate_weight": gate_weight, "up_weight": up_weight, "down_weight": down_weight}


@jax.custom_vjp
def low(v):
    return lax.optimization_barrier(v.astype(jnp.bfloat16)).astype(jnp.float32)

@jax.custom_vjp
def low_back(v):
    return v

def low_keep(v):
    return (low(v), None)

def low_pass(kept, grad):
    return (grad,)

def back_keep(v):
    return (v, None)

def back_low(kept, grad):
    return (low(grad),)
low.defvjp(low_keep, low_pass)
low_back.defvjp(back_keep, back_low)
NORM_EPS = 1e-05
MASKED = -1e+30

def product(left, right):
    return jnp.dot(left, right, precision=lax.Precision.HIGHEST)

def normed(values):
    return values * lax.rsqrt(lax.optimization_barrier(jnp.mean(values * values, axis=-1, keepdims=True)) + NORM_EPS)

def layer(hidden_in, ids_block, first_gain, query_weight, key_weight, value_weight, output_weight, second_gain, gate_weight, up_weight, down_weight):
    count_rows = hidden_in.shape[0]
    split = (count_rows, SEQ, HEADS, HEAD_DIM)
    attn_in = low(normed(hidden_in) * first_gain)
    queries = low_back(low(product(attn_in, query_weight))).reshape(split)
    keys_all = low_back(low(product(attn_in, key_weight))).reshape(split)
    values_all = low_back(low(product(attn_in, value_weight))).reshape(split)
    scores = jnp.einsum('rqhd,rkhd->rhqk', queries, keys_all, precision=lax.Precision.HIGHEST) * HEAD_DIM ** (-0.5)
    same = (ids_block[:, :, None] == ids_block[:, None, :])[:, None]
    scores = low_back(jnp.where(same, scores, MASKED))
    probs = low(jax.nn.softmax(scores, axis=-1))
    mixed = jnp.einsum('rhqk,rkhd->rqhd', probs, values_all, precision=lax.Precision.HIGHEST)
    mixed = low_back(low(mixed)).reshape(count_rows, SEQ, DIM)
    after_attn = hidden_in + low_back(product(mixed, output_weight))
    ffn_in = low(normed(after_attn) * second_gain)
    gate_act = low_back(product(ffn_in, gate_weight))
    up_act = low_back(product(ffn_in, up_weight))
    hidden = low(jax.nn.silu(gate_act) * up_act)
    return after_attn + low_back(product(hidden, down_weight))

def reference(tokens, sample_ids, cotangent, first_gain, query_weight, key_weight, value_weight, output_weight, second_gain, gate_weight, up_weight, down_weight):
    stacked = (first_gain, query_weight, key_weight, value_weight, output_weight, second_gain, gate_weight, up_weight, down_weight)
    params_first = tuple((item[0].astype(jnp.float32) for item in stacked))
    params_second = tuple((item[1].astype(jnp.float32) for item in stacked))
    tokens_f = tokens.astype(jnp.float32)
    cot_f = cotangent.astype(jnp.float32)
    groups = ROWS // 8
    ids_groups = sample_ids.reshape(groups, 8, SEQ)

    def whole(tokens_in, delta, first_params, second_params):

        def step(carry, block):
            tok_block, ids_block, delta_block = block
            first_out = jax.checkpoint(layer)(tok_block, ids_block, *first_params)
            sent = low(first_out) + delta_block
            second_out = jax.checkpoint(layer)(low_back(sent), ids_block, *second_params)
            return (carry, (second_out, low(first_out)))
        blocks = (tokens_in.reshape(groups, 8, SEQ, DIM), ids_groups, delta.reshape(groups, 8, SEQ, DIM))
        unused, (second_all, first_all) = lax.scan(step, jnp.zeros((), jnp.float32), blocks)
        return (second_all.reshape(ROWS, SEQ, DIM), first_all.reshape(ROWS, SEQ, DIM))
    delta = jnp.zeros_like(tokens_f)
    final_out, pullback, first_low = jax.vjp(whole, tokens_f, delta, params_first, params_second, has_aux=True)
    grad_tokens, grad_delta, grads_first, grads_second = pullback(cot_f)
    layer_outputs = jnp.stack([first_low, final_out]).astype(jnp.bfloat16)
    input_grads = jnp.stack([grad_tokens, grad_delta]).astype(jnp.float32)
    pairs = [jnp.stack([grads_first[index], grads_second[index]]).astype(jnp.float32) for index in range(9)]
    return (layer_outputs, input_grads, pairs[0], pairs[1], pairs[2], pairs[3], pairs[4], pairs[5], pairs[6], pairs[7], pairs[8])
```

```python
import functools
import types

import jax
import jax.numpy as jnp
from jax import lax
from jax.experimental import pallas as pl
from jax.experimental.pallas import tpu as pltpu
from jax.sharding import PartitionSpec as P

MESH = pl.DeviceIdType.MESH
BF = jnp.bfloat16
F32 = jnp.float32
HEADS = 6
HEAD_DIM = 64
NORM_EPS = 1e-05
MASKED = -1e30
GROUP = 16

SEQ = 512
DIM = 384
FF = 1024
HALF = SEQ // 2
CHUNK = FF // 4
UNITS = 12
UNIT = 2304
SHARE = UNIT // 2
PA = 384
PC = SHARE - 2 * PA

LANDINGS = (
    ("A1", PA // 2), ("A2", PA // 4), ("A3", PA // 4), ("A4", PA // 8),
    ("B1", PA // 2), ("B2", PA // 4), ("B3", PA // 4), ("B4", PA // 8),
    ("C1", PC), ("C2", PC // 2), ("C3", PC // 4), ("C4", PC // 8),
)
LAND = {}
LAND_ROWS = 0
for _name, _rows in LANDINGS:
    LAND[_name] = (LAND_ROWS, _rows)
    LAND_ROWS += _rows

COPIES = ["K"] + [part + str(step) for part in "ABC" for step in range(1, 9)] + ["F"]
SEM = {name: index for index, name in enumerate(COPIES)}


def mm(a, b):
    return lax.dot_general(a, b, (((1,), (0,)), ((), ())), preferred_element_type=F32)


def mm_nt(a, b):
    return lax.dot_general(a, b, (((1,), (1,)), ((), ())), preferred_element_type=F32)


def mm_tn(a, b):
    return lax.dot_general(a, b, (((0,), (0,)), ((), ())), preferred_element_type=F32)


def rsqrt_mean(values):
    return lax.rsqrt(jnp.mean(values * values, axis=-1, keepdims=True) + NORM_EPS)


def rows(start, size):
    return pl.ds(pl.multiple_of(start, 16), size)


class Links:
    def __init__(self, s):
        self.s = s
        self.c = lax.axis_index("section")
        self.dp = lax.axis_index("dp")
        local = lax.rem(self.dp, GROUP)
        self.x = lax.rem(local, 2)
        self.y = lax.rem(lax.div(local, 2), 2)
        self.z = lax.div(local, 4)
        self.middle = (self.z == 1) | (self.z == 2)
        self.end = (self.z == 0) | (self.z == 3)
        self.m = lax.div(self.z, 2)
        self.to_core = (1 - self.c, self.dp)
        self.to_x = (self.c, self.dp + 1 - 2 * self.x)
        self.to_y = (self.c, self.dp + 2 - 4 * self.y)
        self.to_pair = (self.c, self.dp + 4 - 8 * lax.rem(self.z, 2))
        self.to_middle = (self.c, self.dp + 4 - 8 * self.m)
        self.a1 = self.x * (PA // 2)
        self.a2 = self.a1 + self.y * (PA // 4)
        self.a3 = self.a2 + self.m * (PA // 8)
        self.b1 = PA + self.y * (PA // 2)
        self.b2 = self.b1 + self.x * (PA // 4)
        self.b3 = self.b2 + self.m * (PA // 8)
        self.c0 = 2 * PA
        self.c1 = self.c0 + self.m * (PC // 2)
        self.c2 = self.c1 + self.x * (PC // 4)
        self.c3 = self.c2 + self.y * (PC // 8)

    def meet(self):
        barrier = pltpu.get_barrier_semaphore()
        for target in (self.to_core, self.to_x, self.to_y, self.to_pair):
            pl.semaphore_signal(barrier, inc=1, device_id=target, device_id_type=MESH)

        @pl.when(self.middle)
        def _():
            pl.semaphore_signal(barrier, inc=1, device_id=self.to_middle, device_id_type=MESH)

    def met(self):
        barrier = pltpu.get_barrier_semaphore()

        @pl.when(self.middle)
        def _():
            pl.semaphore_wait(barrier, 5)

        @pl.when(self.end)
        def _():
            pl.semaphore_wait(barrier, 4)

    def copy(self, u, name, src, dst, target):
        return pltpu.make_async_remote_copy(
            src_ref=src,
            dst_ref=dst,
            send_sem=self.s.send.at[u, SEM[name]],
            recv_sem=self.s.recv.at[u, SEM[name]],
            device_id=target,
            device_id_type=MESH,
        )

    def down(self, u, name, start, target):
        place, size = LAND[name]
        return self.copy(
            u, name, self.s.part.at[u, rows(start, size)], self.s.land.at[u, rows(place, size)], target
        )

    def up(self, u, name, start, size, target):
        here = self.s.done.at[u, rows(start, size)]
        return self.copy(u, name, here, here, target)

    def arrived(self, u, name, start):
        place, size = LAND[name]
        self.down(u, name, start, self.to_core).wait_recv()
        here = rows(start, size)
        self.s.part[u, here] = self.s.part[u, here] + self.s.land[u, rows(place, size)]

    def finish(self, u, name, start):
        place, size = LAND[name]
        self.down(u, name, start, self.to_core).wait_recv()
        here = rows(start, size)
        self.s.done[u, here] = self.s.part[u, here] + self.s.land[u, rows(place, size)]

    def core_copy(self, u):
        return self.copy(
            u, "K", self.s.own.at[u, rows((1 - self.c) * SHARE, SHARE)], self.s.part.at[u], self.to_core
        )

    def result(self, u):
        place = lax.rem(u, 6)
        return self.s.grads_out.at[place, rows(self.c * SHARE, SHARE)]

    def result_local(self, u):
        return pltpu.make_async_copy(self.s.done.at[u], self.result(u), self.s.send.at[u, SEM["F"]])

    def result_copy(self, u):
        return self.copy(u, "F", self.s.done.at[u], self.result(u), self.to_core)

    def sends(self):
        every, middle, end = None, self.middle, self.end
        return {
            "A1": (lambda u: self.down(u, "A1", (1 - self.x) * (PA // 2), self.to_x), every),
            "A2": (lambda u: self.down(u, "A2", self.a1 + (1 - self.y) * (PA // 4), self.to_y), every),
            "A3": (lambda u: self.down(u, "A3", self.a2, self.to_pair), end),
            "A4": (lambda u: self.down(u, "A4", self.a2 + (1 - self.m) * (PA // 8), self.to_middle), middle),
            "A5": (lambda u: self.up(u, "A5", self.a3, PA // 8, self.to_middle), middle),
            "A6": (lambda u: self.up(u, "A6", self.a2, PA // 4, self.to_pair), middle),
            "A7": (lambda u: self.up(u, "A7", self.a2, PA // 4, self.to_y), every),
            "A8": (lambda u: self.up(u, "A8", self.a1, PA // 2, self.to_x), every),
            "B1": (lambda u: self.down(u, "B1", PA + (1 - self.y) * (PA // 2), self.to_y), every),
            "B2": (lambda u: self.down(u, "B2", self.b1 + (1 - self.x) * (PA // 4), self.to_x), every),
            "B3": (lambda u: self.down(u, "B3", self.b2, self.to_pair), end),
            "B4": (lambda u: self.down(u, "B4", self.b2 + (1 - self.m) * (PA // 8), self.to_middle), middle),
            "B5": (lambda u: self.up(u, "B5", self.b3, PA // 8, self.to_middle), middle),
            "B6": (lambda u: self.up(u, "B6", self.b2, PA // 4, self.to_pair), middle),
            "B7": (lambda u: self.up(u, "B7", self.b2, PA // 4, self.to_x), every),
            "B8": (lambda u: self.up(u, "B8", self.b1, PA // 2, self.to_y), every),
            "C1": (lambda u: self.down(u, "C1", self.c0, self.to_pair), end),
            "C2": (lambda u: self.down(u, "C2", self.c0 + (1 - self.m) * (PC // 2), self.to_middle), middle),
            "C3": (lambda u: self.down(u, "C3", self.c1 + (1 - self.x) * (PC // 4), self.to_x), middle),
            "C4": (lambda u: self.down(u, "C4", self.c2 + (1 - self.y) * (PC // 8), self.to_y), middle),
            "C5": (lambda u: self.up(u, "C5", self.c3, PC // 8, self.to_y), middle),
            "C6": (lambda u: self.up(u, "C6", self.c2, PC // 4, self.to_x), middle),
            "C7": (lambda u: self.up(u, "C7", self.c1, PC // 2, self.to_middle), middle),
            "C8": (lambda u: self.up(u, "C8", self.c0, PC, self.to_pair), middle),
        }

    def stage(self, step, u):
        table = self.sends()

        def start(*names):
            for name in names:
                table[name][0](u).start()

        def landed(name, size, at):
            self.up(u, name, at, size, self.to_core).wait_recv()

        if step == 0:
            self.core_copy(u).wait_recv()
            mine = rows(self.c * SHARE, SHARE)
            self.s.part[u] = self.s.part[u] + self.s.own[u, mine]
            start("A1", "B1")
            pl.when(self.end)(lambda: start("C1"))
        elif step == 1:
            self.arrived(u, "A1", self.a1)
            start("A2")
            self.arrived(u, "B1", self.b1)
            start("B2")

            @pl.when(self.middle)
            def _():
                self.arrived(u, "C1", self.c0)
                start("C2")
        elif step == 2:
            self.arrived(u, "A2", self.a2)
            self.arrived(u, "B2", self.b2)
            pl.when(self.end)(lambda: start("A3", "B3"))

            @pl.when(self.middle)
            def _():
                self.arrived(u, "C2", self.c1)
                start("C3")
        elif step == 3:

            @pl.when(self.middle)
            def _():
                self.arrived(u, "A3", self.a2)
                start("A4")
                self.arrived(u, "B3", self.b2)
                start("B4")
                self.arrived(u, "C3", self.c2)
                start("C4")
        elif step == 4:

            @pl.when(self.middle)
            def _():
                self.finish(u, "A4", self.a3)
                start("A5")
                self.finish(u, "B4", self.b3)
                start("B5")
                self.finish(u, "C4", self.c3)
                start("C5")
        elif step == 5:

            @pl.when(self.middle)
            def _():
                landed("A5", PA // 8, self.a3)
                start("A6", "A7")
                landed("B5", PA // 8, self.b3)
                start("B6", "B7")
                landed("C5", PC // 8, self.c3)
                start("C6")
        elif step == 6:

            @pl.when(self.end)
            def _():
                landed("A6", PA // 4, self.a2)
                start("A7")
                landed("B6", PA // 4, self.b2)
                start("B7")

            @pl.when(self.middle)
            def _():
                landed("C6", PC // 4, self.c2)
                start("C7")
        elif step == 7:
            landed("A7", PA // 4, self.a2)
            start("A8")
            landed("B7", PA // 4, self.b2)
            start("B8")

            @pl.when(self.middle)
            def _():
                landed("C7", PC // 2, self.c1)
                start("C8")
        elif step == 8:
            landed("A8", PA // 2, self.a1)
            landed("B8", PA // 2, self.b1)

            @pl.when(self.end)
            def _():
                landed("C8", PC, self.c0)

            layer = 1 - lax.div(u, 6)
            pl.when(layer == self.c)(lambda: self.result_local(u).start())
            pl.when(layer != self.c)(lambda: self.result_copy(u).start())

    def settle(self, u):
        self.core_copy(u).wait_send()
        for make, who in self.sends().values():
            if who is None:
                make(u).wait_send()
            else:
                pl.when(who)(lambda make=make: make(u).wait_send())
        layer = 1 - lax.div(u, 6)

        @pl.when(layer == self.c)
        def _():
            self.result_local(u).wait()
            self.result_copy(u).wait_recv()

        @pl.when(layer != self.c)
        def _():
            self.result_copy(u).wait_send()

    def sum_gains(self):
        s = self.s
        total = s.gain_sum

        def copy(index, target):
            return pltpu.make_async_remote_copy(
                src_ref=total.at[index],
                dst_ref=s.gain_land.at[index],
                send_sem=s.gain_send.at[index],
                recv_sem=s.gain_recv.at[index],
                device_id=target,
                device_id_type=MESH,
            )

        for index, target in enumerate((self.to_core, self.to_x, self.to_y)):
            one = copy(index, target)
            one.start()
            one.wait_recv()
            total[index + 1] = total[index] + s.gain_land[index]

        @pl.when(self.end)
        def _():
            copy(3, self.to_pair).start()
            copy(5, self.to_pair).wait_recv()
            total[6] = s.gain_land[5]

        @pl.when(self.middle)
        def _():
            copy(3, self.to_pair).wait_recv()
            total[4] = total[3] + s.gain_land[3]
            copy(4, self.to_middle).start()
            copy(4, self.to_middle).wait_recv()
            total[5] = total[4] + s.gain_land[4]
            copy(5, self.to_pair).start()
            total[6] = total[5]

        for index in range(3):
            copy(index, self.to_core).wait_send()

        @pl.when(self.end)
        def _():
            copy(3, self.to_pair).wait_send()

        @pl.when(self.middle)
        def _():
            copy(4, self.to_middle).wait_send()
            copy(5, self.to_pair).wait_send()


WEIGHTS = ("first_gain", "query", "key", "value", "output", "second_gain", "gate", "up", "down")


def kernel(names, lag, *refs):
    s = types.SimpleNamespace(**dict(zip(names, refs)))
    links = Links(s)
    c = links.c
    links.meet()

    token_copy = pltpu.make_async_copy(s.tokens.at[c], s.tok, s.in_sem.at[0])
    token_copy.start()
    cot_copy = pltpu.make_async_copy(s.cotangent.at[c], s.cot, s.in_sem.at[1])
    cot_copy.start()

    def place(name, layer):
        where = {
            "first_gain": lambda: s.gain1.at[layer],
            "query": lambda: s.wqkv.at[layer, :, pl.ds(0, DIM)],
            "key": lambda: s.wqkv.at[layer, :, pl.ds(DIM, DIM)],
            "value": lambda: s.wqkv.at[layer, :, pl.ds(2 * DIM, DIM)],
            "output": lambda: s.wo.at[layer],
            "second_gain": lambda: s.gain2.at[layer],
            "gate": lambda: s.wg.at[layer],
            "up": lambda: s.wu.at[layer],
            "down": lambda: s.wd.at[layer],
        }
        return where[name]()

    def source(name):
        ref = getattr(s, "in_" + name)
        return ref if name.endswith("gain") else ref.at[0]

    def weight_local(name, layer):
        index = WEIGHTS.index(name)
        return pltpu.make_async_copy(source(name), place(name, layer), s.w_sem.at[layer, index])

    def weight_copy(name, layer):
        index = WEIGHTS.index(name)
        return pltpu.make_async_remote_copy(
            src_ref=source(name),
            dst_ref=place(name, layer),
            send_sem=s.w_send.at[index],
            recv_sem=s.w_sem.at[layer, index],
            device_id=links.to_core,
            device_id_type=MESH,
        )

    def need(layer, *which):
        for name in which:
            weight_local(name, layer).wait()

    for name in WEIGHTS:
        weight_local(name, c).start()

    ids = s.sample_ids[pl.ds(c, 1), :].astype(F32)
    count = [jnp.sum(jnp.where(ids == v, 1.0, 0.0), axis=-1, keepdims=True) for v in range(3)]
    first = jnp.where(
        count[0] == HALF,
        0.0,
        jnp.where(
            count[1] == HALF,
            count[0],
            jnp.where(count[2] == HALF, count[0] + count[1], count[0] + count[1] + count[2]),
        ),
    ).astype(jnp.int32)
    down_iota = lax.broadcasted_iota(jnp.int32, (SEQ, SEQ), 0)
    lane_iota = lax.broadcasted_iota(jnp.int32, (SEQ, SEQ), 1)
    moved = down_iota + first
    moved = jnp.where(moved >= SEQ, moved - SEQ, moved)
    perm = jnp.where(lane_iota == moved, 1.0, 0.0)
    ids_down = jnp.sum(perm[HALF:] * ids, axis=-1, keepdims=True)
    s.perm[...] = perm.astype(BF)
    moved = lane_iota + first
    moved = jnp.where(moved >= SEQ, moved - SEQ, moved)
    s.back[...] = jnp.where(down_iota == moved, 1.0, 0.0).astype(BF)
    ids_lane = mm(jnp.broadcast_to(ids, (16, SEQ)).astype(BF), s.back[:, HALF:])[:1]
    s.mask[...] = jnp.where(ids_down == ids_lane, 0.0, MASKED)

    token_copy.wait()
    s.x[0] = mm(s.perm[...], s.tok[...]).astype(BF)
    cot_copy.wait()
    s.dy[...] = mm(s.perm[...], s.cot[...]).astype(BF)

    links.met()
    for name in WEIGHTS:
        weight_copy(name, c).start()

    head0 = lax.broadcasted_iota(jnp.int32, (HALF, 128), 1) < HEAD_DIM

    def of_head(values, h):
        return jnp.where(head0 if h == 0 else ~head0, values, jnp.zeros_like(values))

    def output_row(layer, src, out, sems):
        @pl.when(layer == c)
        def _():
            pltpu.make_async_copy(src, out.at[c], sems.at[0]).start()

        @pl.when(layer != c)
        def _():
            pltpu.make_async_remote_copy(
                src_ref=src, dst_ref=out.at[c], send_sem=sems.at[1], recv_sem=sems.at[2],
                device_id=links.to_core, device_id_type=MESH,
            ).start()

    def output_settle(src, out, sems):
        pltpu.make_async_copy(src, out.at[c], sems.at[0]).wait()
        pltpu.make_async_remote_copy(
            src_ref=src, dst_ref=out.at[c], send_sem=sems.at[1], recv_sem=sems.at[2],
            device_id=links.to_core, device_id_type=MESH,
        ).wait()

    def forward(layer):
        need(layer, "first_gain", "query", "key", "value")
        x = s.x[layer].astype(F32)
        r = rsqrt_mean(x)
        s.r1[layer] = r
        a = (x * r * s.gain1[layer]).astype(BF)
        s.a[layer] = a
        for lo, hi in ((0, 512), (512, 1024), (1024, 1152)):
            part = mm(a, s.wqkv[layer, :, lo:hi])
            if lo == 0:
                s.qkv[layer, :, :DIM] = (part[:, :DIM] * HEAD_DIM ** (-0.5)).astype(BF)
                s.qkv[layer, :, DIM:hi] = part[:, DIM:].astype(BF)
            else:
                s.qkv[layer, :, lo:hi] = part.astype(BF)

        @pl.loop(0, HEADS // 2)
        def _(pair):
            for block in range(2):
                at = pl.ds(block * HALF, HALF)
                q, k, v = [
                    s.qkv[layer, at, pl.ds(pl.multiple_of(pair * 128 + part * DIM, 128), 128)]
                    for part in range(3)
                ]
                o = None
                for h in range(2):
                    score = mm_nt(q, of_head(k, h))
                    if block == 1:
                        score = score + s.mask[...]
                    expo = jnp.exp(score - jnp.max(score, axis=-1, keepdims=True))
                    total = jnp.sum(expo, axis=-1, keepdims=True)
                    prob = (expo * (1.0 / total)).astype(BF)
                    s.p[layer, pair * 4 + block * 2 + h] = prob
                    term = mm(prob, of_head(v, h))
                    o = term if o is None else o + term
                s.o[layer, at, pl.ds(pl.multiple_of(pair * 128, 128), 128)] = o.astype(BF)

        need(layer, "output", "second_gain")
        x1 = x + mm(s.o[layer], s.wo[layer])
        s.x1[layer] = x1
        r = rsqrt_mean(x1)
        s.r2[layer] = r
        s.b[layer] = (x1 * r * s.gain2[layer]).astype(BF)
        need(layer, "gate", "up", "down")

    def hidden(layer, j):
        at = pl.ds(pl.multiple_of(j * CHUNK, CHUNK), CHUNK)
        b = s.b[layer]
        g = mm(b, s.wg[layer, :, at])
        u = mm(b, s.wu[layer, :, at])
        sig = 1.0 / (1.0 + jnp.exp(-g))
        return at, g, u, sig

    def layer_result(layer, y):
        low = y.astype(BF)
        s.y_row[layer] = mm(s.back[...], low).astype(BF)
        output_row(layer, s.y_row.at[layer], s.rows_out, s.y_sem)
        return low

    @pl.loop(0, 2)
    def _(layer):
        forward(layer)

        @pl.when(layer == 0)
        def _():
            s.acc[...] = s.x1[0]

            @pl.loop(0, 4)
            def _(j):
                at, g, u, sig = hidden(0, j)
                f = (g * sig * u).astype(BF)
                s.acc[...] += mm(f, s.wd[0, at, :])

            s.x[1] = layer_result(0, s.acc[...])

    def put(u, start, values):
        size, width = values.shape
        for lo in range(0, width, 128):
            s.own[u, pl.ds(start, size), :] = values[:, lo : lo + 128].astype(BF)
            start += size
        return start

    def put_gain(layer, which, values):
        for i in range(DIM // 128):
            s.gain_sum[0, pl.ds(layer * 8 + which * 4 + i, 1), :] = values[:, i * 128 : (i + 1) * 128]

    def tick(t, closing=False):
        for step in reversed(range(9)):
            u = t - lag * step
            if closing and step == 0 and lag > 0:
                continue

            @pl.when((u >= 0) & (u < UNITS))
            def _(step=step, u=u):
                links.stage(step, u)

    def made(u):
        links.core_copy(u).start()

    s.gain_sum[0] = jnp.zeros((16, 128), F32)

    @pl.loop(0, 2)
    def _(turn):
        layer = 1 - turn
        base = turn * 6
        s.bt[...] = s.b[layer].T
        s.db[...] = jnp.zeros((SEQ, DIM), F32)

        @pl.when(layer == 1)
        def _():
            s.acc[...] = s.x1[1]

        @pl.loop(0, 4)
        def _(j):
            at, g, u, sig = hidden(layer, j)
            silu = g * sig
            f = (silu * u).astype(BF)
            dy = s.dy[...]
            df = mm_nt(dy, s.wd[layer, at, :])
            dg = (df * u * sig * (1.0 + g * (1.0 - sig))).astype(BF)
            du = (df * silu).astype(BF)
            unit = base + j
            nxt = put(unit, 0, mm_tn(f, dy))
            nxt = put(unit, nxt, mm(s.bt[...], dg))
            put(unit, nxt, mm(s.bt[...], du))
            made(unit)
            s.db[...] += mm_nt(dg, s.wg[layer, :, at]) + mm_nt(du, s.wu[layer, :, at])

            @pl.when(layer == 1)
            def _():
                s.acc[...] += mm(f, s.wd[layer, at, :])

            tick(unit)

        @pl.when(layer == 1)
        def _():
            layer_result(1, s.acc[...])

        db = s.db[...]
        r = s.r2[layer]
        normed = s.x1[layer] * r
        put_gain(layer, 1, jnp.sum(db * normed, axis=0, keepdims=True))
        part = db * s.gain2[layer]
        dx1 = s.dy[...].astype(F32) + r * (part - normed * jnp.mean(part * normed, axis=-1, keepdims=True))
        s.dx1[...] = dx1
        low = dx1.astype(BF)
        nxt = put(base + 4, 0, mm_tn(s.o[layer], low))
        s.do[...] = mm_nt(low, s.wo[layer]).astype(BF)

        @pl.loop(0, HEADS // 2)
        def _(pair):
            for block in range(2):
                at = pl.ds(block * HALF, HALF)
                q, k, v = [
                    s.qkv[layer, at, pl.ds(pl.multiple_of(pair * 128 + part * DIM, 128), 128)]
                    for part in range(3)
                ]
                do = s.do[at, pl.ds(pl.multiple_of(pair * 128, 128), 128)]
                dq = dk = dv = None
                for h in range(2):
                    prob = s.p[layer, pair * 4 + block * 2 + h]
                    tv = mm_tn(prob, of_head(do, h))
                    dp = mm_nt(do, of_head(v, h))
                    wide = prob.astype(F32)
                    ds = (wide * (dp - jnp.sum(wide * dp, axis=-1, keepdims=True))).astype(BF)
                    tq = mm(ds, of_head(k, h))
                    tk = mm_tn(ds, of_head(q, h))
                    dq, dk, dv = (tq, tk, tv) if h == 0 else (dq + tq, dk + tk, dv + tv)
                for part, values in enumerate((dq * HEAD_DIM ** (-0.5), dk, dv)):
                    s.dqkv[at, pl.ds(pl.multiple_of(pair * 128 + part * DIM, 128), 128)] = values.astype(BF)

        s.at[...] = s.a[layer].T
        put(base + 4, nxt, mm(s.at[...], s.dqkv[:, :DIM]))
        made(base + 4)
        tick(base + 4)
        nxt = put(base + 5, 0, mm(s.at[...], s.dqkv[:, DIM : 2 * DIM]))
        put(base + 5, nxt, mm(s.at[...], s.dqkv[:, 2 * DIM :]))
        made(base + 5)

        da = mm_nt(s.dqkv[...], s.wqkv[layer])
        r = s.r1[layer]
        normed = s.x[layer].astype(F32) * r
        put_gain(layer, 0, jnp.sum(da * normed, axis=0, keepdims=True))
        part = da * s.gain1[layer]
        dx = s.dx1[...] + r * (part - normed * jnp.mean(part * normed, axis=-1, keepdims=True))
        low = dx.astype(BF)
        s.dy[...] = low
        s.dx_row[layer] = mm(s.back[...], low).astype(BF)
        output_row(layer, s.dx_row.at[layer], s.dx_out, s.dx_sem)
        tick(base + 5)

    links.sum_gains()

    @pl.loop(UNITS, UNITS + 8 * lag)
    def _(t):
        tick(t, closing=True)

    s.gains_out[...] = s.gain_sum[6, pl.ds(pl.multiple_of(c * 8, 8), 8), :]

    @pl.loop(0, UNITS)
    def _(u):
        links.settle(u)

    for index, name in enumerate(WEIGHTS):
        weight_copy(name, c).wait_send()
    output_settle(s.y_row.at[0], s.rows_out, s.y_sem)
    output_settle(s.dx_row.at[0], s.dx_out, s.dx_sem)


def spread_kernel(units, rows_in, dx_in, gains_in, rows_out, dx_out, *outs):
    first, query, key, value, output, second, gate, up, down = outs
    i = pl.program_id(0)

    @pl.when(i < 4)
    def _():
        for p in range(3):
            down[0, :, p * 128 : (p + 1) * 128] = units[0, pl.ds(p * CHUNK, CHUNK), :].astype(F32)
        for p in range(2):
            gate[0, :, p * 128 : (p + 1) * 128] = units[0, pl.ds((2 + p) * DIM, DIM), :].astype(F32)
            up[0, :, p * 128 : (p + 1) * 128] = units[0, pl.ds((4 + p) * DIM, DIM), :].astype(F32)
        rows_out[0] = rows_in[...]
        dx_out[0] = dx_in[...].astype(F32)

    def square(ref, panel):
        for p in range(3):
            ref[0, :, p * 128 : (p + 1) * 128] = units[0, pl.ds((panel + p) * DIM, DIM), :].astype(F32)

    @pl.when(i == 4)
    def _():
        square(output, 0)
        square(query, 3)

    @pl.when(i == 5)
    def _():
        square(key, 0)
        square(value, 3)
        for p in range(3):
            first[:, p * 128 : (p + 1) * 128] = gains_in[p : p + 1, :]
            second[:, p * 128 : (p + 1) * 128] = gains_in[4 + p : 5 + p, :]


def spread(units, rows_in, dx_in, gains):
    part = lambda i: jnp.minimum(i, 3)
    whole3 = pl.BlockSpec((1, DIM, DIM), lambda i: (0, 0, 0))
    vector = pl.BlockSpec((1, DIM), lambda i: (0, 0))
    row_block = lambda: pl.BlockSpec((1, 1, HALF, DIM), lambda i: (0, part(i) // 2, part(i) % 2, 0))
    row_in = lambda: pl.BlockSpec((1, HALF, DIM), lambda i: (part(i) // 2, part(i) % 2, 0))
    wide = lambda: pl.BlockSpec((1, DIM, CHUNK), lambda i: (0, 0, part(i)))
    square = jax.ShapeDtypeStruct((1, DIM, DIM), F32)
    return pl.pallas_call(
        spread_kernel,
        grid=(6,),
        in_specs=[
            pl.BlockSpec((1, UNIT, 128), lambda i: (i, 0, 0)),
            row_in(),
            row_in(),
            pl.BlockSpec((8, 128), lambda i: (0, 0)),
        ],
        out_specs=[
            row_block(), row_block(), vector, whole3, whole3, whole3, whole3, vector, wide(), wide(),
            pl.BlockSpec((1, CHUNK, DIM), lambda i: (0, part(i), 0)),
        ],
        out_shape=[
            jax.ShapeDtypeStruct((1, 2, SEQ, DIM), BF),
            jax.ShapeDtypeStruct((1, 2, SEQ, DIM), F32),
            jax.ShapeDtypeStruct((1, DIM), F32),
            square, square, square, square,
            jax.ShapeDtypeStruct((1, DIM), F32),
            jax.ShapeDtypeStruct((1, DIM, FF), F32),
            jax.ShapeDtypeStruct((1, DIM, FF), F32),
            jax.ShapeDtypeStruct((1, FF, DIM), F32),
        ],
        compiler_params=pltpu.CompilerParams(vmem_limit_bytes=32 * 2**20),
    )(units, rows_in, dx_in, gains)


def layers(lag, tokens, sample_ids, cotangent, *weights):
    anywhere = pl.BlockSpec(memory_space=pl.ANY)
    vmem = pl.BlockSpec(memory_space=pltpu.VMEM)
    inputs = ["tokens", "cotangent"] + ["in_" + name for name in WEIGHTS] + ["sample_ids"]
    outputs = {
        "grads_out": jax.ShapeDtypeStruct((UNITS // 2, UNIT, 128), BF),
        "rows_out": jax.ShapeDtypeStruct((2, SEQ, DIM), BF),
        "dx_out": jax.ShapeDtypeStruct((2, SEQ, DIM), BF),
        "gains_out": jax.ShapeDtypeStruct((8, 128), F32),
    }
    dma = pltpu.SemaphoreType.DMA
    scratch = {
        "tok": pltpu.VMEM((SEQ, DIM), BF),
        "cot": pltpu.VMEM((SEQ, DIM), BF),
        "gain1": pltpu.VMEM((2, 1, DIM), F32),
        "gain2": pltpu.VMEM((2, 1, DIM), F32),
        "wqkv": pltpu.VMEM((2, DIM, 3 * DIM), BF),
        "wo": pltpu.VMEM((2, DIM, DIM), BF),
        "wg": pltpu.VMEM((2, DIM, FF), BF),
        "wu": pltpu.VMEM((2, DIM, FF), BF),
        "wd": pltpu.VMEM((2, FF, DIM), BF),
        "perm": pltpu.VMEM((SEQ, SEQ), BF),
        "back": pltpu.VMEM((SEQ, SEQ), BF),
        "mask": pltpu.VMEM((HALF, HALF), F32),
        "x": pltpu.VMEM((2, SEQ, DIM), BF),
        "a": pltpu.VMEM((2, SEQ, DIM), BF),
        "qkv": pltpu.VMEM((2, SEQ, 3 * DIM), BF),
        "p": pltpu.VMEM((2, 2 * HEADS, HALF, HALF), BF),
        "o": pltpu.VMEM((2, SEQ, DIM), BF),
        "x1": pltpu.VMEM((2, SEQ, DIM), F32),
        "b": pltpu.VMEM((2, SEQ, DIM), BF),
        "r1": pltpu.VMEM((2, SEQ, 1), F32),
        "r2": pltpu.VMEM((2, SEQ, 1), F32),
        "acc": pltpu.VMEM((SEQ, DIM), F32),
        "bt": pltpu.VMEM((DIM, SEQ), BF),
        "at": pltpu.VMEM((DIM, SEQ), BF),
        "db": pltpu.VMEM((SEQ, DIM), F32),
        "dy": pltpu.VMEM((SEQ, DIM), BF),
        "dx1": pltpu.VMEM((SEQ, DIM), F32),
        "do": pltpu.VMEM((SEQ, DIM), BF),
        "dqkv": pltpu.VMEM((SEQ, 3 * DIM), BF),
        "y_row": pltpu.VMEM((2, SEQ, DIM), BF),
        "dx_row": pltpu.VMEM((2, SEQ, DIM), BF),
        "own": pltpu.VMEM((UNITS, UNIT, 128), BF),
        "part": pltpu.VMEM((UNITS, SHARE, 128), BF),
        "land": pltpu.VMEM((UNITS, LAND_ROWS, 128), BF),
        "done": pltpu.VMEM((UNITS, SHARE, 128), BF),
        "gain_sum": pltpu.VMEM((7, 16, 128), F32),
        "gain_land": pltpu.VMEM((6, 16, 128), F32),
        "in_sem": dma((2,)),
        "w_sem": dma((2, len(WEIGHTS))),
        "w_send": dma((len(WEIGHTS),)),
        "send": dma((UNITS, len(COPIES))),
        "recv": dma((UNITS, len(COPIES))),
        "gain_send": dma((6,)),
        "gain_recv": dma((6,)),
        "y_sem": dma((3,)),
        "dx_sem": dma((3,)),
    }
    names = inputs + list(outputs) + list(scratch)
    return pl.pallas_call(
        functools.partial(kernel, names, lag),
        out_shape=list(outputs.values()),
        in_specs=[anywhere] * (len(inputs) - 1) + [vmem],
        out_specs=[anywhere, anywhere, anywhere, vmem],
        scratch_shapes=list(scratch.values()),
        compiler_params=pltpu.CompilerParams(
            collective_id=0, has_side_effects=True, vmem_limit_bytes=62 * 2**20
        ),
        cost_estimate=pl.CostEstimate(flops=15 * 10**9, bytes_accessed=10**7, transcendentals=4 * 10**6),
    )(tokens, cotangent, *weights, sample_ids)


def solution(mesh):
    count = mesh.shape["dp"]

    def per_device(tokens, sample_ids, cotangent, *weights):
        units, rows_out, dx_out, gains = layers(2, tokens, sample_ids, cotangent, *weights)
        outs = spread(units, rows_out, dx_out, gains)
        if count > GROUP:
            members = [[g * GROUP + i for g in range(count // GROUP)] for i in range(GROUP)]
            outs = list(outs[:2]) + list(lax.psum(tuple(outs[2:]), "dp", axis_index_groups=members))
        return tuple(outs)

    matrix = P("section", None, None)
    vector = P("section", None)
    rows4 = P("section", "dp", None, None)
    grads = (vector, matrix, matrix, matrix, matrix, vector, matrix, matrix, matrix)
    return jax.shard_map(
        per_device,
        mesh=mesh,
        in_specs=(P("dp", None, None), P("dp", None), P("dp", None, None)) + grads,
        out_specs=(rows4, rows4) + grads,
        check_vma=False,
    )
```

```python
import functools
import types

import jax
import jax.numpy as jnp
from jax import lax
from jax.experimental import pallas as pl
from jax.experimental.pallas import tpu as pltpu
from jax.sharding import PartitionSpec as P

MESH = pl.DeviceIdType.MESH
BF = jnp.bfloat16
F32 = jnp.float32
HEADS = 6
HEAD_DIM = 64
NORM_EPS = 1e-05
MASKED = -1e30
GROUP = 16

SEQ = 512
DIM = 384
FF = 1024
HALF = SEQ // 2
CHUNK = FF // 4
UNITS = 12
UNIT = 2304
SHARE = UNIT // 2
PIECE = SHARE // 3
SIZES = (PIECE // 2, PIECE // 4, PIECE // 8)
LAND_AT = (0, PIECE // 2, 3 * PIECE // 4, 7 * PIECE // 8)
STAGES = 8

SENT = 3 * sum(SIZES) * 2 + 3 * SIZES[2]


def mm(a, b):
    return lax.dot_general(a, b, (((1,), (0,)), ((), ())), preferred_element_type=F32)


def mm_nt(a, b):
    return lax.dot_general(a, b, (((1,), (1,)), ((), ())), preferred_element_type=F32)


def mm_tn(a, b):
    return lax.dot_general(a, b, (((0,), (0,)), ((), ())), preferred_element_type=F32)


def rsqrt_mean(values):
    return lax.rsqrt(jnp.mean(values * values, axis=-1, keepdims=True) + NORM_EPS)


def rows(start, size):
    return pl.ds(pl.multiple_of(start, 16), size)


class Links:
    def __init__(self, s):
        self.s = s
        self.c = lax.axis_index("section")
        self.dp = lax.axis_index("dp")
        local = lax.rem(self.dp, GROUP)
        x = lax.rem(local, 2)
        y = lax.rem(lax.div(local, 2), 2)
        p = lax.rem(lax.div(local, 4), 2)
        q = lax.div(local, 8)
        c = self.c
        self.to_core = (1 - c, self.dp)
        step_x, step_y = 1 - 2 * x, 2 - 4 * y
        self.to_x = (c, self.dp + step_x)
        self.to_y = (c, self.dp + step_y)
        self.to_p = (c, self.dp + 4 - 8 * p)
        self.to_q = (c, self.dp + 8 - 16 * q)
        along_x, along_y, along_p = (x, self.to_x), (y, self.to_y), (p, self.to_p)
        one = (x + c * (y - x), (c, self.dp + step_x + c * (step_y - step_x)))
        two = (y + c * (x - y), (c, self.dp + step_y + c * (step_x - step_y)))
        orders = ((along_x, along_y, along_p), (along_y, along_x, along_p), (along_p, one, two))
        self.pieces = []
        for index, order in enumerate(orders):
            starts = [index * PIECE]
            for (bit, _), size in zip(order, SIZES):
                starts.append(starts[-1] + bit * size)
            self.pieces.append((index, order, starts))

    def meet(self):
        barrier = pltpu.get_barrier_semaphore()
        for target in (self.to_core, self.to_x, self.to_y, self.to_p, self.to_q):
            pl.semaphore_signal(barrier, inc=1, device_id=target, device_id_type=MESH)

    def met(self):
        pl.semaphore_wait(pltpu.get_barrier_semaphore(), 5)

    def copy(self, u, step, src, dst, target):
        return pltpu.make_async_remote_copy(
            src_ref=src,
            dst_ref=dst,
            send_sem=self.s.sent.at[u],
            recv_sem=self.s.recv.at[u, step],
            device_id=target,
            device_id_type=MESH,
        )

    def landing(self, index, step):
        size = SIZES[min(step, 2)]
        return pl.ds(index * PIECE + LAND_AT[step], size)

    def piece_copy(self, u, piece, step):
        index, order, starts = piece
        s = self.s
        if step < 3:
            (bit, target), size = order[step], SIZES[step]
            src = s.part.at[u, rows(starts[step] + (1 - bit) * size, size)]
            return self.copy(u, step, src, s.land.at[u, self.landing(index, step)], target)
        if step == 3:
            src = s.part.at[u, rows(starts[3], SIZES[2])]
            return self.copy(u, 3, src, s.land.at[u, self.landing(index, 3)], self.to_q)
        back = 6 - step
        here = s.done.at[u, rows(starts[back + 1], SIZES[back])]
        return self.copy(u, step, here, here, order[back][1])

    def arrived(self, u, step):
        size = 3 * SIZES[(0, 1, 2, 2, 2, 1, 0)[step]]
        there = self.s.land.at[u, pl.ds(0, size)]
        self.copy(u, step, there, there, self.to_core).wait_recv()

    def all_sent(self, u):
        here = self.s.own.at[u, pl.ds(0, SENT)]
        self.copy(u, 0, here, here, self.to_core).wait_send()

    def core_copy(self, u):
        return pltpu.make_async_remote_copy(
            src_ref=self.s.own.at[u, rows((1 - self.c) * SHARE, SHARE)],
            dst_ref=self.s.part.at[u],
            send_sem=self.s.core_sent.at[u],
            recv_sem=self.s.core_recv.at[u],
            device_id=self.to_core,
            device_id_type=MESH,
        )

    def result(self, u):
        place = lax.rem(u, 6)
        return self.s.grads_out.at[place, rows(self.c * SHARE, SHARE)]

    def result_local(self, u):
        return pltpu.make_async_copy(self.s.done.at[u], self.result(u), self.s.out_sent.at[u])

    def result_copy(self, u):
        return pltpu.make_async_remote_copy(
            src_ref=self.s.done.at[u],
            dst_ref=self.result(u),
            send_sem=self.s.out_sent.at[u],
            recv_sem=self.s.out_recv.at[u],
            device_id=self.to_core,
            device_id_type=MESH,
        )

    def stage(self, step, u):
        s = self.s
        if step == 0:
            self.core_copy(u).wait_recv()
            s.part[u] = s.part[u] + s.own[u, rows(self.c * SHARE, SHARE)]
        else:
            self.arrived(u, step - 1)
        for piece in self.pieces:
            index, _, starts = piece
            if 1 <= step <= 4:
                here = rows(starts[min(step, 3)], SIZES[min(step - 1, 2)])
                total = s.part[u, here] + s.land[u, self.landing(index, step - 1)]
                if step < 4:
                    s.part[u, here] = total
                else:
                    s.done[u, here] = total
            if step < 7:
                self.piece_copy(u, piece, step).start()
        if step == 7:
            layer = 1 - lax.div(u, 6)
            pl.when(layer == self.c)(lambda: self.result_local(u).start())
            pl.when(layer != self.c)(lambda: self.result_copy(u).start())
            self.core_copy(u).wait_send()
            self.all_sent(u)

    def settle(self, u):
        layer = 1 - lax.div(u, 6)

        @pl.when(layer == self.c)
        def _():
            self.result_local(u).wait()
            self.result_copy(u).wait_recv()

        @pl.when(layer != self.c)
        def _():
            self.result_copy(u).wait_send()

    def sum_gains(self, step):
        s = self.s
        total = s.gain_sum
        targets = (self.to_core, self.to_x, self.to_y, self.to_p, self.to_q)

        def copy(index):
            return pltpu.make_async_remote_copy(
                src_ref=total.at[index],
                dst_ref=s.gain_land.at[index],
                send_sem=s.gain_send.at[index],
                recv_sem=s.gain_recv.at[index],
                device_id=targets[index],
                device_id_type=MESH,
            )

        if step > 0:
            copy(step - 1).wait()
            total[step] = total[step - 1] + s.gain_land[step - 1]
        if step < 5:
            copy(step).start()


WEIGHTS = ("first_gain", "query", "key", "value", "output", "second_gain", "gate", "up", "down")


def kernel(names, lag, *refs):
    s = types.SimpleNamespace(**dict(zip(names, refs)))
    links = Links(s)
    c = links.c
    links.meet()

    token_copy = pltpu.make_async_copy(s.tokens.at[c], s.tok, s.in_sem.at[0])
    token_copy.start()
    cot_copy = pltpu.make_async_copy(s.cotangent.at[c], s.cot, s.in_sem.at[1])
    cot_copy.start()

    def place(name, layer):
        where = {
            "first_gain": lambda: s.gain1.at[layer],
            "query": lambda: s.wqkv.at[layer, :, pl.ds(0, DIM)],
            "key": lambda: s.wqkv.at[layer, :, pl.ds(DIM, DIM)],
            "value": lambda: s.wqkv.at[layer, :, pl.ds(2 * DIM, DIM)],
            "output": lambda: s.wo.at[layer],
            "second_gain": lambda: s.gain2.at[layer],
            "gate": lambda: s.wg.at[layer],
            "up": lambda: s.wu.at[layer],
            "down": lambda: s.wd.at[layer],
        }
        return where[name]()

    def source(name):
        ref = getattr(s, "in_" + name)
        return ref if name.endswith("gain") else ref.at[0]

    def weight_local(name, layer):
        index = WEIGHTS.index(name)
        return pltpu.make_async_copy(source(name), place(name, layer), s.w_sem.at[layer, index])

    def weight_copy(name, layer):
        index = WEIGHTS.index(name)
        return pltpu.make_async_remote_copy(
            src_ref=source(name),
            dst_ref=place(name, layer),
            send_sem=s.w_send.at[index],
            recv_sem=s.w_sem.at[layer, index],
            device_id=links.to_core,
            device_id_type=MESH,
        )

    def need(layer, *which):
        for name in which:
            weight_local(name, layer).wait()

    for name in WEIGHTS:
        weight_local(name, c).start()

    ids = s.sample_ids[pl.ds(c, 1), :].astype(F32)
    count = [jnp.sum(jnp.where(ids == v, 1.0, 0.0), axis=-1, keepdims=True) for v in range(3)]
    first = jnp.where(
        count[0] == HALF,
        0.0,
        jnp.where(
            count[1] == HALF,
            count[0],
            jnp.where(count[2] == HALF, count[0] + count[1], count[0] + count[1] + count[2]),
        ),
    ).astype(jnp.int32)
    down_iota = lax.broadcasted_iota(jnp.int32, (SEQ, SEQ), 0)
    lane_iota = lax.broadcasted_iota(jnp.int32, (SEQ, SEQ), 1)
    moved = down_iota + first
    moved = jnp.where(moved >= SEQ, moved - SEQ, moved)
    perm = jnp.where(lane_iota == moved, 1.0, 0.0)
    ids_down = jnp.sum(perm[HALF:] * ids, axis=-1, keepdims=True)
    s.perm[...] = perm.astype(BF)
    moved = lane_iota + first
    moved = jnp.where(moved >= SEQ, moved - SEQ, moved)
    s.back[...] = jnp.where(down_iota == moved, 1.0, 0.0).astype(BF)
    ids_lane = mm(jnp.broadcast_to(ids, (16, SEQ)).astype(BF), s.back[:, HALF:])[:1]
    s.mask[...] = jnp.where(ids_down == ids_lane, 0.0, MASKED)

    token_copy.wait()
    s.x[0] = mm(s.perm[...], s.tok[...]).astype(BF)
    cot_copy.wait()
    s.dy[...] = mm(s.perm[...], s.cot[...]).astype(BF)

    links.met()
    for name in WEIGHTS:
        weight_copy(name, c).start()

    head0 = lax.broadcasted_iota(jnp.int32, (HALF, 128), 1) < HEAD_DIM

    def of_head(values, h):
        return jnp.where(head0 if h == 0 else ~head0, values, jnp.zeros_like(values))

    def output_row(layer, src, out, sems):
        @pl.when(layer == c)
        def _():
            pltpu.make_async_copy(src, out.at[c], sems.at[0]).start()

        @pl.when(layer != c)
        def _():
            pltpu.make_async_remote_copy(
                src_ref=src, dst_ref=out.at[c], send_sem=sems.at[1], recv_sem=sems.at[2],
                device_id=links.to_core, device_id_type=MESH,
            ).start()

    def output_settle(src, out, sems):
        pltpu.make_async_copy(src, out.at[c], sems.at[0]).wait()
        pltpu.make_async_remote_copy(
            src_ref=src, dst_ref=out.at[c], send_sem=sems.at[1], recv_sem=sems.at[2],
            device_id=links.to_core, device_id_type=MESH,
        ).wait()

    def forward(layer):
        need(layer, "first_gain", "query", "key", "value")
        x = s.x[layer].astype(F32)
        r = rsqrt_mean(x)
        s.r1[layer] = r
        a = (x * r * s.gain1[layer]).astype(BF)
        s.a[layer] = a
        for lo, hi in ((0, 512), (512, 1024), (1024, 1152)):
            part = mm(a, s.wqkv[layer, :, lo:hi])
            if lo == 0:
                s.qkv[layer, :, :DIM] = (part[:, :DIM] * HEAD_DIM ** (-0.5)).astype(BF)
                s.qkv[layer, :, DIM:hi] = part[:, DIM:].astype(BF)
            else:
                s.qkv[layer, :, lo:hi] = part.astype(BF)

        @pl.loop(0, HEADS // 2)
        def _(pair):
            for block in range(2):
                at = pl.ds(block * HALF, HALF)
                q, k, v = [
                    s.qkv[layer, at, pl.ds(pl.multiple_of(pair * 128 + part * DIM, 128), 128)]
                    for part in range(3)
                ]
                o = None
                for h in range(2):
                    score = mm_nt(q, of_head(k, h))
                    if block == 1:
                        score = score + s.mask[...]
                    expo = jnp.exp(score - jnp.max(score, axis=-1, keepdims=True))
                    total = jnp.sum(expo, axis=-1, keepdims=True)
                    prob = (expo * (1.0 / total)).astype(BF)
                    s.p[layer, pair * 4 + block * 2 + h] = prob
                    term = mm(prob, of_head(v, h))
                    o = term if o is None else o + term
                s.o[layer, at, pl.ds(pl.multiple_of(pair * 128, 128), 128)] = o.astype(BF)

        need(layer, "output", "second_gain")
        x1 = x + mm(s.o[layer], s.wo[layer])
        s.x1[layer] = x1
        r = rsqrt_mean(x1)
        s.r2[layer] = r
        s.b[layer] = (x1 * r * s.gain2[layer]).astype(BF)
        need(layer, "gate", "up", "down")

    def hidden(layer, j):
        at = pl.ds(pl.multiple_of(j * CHUNK, CHUNK), CHUNK)
        b = s.b[layer]
        g = mm(b, s.wg[layer, :, at])
        u = mm(b, s.wu[layer, :, at])
        sig = 1.0 / (1.0 + jnp.exp(-g))
        return at, g, u, sig

    def layer_result(layer, y):
        low = y.astype(BF)
        s.y_row[layer] = mm(s.back[...], low).astype(BF)
        output_row(layer, s.y_row.at[layer], s.rows_out, s.y_sem)
        return low

    @pl.loop(0, 2)
    def _(layer):
        forward(layer)

        @pl.when(layer == 0)
        def _():
            s.acc[...] = s.x1[0]

            @pl.loop(0, 4)
            def _(j):
                at, g, u, sig = hidden(0, j)
                f = (g * sig * u).astype(BF)
                s.acc[...] += mm(f, s.wd[0, at, :])

            s.x[1] = layer_result(0, s.acc[...])

    def put(u, start, values):
        size, width = values.shape
        for lo in range(0, width, 128):
            s.own[u, pl.ds(start, size), :] = values[:, lo : lo + 128].astype(BF)
            start += size
        return start

    def put_gain(layer, which, values):
        for i in range(DIM // 128):
            s.gain_sum[0, pl.ds(layer * 8 + which * 4 + i, 1), :] = values[:, i * 128 : (i + 1) * 128]

    def tick(t, odd):
        for step in reversed(range(STAGES)):
            wait = 2 + lag * step
            if wait % 2 != odd:
                continue
            u = lax.div(2 * t + odd - wait, 2)

            @pl.when((2 * t + odd >= wait) & (u < UNITS))
            def _(step=step, u=u):
                links.stage(step, u)

    def made(u):
        links.core_copy(u).start()

    s.gain_sum[0] = jnp.zeros((16, 128), F32)

    @pl.loop(0, 2)
    def _(turn):
        layer = 1 - turn
        base = turn * 6
        s.bt[...] = s.b[layer].T
        s.db[...] = jnp.zeros((SEQ, DIM), F32)

        @pl.when(layer == 1)
        def _():
            s.acc[...] = s.x1[1]

        @pl.loop(0, 4)
        def _(j):
            at, g, u, sig = hidden(layer, j)
            silu = g * sig
            f = (silu * u).astype(BF)
            dy = s.dy[...]
            df = mm_nt(dy, s.wd[layer, at, :])
            dg = (df * u * sig * (1.0 + g * (1.0 - sig))).astype(BF)
            du = (df * silu).astype(BF)
            unit = base + j
            tick(unit, 0)
            nxt = put(unit, 0, mm_tn(f, dy))
            nxt = put(unit, nxt, mm(s.bt[...], dg))
            put(unit, nxt, mm(s.bt[...], du))
            made(unit)
            s.db[...] += mm_nt(dg, s.wg[layer, :, at]) + mm_nt(du, s.wu[layer, :, at])

            @pl.when(layer == 1)
            def _():
                s.acc[...] += mm(f, s.wd[layer, at, :])

            tick(unit, 1)

        @pl.when(layer == 1)
        def _():
            layer_result(1, s.acc[...])

        db = s.db[...]
        r = s.r2[layer]
        normed = s.x1[layer] * r
        put_gain(layer, 1, jnp.sum(db * normed, axis=0, keepdims=True))
        part = db * s.gain2[layer]
        dx1 = s.dy[...].astype(F32) + r * (part - normed * jnp.mean(part * normed, axis=-1, keepdims=True))
        s.dx1[...] = dx1
        low = dx1.astype(BF)
        nxt = put(base + 4, 0, mm_tn(s.o[layer], low))
        s.do[...] = mm_nt(low, s.wo[layer]).astype(BF)

        @pl.loop(0, HEADS // 2)
        def _(pair):
            for block in range(2):
                at = pl.ds(block * HALF, HALF)
                q, k, v = [
                    s.qkv[layer, at, pl.ds(pl.multiple_of(pair * 128 + part * DIM, 128), 128)]
                    for part in range(3)
                ]
                do = s.do[at, pl.ds(pl.multiple_of(pair * 128, 128), 128)]
                dq = dk = dv = None
                for h in range(2):
                    prob = s.p[layer, pair * 4 + block * 2 + h]
                    tv = mm_tn(prob, of_head(do, h))
                    dp = mm_nt(do, of_head(v, h))
                    wide = prob.astype(F32)
                    ds = (wide * (dp - jnp.sum(wide * dp, axis=-1, keepdims=True))).astype(BF)
                    tq = mm(ds, of_head(k, h))
                    tk = mm_tn(ds, of_head(q, h))
                    dq, dk, dv = (tq, tk, tv) if h == 0 else (dq + tq, dk + tk, dv + tv)
                for part, values in enumerate((dq * HEAD_DIM ** (-0.5), dk, dv)):
                    s.dqkv[at, pl.ds(pl.multiple_of(pair * 128 + part * DIM, 128), 128)] = values.astype(BF)

        s.at[...] = s.a[layer].T
        put(base + 4, nxt, mm(s.at[...], s.dqkv[:, :DIM]))
        tick(base + 4, 0)
        made(base + 4)
        tick(base + 4, 1)
        nxt = put(base + 5, 0, mm(s.at[...], s.dqkv[:, DIM : 2 * DIM]))
        put(base + 5, nxt, mm(s.at[...], s.dqkv[:, 2 * DIM :]))
        tick(base + 5, 0)
        made(base + 5)

        da = mm_nt(s.dqkv[...], s.wqkv[layer])
        r = s.r1[layer]
        normed = s.x[layer].astype(F32) * r
        put_gain(layer, 0, jnp.sum(da * normed, axis=0, keepdims=True))
        part = da * s.gain1[layer]
        dx = s.dx1[...] + r * (part - normed * jnp.mean(part * normed, axis=-1, keepdims=True))
        low = dx.astype(BF)
        s.dy[...] = low
        s.dx_row[layer] = mm(s.back[...], low).astype(BF)
        output_row(layer, s.dx_row.at[layer], s.dx_out, s.dx_sem)
        tick(base + 5, 1)

    last = 2 * (UNITS - 1) + 2 + lag * (STAGES - 1)

    @pl.loop(UNITS, max(last // 2, UNITS + 10) + 1)
    def _(t):
        for odd in range(2):
            tick(t, odd)
        for step in range(6):

            @pl.when(t == UNITS + 2 * step)
            def _(step=step):
                links.sum_gains(step)

    s.gains_out[...] = s.gain_sum[5, pl.ds(pl.multiple_of(c * 8, 8), 8), :]

    @pl.loop(0, UNITS)
    def _(u):
        links.settle(u)

    for index, name in enumerate(WEIGHTS):
        weight_copy(name, c).wait_send()
    output_settle(s.y_row.at[0], s.rows_out, s.y_sem)
    output_settle(s.dx_row.at[0], s.dx_out, s.dx_sem)


def spread_kernel(units, rows_in, dx_in, gains_in, rows_out, dx_out, *outs):
    first, query, key, value, output, second, gate, up, down = outs
    i = pl.program_id(0)

    @pl.when(i < 4)
    def _():
        for p in range(3):
            down[0, :, p * 128 : (p + 1) * 128] = units[0, pl.ds(p * CHUNK, CHUNK), :].astype(F32)
        for p in range(2):
            gate[0, :, p * 128 : (p + 1) * 128] = units[0, pl.ds((2 + p) * DIM, DIM), :].astype(F32)
            up[0, :, p * 128 : (p + 1) * 128] = units[0, pl.ds((4 + p) * DIM, DIM), :].astype(F32)
        rows_out[0] = rows_in[...]
        dx_out[0] = dx_in[...].astype(F32)

    def square(ref, panel):
        for p in range(3):
            ref[0, :, p * 128 : (p + 1) * 128] = units[0, pl.ds((panel + p) * DIM, DIM), :].astype(F32)

    @pl.when(i == 4)
    def _():
        square(output, 0)
        square(query, 3)

    @pl.when(i == 5)
    def _():
        square(key, 0)
        square(value, 3)
        for p in range(3):
            first[:, p * 128 : (p + 1) * 128] = gains_in[p : p + 1, :]
            second[:, p * 128 : (p + 1) * 128] = gains_in[4 + p : 5 + p, :]


def spread(units, rows_in, dx_in, gains):
    part = lambda i: jnp.minimum(i, 3)
    whole3 = pl.BlockSpec((1, DIM, DIM), lambda i: (0, 0, 0))
    vector = pl.BlockSpec((1, DIM), lambda i: (0, 0))
    row_block = lambda: pl.BlockSpec((1, 1, HALF, DIM), lambda i: (0, part(i) // 2, part(i) % 2, 0))
    row_in = lambda: pl.BlockSpec((1, HALF, DIM), lambda i: (part(i) // 2, part(i) % 2, 0))
    wide = lambda: pl.BlockSpec((1, DIM, CHUNK), lambda i: (0, 0, part(i)))
    square = jax.ShapeDtypeStruct((1, DIM, DIM), F32)
    return pl.pallas_call(
        spread_kernel,
        grid=(6,),
        in_specs=[
            pl.BlockSpec((1, UNIT, 128), lambda i: (i, 0, 0)),
            row_in(),
            row_in(),
            pl.BlockSpec((8, 128), lambda i: (0, 0)),
        ],
        out_specs=[
            row_block(), row_block(), vector, whole3, whole3, whole3, whole3, vector, wide(), wide(),
            pl.BlockSpec((1, CHUNK, DIM), lambda i: (0, part(i), 0)),
        ],
        out_shape=[
            jax.ShapeDtypeStruct((1, 2, SEQ, DIM), BF),
            jax.ShapeDtypeStruct((1, 2, SEQ, DIM), F32),
            jax.ShapeDtypeStruct((1, DIM), F32),
            square, square, square, square,
            jax.ShapeDtypeStruct((1, DIM), F32),
            jax.ShapeDtypeStruct((1, DIM, FF), F32),
            jax.ShapeDtypeStruct((1, DIM, FF), F32),
            jax.ShapeDtypeStruct((1, FF, DIM), F32),
        ],
        compiler_params=pltpu.CompilerParams(vmem_limit_bytes=62 * 2**20),
    )(units, rows_in, dx_in, gains)


def layers(lag, tokens, sample_ids, cotangent, *weights):
    anywhere = pl.BlockSpec(memory_space=pl.ANY)
    vmem = pl.BlockSpec(memory_space=pltpu.VMEM)
    inputs = ["tokens", "cotangent"] + ["in_" + name for name in WEIGHTS] + ["sample_ids"]
    outputs = {
        "grads_out": jax.ShapeDtypeStruct((UNITS // 2, UNIT, 128), BF),
        "rows_out": jax.ShapeDtypeStruct((2, SEQ, DIM), BF),
        "dx_out": jax.ShapeDtypeStruct((2, SEQ, DIM), BF),
        "gains_out": jax.ShapeDtypeStruct((8, 128), F32),
    }
    dma = pltpu.SemaphoreType.DMA
    scratch = {
        "tok": pltpu.VMEM((SEQ, DIM), BF),
        "cot": pltpu.VMEM((SEQ, DIM), BF),
        "gain1": pltpu.VMEM((2, 1, DIM), F32),
        "gain2": pltpu.VMEM((2, 1, DIM), F32),
        "wqkv": pltpu.VMEM((2, DIM, 3 * DIM), BF),
        "wo": pltpu.VMEM((2, DIM, DIM), BF),
        "wg": pltpu.VMEM((2, DIM, FF), BF),
        "wu": pltpu.VMEM((2, DIM, FF), BF),
        "wd": pltpu.VMEM((2, FF, DIM), BF),
        "perm": pltpu.VMEM((SEQ, SEQ), BF),
        "back": pltpu.VMEM((SEQ, SEQ), BF),
        "mask": pltpu.VMEM((HALF, HALF), F32),
        "x": pltpu.VMEM((2, SEQ, DIM), BF),
        "a": pltpu.VMEM((2, SEQ, DIM), BF),
        "qkv": pltpu.VMEM((2, SEQ, 3 * DIM), BF),
        "p": pltpu.VMEM((2, 2 * HEADS, HALF, HALF), BF),
        "o": pltpu.VMEM((2, SEQ, DIM), BF),
        "x1": pltpu.VMEM((2, SEQ, DIM), F32),
        "b": pltpu.VMEM((2, SEQ, DIM), BF),
        "r1": pltpu.VMEM((2, SEQ, 1), F32),
        "r2": pltpu.VMEM((2, SEQ, 1), F32),
        "acc": pltpu.VMEM((SEQ, DIM), F32),
        "bt": pltpu.VMEM((DIM, SEQ), BF),
        "at": pltpu.VMEM((DIM, SEQ), BF),
        "db": pltpu.VMEM((SEQ, DIM), F32),
        "dy": pltpu.VMEM((SEQ, DIM), BF),
        "dx1": pltpu.VMEM((SEQ, DIM), F32),
        "do": pltpu.VMEM((SEQ, DIM), BF),
        "dqkv": pltpu.VMEM((SEQ, 3 * DIM), BF),
        "y_row": pltpu.VMEM((2, SEQ, DIM), BF),
        "dx_row": pltpu.VMEM((2, SEQ, DIM), BF),
        "own": pltpu.VMEM((UNITS, UNIT, 128), BF),
        "part": pltpu.VMEM((UNITS, SHARE, 128), BF),
        "land": pltpu.VMEM((UNITS, SHARE, 128), BF),
        "done": pltpu.VMEM((UNITS, SHARE, 128), BF),
        "gain_sum": pltpu.VMEM((6, 16, 128), F32),
        "gain_land": pltpu.VMEM((5, 16, 128), F32),
        "in_sem": dma((2,)),
        "w_sem": dma((2, len(WEIGHTS))),
        "w_send": dma((len(WEIGHTS),)),
        "sent": dma((UNITS,)),
        "recv": dma((UNITS, 7)),
        "core_sent": dma((UNITS,)),
        "core_recv": dma((UNITS,)),
        "out_sent": dma((UNITS,)),
        "out_recv": dma((UNITS,)),
        "gain_send": dma((5,)),
        "gain_recv": dma((5,)),
        "y_sem": dma((3,)),
        "dx_sem": dma((3,)),
    }
    names = inputs + list(outputs) + list(scratch)
    return pl.pallas_call(
        functools.partial(kernel, names, lag),
        out_shape=list(outputs.values()),
        in_specs=[anywhere] * (len(inputs) - 1) + [vmem],
        out_specs=[anywhere, anywhere, anywhere, vmem],
        scratch_shapes=list(scratch.values()),
        compiler_params=pltpu.CompilerParams(
            collective_id=0, has_side_effects=True, vmem_limit_bytes=62 * 2**20
        ),
        cost_estimate=pl.CostEstimate(flops=15 * 10**9, bytes_accessed=10**7, transcendentals=4 * 10**6),
    )(tokens, cotangent, *weights, sample_ids)


def solution(mesh):
    count = mesh.shape["dp"]

    def per_device(tokens, sample_ids, cotangent, *weights):
        units, rows_out, dx_out, gains = layers(3, tokens, sample_ids, cotangent, *weights)
        outs = spread(units, rows_out, dx_out, gains)
        if count > GROUP:
            members = [[g * GROUP + i for g in range(count // GROUP)] for i in range(GROUP)]
            outs = list(outs[:2]) + list(lax.psum(tuple(outs[2:]), "dp", axis_index_groups=members))
        return tuple(outs)

    matrix = P("section", None, None)
    vector = P("section", None)
    rows4 = P("section", "dp", None, None)
    grads = (vector, matrix, matrix, matrix, matrix, vector, matrix, matrix, matrix)
    return jax.shard_map(
        per_device,
        mesh=mesh,
        in_specs=(P("dp", None, None), P("dp", None), P("dp", None, None)) + grads,
        out_specs=(rows4, rows4) + grads,
        check_vma=False,
    )
```

```python
import functools
import types

import jax
import jax.numpy as jnp
from jax import lax
from jax.experimental import pallas as pl
from jax.experimental.pallas import tpu as pltpu
from jax.sharding import PartitionSpec as P

MESH = pl.DeviceIdType.MESH
BF = jnp.bfloat16
F32 = jnp.float32
HEADS = 6
HEAD_DIM = 64
NORM_EPS = 1e-05
MASKED = -1e30
GROUP = 16

SEQ = 512
DIM = 384
FF = 1024
HALF = SEQ // 2
CHUNK = FF // 4
UNITS = 12
UNIT = 2304
SHARE = UNIT // 2
PIECE = SHARE // 3
SLOTS = 15
WHEN = (
    (2, 6, 11, 17, 21, 25, 34, 52),
    (4, 8, 13, 17, 22, 28, 37, 58),
    (6, 12, 16, 20, 24, 29, 40, 50),
    (8, 12, 17, 21, 25, 35, 46, 61),
    (14, 18, 22, 26, 31, 37, 44, 63),
    (15, 19, 24, 28, 33, 40, 48, 69),
)
HALVES = (PIECE // 2, PIECE // 4, PIECE // 8)
STAGES = 8
FLAT = (PIECE // 2, PIECE // 4, PIECE // 4, PIECE // 4, PIECE // 4, PIECE // 4, PIECE // 2)
TALL = (PIECE // 2, PIECE // 4, PIECE // 8, PIECE // 8, PIECE // 8, PIECE // 4, PIECE // 2)
FLAT_LAND = sum(FLAT[:4])
LAND_ROWS = 2 * FLAT_LAND + sum(TALL[:4])


def mm(a, b):
    return lax.dot_general(a, b, (((1,), (0,)), ((), ())), preferred_element_type=F32)


def mm_nt(a, b):
    return lax.dot_general(a, b, (((1,), (1,)), ((), ())), preferred_element_type=F32)


def mm_tn(a, b):
    return lax.dot_general(a, b, (((0,), (0,)), ((), ())), preferred_element_type=F32)


def rsqrt_mean(values):
    return lax.rsqrt(jnp.mean(values * values, axis=-1, keepdims=True) + NORM_EPS)


PARTS = [(pair, block) for pair in range(HEADS // 2) for block in range(2)]


def lanes(pair, part=0):
    return pl.ds(part * DIM + pair * 2 * HEAD_DIM, 2 * HEAD_DIM)


def rows(start, size):
    return pl.ds(pl.multiple_of(start, 16), size)


class Links:
    def __init__(self, s):
        self.s = s
        self.c = lax.axis_index("section")
        self.dp = lax.axis_index("dp")
        local = lax.rem(self.dp, GROUP)
        x = lax.rem(local, 2)
        y = lax.rem(lax.div(local, 2), 2)
        z = lax.div(local, 4)
        p = lax.rem(z, 2)
        q = lax.div(z, 2)
        c = self.c
        self.middle = (z == 1) | (z == 2)
        self.end = (z == 0) | (z == 3)
        self.to_core = (1 - c, self.dp)
        step_x, step_y = 1 - 2 * x, 2 - 4 * y
        self.to_x = (c, self.dp + step_x)
        self.to_y = (c, self.dp + step_y)
        self.to_p = (c, self.dp + 4 - 8 * p)
        self.to_q = (c, self.dp + 8 - 16 * q)
        self.to_m = (c, self.dp + 4 - 8 * q)
        along_x, along_y, along_p = (x, self.to_x), (y, self.to_y), (p, self.to_p)
        one = (x + c * (y - x), (c, self.dp + step_x + c * (step_y - step_x)))
        two = (y + c * (x - y), (c, self.dp + step_y + c * (step_x - step_y)))
        orders = ((along_x, along_y), (along_y, along_x), (along_p, one, two))
        self.pieces = []
        for index, order in enumerate(orders):
            starts = [index * PIECE]
            for (bit, _), size in zip(order, HALVES):
                starts.append(starts[-1] + bit * size)
            self.pieces.append((index, order, starts))

    def meet(self):
        barrier = pltpu.get_barrier_semaphore()
        for target in (self.to_core, self.to_x, self.to_y, self.to_p, self.to_q):
            pl.semaphore_signal(barrier, inc=1, device_id=target, device_id_type=MESH)

        @pl.when(self.middle)
        def _():
            pl.semaphore_signal(barrier, inc=1, device_id=self.to_m, device_id_type=MESH)

    def met(self):
        barrier = pltpu.get_barrier_semaphore()

        @pl.when(self.middle)
        def _():
            pl.semaphore_wait(barrier, 6)

        @pl.when(self.end)
        def _():
            pl.semaphore_wait(barrier, 5)

    def landing(self, index, step):
        table = FLAT if index < 2 else TALL
        return pl.ds(index * FLAT_LAND + sum(table[:step]), table[step])

    def send(self, u, piece, step):
        index, order, starts = piece
        s = self.s
        table = FLAT if index < 2 else TALL
        halvings = len(order)
        if step < halvings:
            bit, target = order[step]
            src = s.part.at[u, rows(starts[step] + (1 - bit) * table[step], table[step])]
        elif step < 4:
            target = self.to_p if step == 2 else self.to_m if index < 2 else self.to_q
            src = s.part.at[u, rows(starts[halvings], table[step])]
        else:
            back = min(6 - step, halvings)
            target = order[back][1] if back < halvings else self.to_p
            src = s.done.at[u, rows(starts[min(back + 1, halvings)], table[step])]
        pltpu.make_async_remote_copy(
            src_ref=src,
            dst_ref=s.land.at[u, self.landing(index, step)] if step < 4 else src,
            send_sem=s.sent.at[u],
            recv_sem=s.recv.at[u, step],
            device_id=target,
            device_id_type=MESH,
        ).start()

    def wait(self, u, step, size, sent=False):
        some = self.s.own.at[u, pl.ds(0, size)]
        copy = pltpu.make_async_remote_copy(
            src_ref=some,
            dst_ref=some,
            send_sem=self.s.sent.at[u],
            recv_sem=self.s.recv.at[u, step],
            device_id=self.to_core,
            device_id_type=MESH,
        )
        copy.wait_send() if sent else copy.wait_recv()

    def add(self, u, piece, step):
        index, order, starts = piece
        s = self.s
        table = FLAT if index < 2 else TALL
        here = rows(starts[min(step + 1, len(order))], table[step])
        total = s.part[u, here] + s.land[u, self.landing(index, step)]
        if step < 3:
            s.part[u, here] = total
        else:
            s.done[u, here] = total

    def core_copy(self, u):
        return pltpu.make_async_remote_copy(
            src_ref=self.s.own.at[u, rows((1 - self.c) * SHARE, SHARE)],
            dst_ref=self.s.part.at[u],
            send_sem=self.s.core_sent.at[u],
            recv_sem=self.s.core_recv.at[u],
            device_id=self.to_core,
            device_id_type=MESH,
        )

    def result(self, k):
        return self.s.grads_out.at[k, rows(self.c * SHARE, SHARE)]

    def result_local(self, u, k):
        return pltpu.make_async_copy(self.s.done.at[u], self.result(k), self.s.out_sent.at[u])

    def result_copy(self, u, k):
        return pltpu.make_async_remote_copy(
            src_ref=self.s.done.at[u],
            dst_ref=self.result(k),
            send_sem=self.s.out_sent.at[u],
            recv_sem=self.s.out_recv.at[u],
            device_id=self.to_core,
            device_id_type=MESH,
        )

    def stage(self, step, u, k, layer):
        s = self.s
        flat, tall = self.pieces[:2], self.pieces[2]
        both, everything = 2 * FLAT[2] + TALL[2], self.pieces
        if step == 0:
            self.core_copy(u).wait_recv()
            s.part[u] = s.part[u] + s.own[u, rows(self.c * SHARE, SHARE)]
            for piece in everything:
                self.send(u, piece, 0)
        elif step == 1:
            self.wait(u, 0, 3 * FLAT[0])
            for piece in everything:
                self.add(u, piece, 0)
                self.send(u, piece, 1)
        elif step == 2:
            self.wait(u, 1, 3 * FLAT[1])
            for piece in everything:
                self.add(u, piece, 1)
            self.send(u, tall, 2)

            @pl.when(self.end)
            def _():
                for piece in flat:
                    self.send(u, piece, 2)
        elif step == 3:
            pl.when(self.middle)(lambda: self.wait(u, 2, both))
            pl.when(self.end)(lambda: self.wait(u, 2, TALL[2]))
            self.add(u, tall, 2)
            self.send(u, tall, 3)

            @pl.when(self.middle)
            def _():
                for piece in flat:
                    self.add(u, piece, 2)
                    self.send(u, piece, 3)
        elif step == 4:
            pl.when(self.middle)(lambda: self.wait(u, 3, both))
            pl.when(self.end)(lambda: self.wait(u, 3, TALL[3]))
            self.add(u, tall, 3)
            self.send(u, tall, 4)

            @pl.when(self.middle)
            def _():
                for piece in flat:
                    self.add(u, piece, 3)
                    self.send(u, piece, 4)
                    self.send(u, piece, 5)
        elif step == 5:
            pl.when(self.middle)(lambda: self.wait(u, 4, TALL[4]))
            pl.when(self.end)(lambda: self.wait(u, 4, both))
            self.send(u, tall, 5)

            @pl.when(self.end)
            def _():
                for piece in flat:
                    self.send(u, piece, 5)
        elif step == 6:
            self.wait(u, 5, 3 * FLAT[5])
            for piece in everything:
                self.send(u, piece, 6)
        elif step == 7:
            self.wait(u, 6, 3 * FLAT[6])
            pl.when(layer == self.c)(lambda: self.result_local(u, k).start())
            pl.when(layer != self.c)(lambda: self.result_copy(u, k).start())
            self.core_copy(u).wait_send()
            sent = sum(TALL) + 2 * (FLAT[0] + FLAT[1] + FLAT[5] + FLAT[6])
            pl.when(self.middle)(lambda: self.wait(u, 0, sent + 2 * (FLAT[3] + FLAT[4]), sent=True))
            pl.when(self.end)(lambda: self.wait(u, 0, sent + 2 * FLAT[2], sent=True))

    def settle(self, u):
        layer, k = 1 - lax.div(u, 6), lax.rem(u, 6)

        @pl.when(layer == self.c)
        def _():
            self.result_local(u, k).wait()
            self.result_copy(u, k).wait_recv()

        @pl.when(layer != self.c)
        def _():
            self.result_copy(u, k).wait_send()

    def sum_gains(self, step):
        s = self.s
        total = s.gain_sum
        targets = (self.to_core, self.to_x, self.to_y, self.to_p, self.to_q)

        def copy(index):
            return pltpu.make_async_remote_copy(
                src_ref=total.at[index],
                dst_ref=s.gain_land.at[index],
                send_sem=s.gain_send.at[index],
                recv_sem=s.gain_recv.at[index],
                device_id=targets[index],
                device_id_type=MESH,
            )

        if step > 0:
            copy(step - 1).wait()
            total[step] = total[step - 1] + s.gain_land[step - 1]
        if step < 5:
            copy(step).start()


WEIGHTS = ("first_gain", "query", "key", "value", "output", "second_gain", "gate", "up", "down")


def kernel(names, *refs):
    s = types.SimpleNamespace(**dict(zip(names, refs)))
    links = Links(s)
    c = links.c
    links.meet()

    token_copy = pltpu.make_async_copy(s.tokens.at[c], s.tok, s.in_sem.at[0])
    token_copy.start()
    cot_copy = pltpu.make_async_copy(s.cotangent.at[c], s.cot, s.in_sem.at[1])
    cot_copy.start()

    def place(name, layer):
        where = {
            "first_gain": lambda: s.gain1.at[layer],
            "query": lambda: s.wqkv.at[layer, :, pl.ds(0, DIM)],
            "key": lambda: s.wqkv.at[layer, :, pl.ds(DIM, DIM)],
            "value": lambda: s.wqkv.at[layer, :, pl.ds(2 * DIM, DIM)],
            "output": lambda: s.wo.at[layer],
            "second_gain": lambda: s.gain2.at[layer],
            "gate": lambda: s.wg.at[layer],
            "up": lambda: s.wu.at[layer],
            "down": lambda: s.wd.at[layer],
        }
        return where[name]()

    def source(name):
        ref = getattr(s, "in_" + name)
        return ref if name.endswith("gain") else ref.at[0]

    def weight_local(name, layer):
        index = WEIGHTS.index(name)
        return pltpu.make_async_copy(source(name), place(name, layer), s.w_sem.at[layer, index])

    def weight_copy(name, layer):
        index = WEIGHTS.index(name)
        return pltpu.make_async_remote_copy(
            src_ref=source(name),
            dst_ref=place(name, layer),
            send_sem=s.w_send.at[index],
            recv_sem=s.w_sem.at[layer, index],
            device_id=links.to_core,
            device_id_type=MESH,
        )

    def need(layer, *which):
        for name in which:
            weight_local(name, layer).wait()

    for name in WEIGHTS:
        weight_local(name, c).start()

    ids = s.sample_ids[pl.ds(c, 1), :].astype(F32)
    count = [jnp.sum(jnp.where(ids == v, 1.0, 0.0), axis=-1, keepdims=True) for v in range(3)]
    first = jnp.where(
        count[0] == HALF,
        0.0,
        jnp.where(
            count[1] == HALF,
            count[0],
            jnp.where(count[2] == HALF, count[0] + count[1], count[0] + count[1] + count[2]),
        ),
    ).astype(jnp.int32)
    down_iota = lax.broadcasted_iota(jnp.int32, (SEQ, SEQ), 0)
    lane_iota = lax.broadcasted_iota(jnp.int32, (SEQ, SEQ), 1)
    moved = down_iota + first
    moved = jnp.where(moved >= SEQ, moved - SEQ, moved)
    perm = jnp.where(lane_iota == moved, 1.0, 0.0)
    ids_down = jnp.sum(perm[HALF:] * ids, axis=-1, keepdims=True)
    s.perm[...] = perm.astype(BF)
    moved = lane_iota + first
    moved = jnp.where(moved >= SEQ, moved - SEQ, moved)
    s.back[...] = jnp.where(down_iota == moved, 1.0, 0.0).astype(BF)
    ids_lane = mm(jnp.broadcast_to(ids, (16, SEQ)).astype(BF), s.back[:, HALF:])[:1]
    s.mask[...] = jnp.where(ids_down == ids_lane, 0.0, MASKED)

    token_copy.wait()
    s.x[0] = mm(s.perm[...], s.tok[...]).astype(BF)
    cot_copy.wait()
    s.dy[...] = mm(s.perm[...], s.cot[...]).astype(BF)

    links.met()
    for name in WEIGHTS[:6]:
        weight_copy(name, c).start()

    head0 = lax.broadcasted_iota(jnp.int32, (HALF, 128), 1) < HEAD_DIM

    def of_head(values, h):
        return jnp.where(head0 if h == 0 else ~head0, values, jnp.zeros_like(values))

    def output_row(layer, src, out, sems):
        @pl.when(layer == c)
        def _():
            pltpu.make_async_copy(src, out.at[c], sems.at[0]).start()

        @pl.when(layer != c)
        def _():
            pltpu.make_async_remote_copy(
                src_ref=src, dst_ref=out.at[c], send_sem=sems.at[1], recv_sem=sems.at[2],
                device_id=links.to_core, device_id_type=MESH,
            ).start()

    def output_settle(src, out, sems):
        pltpu.make_async_copy(src, out.at[c], sems.at[0]).wait()
        pltpu.make_async_remote_copy(
            src_ref=src, dst_ref=out.at[c], send_sem=sems.at[1], recv_sem=sems.at[2],
            device_id=links.to_core, device_id_type=MESH,
        ).wait()

    def forward(layer):
        need(layer, "first_gain", "query", "key", "value")
        x = s.x[layer].astype(F32)
        r = rsqrt_mean(x)
        s.r1[layer] = r
        a = (x * r * s.gain1[layer]).astype(BF)
        s.a[layer] = a
        for lo, hi in ((0, 512), (512, 1024), (1024, 1152)):
            part = mm(a, s.wqkv[layer, :, lo:hi])
            if lo == 0:
                s.qkv[layer, :, :DIM] = (part[:, :DIM] * HEAD_DIM ** (-0.5)).astype(BF)
                s.qkv[layer, :, DIM:hi] = part[:, DIM:].astype(BF)
            else:
                s.qkv[layer, :, lo:hi] = part.astype(BF)

        @pl.when(layer == 0)
        def _():
            for name in WEIGHTS[6:]:
                weight_copy(name, c).start()


        for pair, block in PARTS:
            at = pl.ds(block * HALF, HALF)
            q, k, v = [s.qkv[layer, at, lanes(pair, part)] for part in range(3)]
            outs = []
            for h in range(2):
                score = mm_nt(q, of_head(k, h))
                if block == 1:
                    score = score + s.mask[...]
                expo = jnp.exp(score - jnp.max(score, axis=-1, keepdims=True)).astype(BF)
                s.e[layer, pair * 4 + block * 2 + h] = expo
                outs.append(mm(expo, jnp.where(head0 if h == 0 else ~head0, v, jnp.ones_like(v))))
            inverse = 1.0 / pltpu.roll(jnp.where(head0, outs[1], outs[0]), HEAD_DIM, 1)
            s.inverse[layer, pair * 2 + block] = inverse
            s.o[layer, at, lanes(pair)] = (jnp.where(head0, outs[0], outs[1]) * inverse).astype(BF)

        need(layer, "output", "second_gain")
        x1 = x + mm(s.o[layer], s.wo[layer])
        s.x1[layer] = x1
        r = rsqrt_mean(x1)
        s.r2[layer] = r
        s.b[layer] = (x1 * r * s.gain2[layer]).astype(BF)
        need(layer, "gate", "up", "down")

    def hidden(layer, j):
        at = pl.ds(j * CHUNK if isinstance(j, int) else pl.multiple_of(j * CHUNK, CHUNK), CHUNK)
        b = s.b[layer]
        g = mm(b, s.wg[layer, :, at])
        u = mm(b, s.wu[layer, :, at])
        sig = 1.0 / (1.0 + jnp.exp(-g))
        return at, g, u, sig

    def unroll(layer, low, out, dst, sems):
        out[layer] = mm(s.back[...], low[...]).astype(BF)
        output_row(layer, out.at[layer], dst, sems)

    @pl.loop(0, 2)
    def _(layer):
        forward(layer)

        @pl.when(layer == 0)
        def _():
            s.acc[...] = s.x1[0]

            @pl.loop(0, 4)
            def _(j):
                at, g, u, sig = hidden(0, j)
                f = (g * sig * u).astype(BF)
                s.acc[...] += mm(f, s.wd[0, at, :])

            s.x[1] = s.acc[...].astype(BF)

    def put(u, start, values):
        size, width = values.shape
        for lo in range(0, width, 128):
            s.own[u, pl.ds(start, size), :] = values[:, lo : lo + 128].astype(BF)
            start += size
        return start

    def put_gain(layer, which, values):
        for i in range(DIM // 128):
            s.gain_sum[0, pl.ds(layer * 8 + which * 4 + i, 1), :] = values[:, i * 128 : (i + 1) * 128]

    def slot(turn, index):
        found = []
        for k in range(6):
            for step in range(STAGES):
                before, place = divmod(WHEN[k][step], SLOTS)
                if place == index and before < 2:
                    found.append((-step, -before, k))
        for step, before, k in sorted(found):
            if before == 0:
                links.stage(-step, 6 * turn + k, k, 1 - turn)
            else:
                pl.when(turn == 1)(functools.partial(links.stage, -step, k, k, 1))

    def after_compute():
        found = []
        for turn in range(2):
            for k in range(6):
                for step in range(STAGES):
                    place = turn * SLOTS + WHEN[k][step]
                    if place >= 2 * SLOTS:
                        found.append((place, -step, 6 * turn + k))
        return [(-step, u) for _, step, u in sorted(found)]

    def made(u):
        links.core_copy(u).start()

    s.gain_sum[0] = jnp.zeros((16, 128), F32)

    @pl.loop(0, 2)
    def _(turn):
        layer = 1 - turn
        base = turn * 6
        s.bt[...] = s.b[layer].T
        s.db[...] = jnp.zeros((SEQ, DIM), F32)

        for j in range(4):
            at, g, u, sig = hidden(layer, j)
            silu = g * sig
            f = (silu * u).astype(BF)
            dy = s.dy[...]
            df = mm_nt(dy, s.wd[layer, at, :])
            dg = (df * u * sig * (1.0 + g * (1.0 - sig))).astype(BF)
            du = (df * silu).astype(BF)
            s.f[:, at] = f
            nxt = put(base + j, 0, mm_tn(f, dy))
            nxt = put(base + j, nxt, mm(s.bt[...], dg))
            put(base + j, nxt, mm(s.bt[...], du))
            made(base + j)
            slot(turn, 2 * j)
            s.db[...] += mm_nt(dg, s.wg[layer, :, at]) + mm_nt(du, s.wu[layer, :, at])
            slot(turn, 2 * j + 1)

        @pl.when(layer == 1)
        def _():
            s.y[...] = (s.x1[1] + mm(s.f[...], s.wd[1])).astype(BF)

        db = s.db[...]
        r = s.r2[layer]
        normed = s.x1[layer] * r
        put_gain(layer, 1, jnp.sum(db * normed, axis=0, keepdims=True))
        part = db * s.gain2[layer]
        dx1 = s.dy[...].astype(F32) + r * (part - normed * jnp.mean(part * normed, axis=-1, keepdims=True))
        s.dx1[...] = dx1
        low = dx1.astype(BF)
        nxt = put(base + 4, 0, mm_tn(s.o[layer], low))
        s.do[...] = mm_nt(low, s.wo[layer]).astype(BF)
        slot(turn, 8)

        for pair, block in PARTS:
            at = pl.ds(block * HALF, HALF)
            q, k, v = [s.qkv[layer, at, lanes(pair, part)] for part in range(3)]
            do = s.do[at, lanes(pair)].astype(F32) * s.inverse[layer, pair * 2 + block]
            inner = do * s.o[layer, at, lanes(pair)].astype(F32)
            do = do.astype(BF)
            q_t, do_t = q.T, do.T
            dq, dk_t, dv_t = None, [], []
            for h in range(2):
                mine = slice(h * HEAD_DIM, (h + 1) * HEAD_DIM)
                expo = s.e[layer, pair * 4 + block * 2 + h]
                dv_t.append(mm(do_t[mine], expo))
                dp = mm_nt(do, of_head(v, h))
                ds = expo.astype(F32) * (dp - jnp.sum(of_head(inner, h), axis=-1, keepdims=True))
                ds = ds.astype(BF)
                term = mm(ds, of_head(k, h))
                dk_t.append(mm(q_t[mine], ds))
                dq = term if h == 0 else dq + term
            s.dqkv[at, lanes(pair, 0)] = (dq * HEAD_DIM ** (-0.5)).astype(BF)
            s.dqkv[at, lanes(pair, 1)] = jnp.concatenate(dk_t, 0).astype(BF).T
            s.dqkv[at, lanes(pair, 2)] = jnp.concatenate(dv_t, 0).astype(BF).T
            if block == 1:
                slot(turn, 9 + pair)

        s.at[...] = s.a[layer].T
        put(base + 4, nxt, mm(s.at[...], s.dqkv[:, :DIM]))
        made(base + 4)
        slot(turn, 12)
        nxt = put(base + 5, 0, mm(s.at[...], s.dqkv[:, DIM : 2 * DIM]))
        put(base + 5, nxt, mm(s.at[...], s.dqkv[:, 2 * DIM :]))
        made(base + 5)
        slot(turn, 13)

        da = mm_nt(s.dqkv[...], s.wqkv[layer])
        r = s.r1[layer]
        normed = s.x[layer].astype(F32) * r
        put_gain(layer, 0, jnp.sum(da * normed, axis=0, keepdims=True))
        part = da * s.gain1[layer]
        dx = s.dx1[...] + r * (part - normed * jnp.mean(part * normed, axis=-1, keepdims=True))
        low = dx.astype(BF)
        s.dy[...] = low
        s.dx[layer] = low
        slot(turn, 14)

    left = after_compute()
    beside = {2 + 2 * i: functools.partial(unroll, *row) for i, row in enumerate((
        (0, s.dx.at[0], s.dx_row, s.dx_out, s.dx_sem),
        (1, s.dx.at[1], s.dx_row, s.dx_out, s.dx_sem),
        (0, s.x.at[1], s.y_row, s.rows_out, s.y_sem),
        (1, s.y, s.y_row, s.rows_out, s.y_sem),
    ))}
    gap = max((len(left) - 4) // 5, 1)
    for index, (step, u) in enumerate(left):
        if index % gap == 0 and index // gap < 6:
            links.sum_gains(index // gap)
        links.stage(step, u, u % 6, 1 - u // 6)
        if index in beside:
            beside[index]()

    s.gains_out[...] = s.gain_sum[5, pl.ds(pl.multiple_of(c * 8, 8), 8), :]

    @pl.loop(0, UNITS)
    def _(u):
        links.settle(u)

    for index, name in enumerate(WEIGHTS):
        weight_copy(name, c).wait_send()
    output_settle(s.y_row.at[0], s.rows_out, s.y_sem)
    output_settle(s.dx_row.at[0], s.dx_out, s.dx_sem)


def spread_kernel(*refs):
    s = types.SimpleNamespace(**dict(zip(SPREAD_NAMES, refs)))

    def load(index, src, dst):
        return pltpu.make_async_copy(src, dst, s.in_sem.at[index])

    def store(index, src, dst):
        return pltpu.make_async_copy(src, dst, s.out_sem.at[index])

    unit_loads = [load(u, s.units.at[u], s.unit.at[u]) for u in range(6)]
    dx_load = load(6, s.dx_in, s.dx)
    rows_load = load(7, s.rows_in, s.rows)
    stores = []
    for u in (4, 5, 0, 1, 2, 3):
        unit_loads[u].start()
    rows_load.start()
    dx_load.start()

    def panels(u, first, size, wide, dst):
        for p in range(wide):
            dst[:, p * 128 : (p + 1) * 128] = s.unit[u, pl.ds((first + p) * size, size), :].astype(F32)

    squares = ((4, 0, s.output), (4, 3, s.query), (5, 0, s.key), (5, 3, s.value))
    for index, (u, first, out) in enumerate(squares):
        if first == 0:
            unit_loads[u].wait()
        panels(u, first, DIM, 3, s.square.at[index])
        stores.append(store(1 + index, s.square.at[index], out.at[0]))
        stores[-1].start()
    for p in range(3):
        s.vectors[0:1, p * 128 : (p + 1) * 128] = s.gains_in[p : p + 1, :]
        s.vectors[8:9, p * 128 : (p + 1) * 128] = s.gains_in[4 + p : 5 + p, :]
    stores.append(store(5, s.vectors.at[pl.ds(0, 1)], s.first))
    stores.append(store(6, s.vectors.at[pl.ds(8, 1)], s.second))
    stores[-2].start()
    stores[-1].start()
    rows_load.wait()
    stores.append(store(0, s.rows, s.rows_out.at[0]))
    stores[-1].start()
    dx_load.wait()

    @pl.loop(0, 2)
    def _(row):
        s.dx_wide[row] = s.dx[row].astype(F32)

    stores.append(store(7, s.dx_wide, s.dx_out.at[0]))
    stores[-1].start()

    def chunk_stores(u):
        at = pl.ds(pl.multiple_of(u * CHUNK, CHUNK), CHUNK)
        return (
            store(8 + u, s.down_wide.at[u], s.down.at[0, at, :]),
            store(12 + u, s.gate_wide.at[u], s.gate.at[0, :, at]),
            store(16 + u, s.up_wide.at[u], s.up.at[0, :, at]),
        )

    @pl.loop(0, 4)
    def _(u):
        load(u, s.units.at[u], s.unit.at[u]).wait()
        panels(u, 0, CHUNK, 3, s.down_wide.at[u])
        panels(u, 2, DIM, 2, s.gate_wide.at[u])
        panels(u, 4, DIM, 2, s.up_wide.at[u])
        for one in chunk_stores(u):
            one.start()

    for one in stores:
        one.wait()

    @pl.loop(0, 4)
    def _(u):
        for one in chunk_stores(u):
            one.wait()


SPREAD_OUTS = {
    "rows_out": ((1, 2, SEQ, DIM), BF),
    "dx_out": ((1, 2, SEQ, DIM), F32),
    "first": ((1, DIM), F32),
    "query": ((1, DIM, DIM), F32),
    "key": ((1, DIM, DIM), F32),
    "value": ((1, DIM, DIM), F32),
    "output": ((1, DIM, DIM), F32),
    "second": ((1, DIM), F32),
    "gate": ((1, DIM, FF), F32),
    "up": ((1, DIM, FF), F32),
    "down": ((1, FF, DIM), F32),
}
SPREAD_SCRATCH = {
    "unit": pltpu.VMEM((6, UNIT, 128), BF),
    "rows": pltpu.VMEM((2, SEQ, DIM), BF),
    "dx": pltpu.VMEM((2, SEQ, DIM), BF),
    "dx_wide": pltpu.VMEM((2, SEQ, DIM), F32),
    "square": pltpu.VMEM((4, DIM, DIM), F32),
    "vectors": pltpu.VMEM((16, DIM), F32),
    "down_wide": pltpu.VMEM((4, CHUNK, DIM), F32),
    "gate_wide": pltpu.VMEM((4, DIM, CHUNK), F32),
    "up_wide": pltpu.VMEM((4, DIM, CHUNK), F32),
    "in_sem": pltpu.SemaphoreType.DMA((8,)),
    "out_sem": pltpu.SemaphoreType.DMA((20,)),
}
SPREAD_NAMES = ["units", "rows_in", "dx_in", "gains_in", *SPREAD_OUTS, *SPREAD_SCRATCH]


def spread(units, rows_in, dx_in, gains):
    anywhere = pl.BlockSpec(memory_space=pl.ANY)
    return pl.pallas_call(
        spread_kernel,
        in_specs=[anywhere] * 3 + [pl.BlockSpec(memory_space=pltpu.VMEM)],
        out_specs=[anywhere] * len(SPREAD_OUTS),
        out_shape=[jax.ShapeDtypeStruct(*shape) for shape in SPREAD_OUTS.values()],
        scratch_shapes=list(SPREAD_SCRATCH.values()),
        compiler_params=pltpu.CompilerParams(vmem_limit_bytes=62 * 2**20),
    )(units, rows_in, dx_in, gains)


def layers(tokens, sample_ids, cotangent, *weights):
    anywhere = pl.BlockSpec(memory_space=pl.ANY)
    vmem = pl.BlockSpec(memory_space=pltpu.VMEM)
    inputs = ["tokens", "cotangent"] + ["in_" + name for name in WEIGHTS] + ["sample_ids"]
    outputs = {
        "grads_out": jax.ShapeDtypeStruct((UNITS // 2, UNIT, 128), BF),
        "rows_out": jax.ShapeDtypeStruct((2, SEQ, DIM), BF),
        "dx_out": jax.ShapeDtypeStruct((2, SEQ, DIM), BF),
        "gains_out": jax.ShapeDtypeStruct((8, 128), F32),
    }
    dma = pltpu.SemaphoreType.DMA
    scratch = {
        "tok": pltpu.VMEM((SEQ, DIM), BF),
        "cot": pltpu.VMEM((SEQ, DIM), BF),
        "gain1": pltpu.VMEM((2, 1, DIM), F32),
        "gain2": pltpu.VMEM((2, 1, DIM), F32),
        "wqkv": pltpu.VMEM((2, DIM, 3 * DIM), BF),
        "wo": pltpu.VMEM((2, DIM, DIM), BF),
        "wg": pltpu.VMEM((2, DIM, FF), BF),
        "wu": pltpu.VMEM((2, DIM, FF), BF),
        "wd": pltpu.VMEM((2, FF, DIM), BF),
        "perm": pltpu.VMEM((SEQ, SEQ), BF),
        "back": pltpu.VMEM((SEQ, SEQ), BF),
        "mask": pltpu.VMEM((HALF, HALF), F32),
        "x": pltpu.VMEM((2, SEQ, DIM), BF),
        "a": pltpu.VMEM((2, SEQ, DIM), BF),
        "qkv": pltpu.VMEM((2, SEQ, 3 * DIM), BF),
        "e": pltpu.VMEM((2, 2 * HEADS, HALF, HALF), BF),
        "inverse": pltpu.VMEM((2, HEADS, HALF, 128), F32),
        "f": pltpu.VMEM((SEQ, FF), BF),
        "o": pltpu.VMEM((2, SEQ, DIM), BF),
        "x1": pltpu.VMEM((2, SEQ, DIM), F32),
        "b": pltpu.VMEM((2, SEQ, DIM), BF),
        "r1": pltpu.VMEM((2, SEQ, 1), F32),
        "r2": pltpu.VMEM((2, SEQ, 1), F32),
        "acc": pltpu.VMEM((SEQ, DIM), F32),
        "bt": pltpu.VMEM((DIM, SEQ), BF),
        "at": pltpu.VMEM((DIM, SEQ), BF),
        "db": pltpu.VMEM((SEQ, DIM), F32),
        "dy": pltpu.VMEM((SEQ, DIM), BF),
        "dx1": pltpu.VMEM((SEQ, DIM), F32),
        "dx": pltpu.VMEM((2, SEQ, DIM), BF),
        "y": pltpu.VMEM((SEQ, DIM), BF),
        "do": pltpu.VMEM((SEQ, DIM), BF),
        "dqkv": pltpu.VMEM((SEQ, 3 * DIM), BF),
        "y_row": pltpu.VMEM((2, SEQ, DIM), BF),
        "dx_row": pltpu.VMEM((2, SEQ, DIM), BF),
        "own": pltpu.VMEM((UNITS, UNIT, 128), BF),
        "part": pltpu.VMEM((UNITS, SHARE, 128), BF),
        "land": pltpu.VMEM((UNITS, LAND_ROWS, 128), BF),
        "done": pltpu.VMEM((UNITS, SHARE, 128), BF),
        "gain_sum": pltpu.VMEM((6, 16, 128), F32),
        "gain_land": pltpu.VMEM((5, 16, 128), F32),
        "in_sem": dma((2,)),
        "w_sem": dma((2, len(WEIGHTS))),
        "w_send": dma((len(WEIGHTS),)),
        "sent": dma((UNITS,)),
        "recv": dma((UNITS, 7)),
        "core_sent": dma((UNITS,)),
        "core_recv": dma((UNITS,)),
        "out_sent": dma((UNITS,)),
        "out_recv": dma((UNITS,)),
        "gain_send": dma((5,)),
        "gain_recv": dma((5,)),
        "y_sem": dma((3,)),
        "dx_sem": dma((3,)),
    }
    names = inputs + list(outputs) + list(scratch)
    return pl.pallas_call(
        functools.partial(kernel, names),
        out_shape=list(outputs.values()),
        in_specs=[anywhere] * (len(inputs) - 1) + [vmem],
        out_specs=[anywhere, anywhere, anywhere, vmem],
        scratch_shapes=list(scratch.values()),
        compiler_params=pltpu.CompilerParams(
            collective_id=0, has_side_effects=True, vmem_limit_bytes=62 * 2**20
        ),
        cost_estimate=pl.CostEstimate(flops=15 * 10**9, bytes_accessed=10**7, transcendentals=4 * 10**6),
    )(tokens, cotangent, *weights, sample_ids)


def solution(mesh):
    count = mesh.shape["dp"]

    def per_device(tokens, sample_ids, cotangent, *weights):
        units, rows_out, dx_out, gains = layers(tokens, sample_ids, cotangent, *weights)
        outs = spread(units, rows_out, dx_out, gains)
        if count > GROUP:
            members = [[g * GROUP + i for g in range(count // GROUP)] for i in range(GROUP)]
            outs = list(outs[:2]) + list(lax.psum(tuple(outs[2:]), "dp", axis_index_groups=members))
        return tuple(outs)

    matrix = P("section", None, None)
    vector = P("section", None)
    rows4 = P("section", "dp", None, None)
    grads = (vector, matrix, matrix, matrix, matrix, vector, matrix, matrix, matrix)
    return jax.shard_map(
        per_device,
        mesh=mesh,
        in_specs=(P("dp", None, None), P("dp", None), P("dp", None, None)) + grads,
        out_specs=(rows4, rows4) + grads,
        check_vma=False,
    )
```

```python
import functools
import types

import jax
import jax.numpy as jnp
from jax import lax
from jax.experimental import pallas as pl
from jax.experimental.pallas import tpu as pltpu
from jax.sharding import PartitionSpec as P

MESH = pl.DeviceIdType.MESH
BF = jnp.bfloat16
F32 = jnp.float32
HEADS = 6
HEAD_DIM = 64
NORM_EPS = 1e-05
MASKED = -1e30
GROUP = 16

SEQ = 512
DIM = 384
FF = 1024
HALF = SEQ // 2
CHUNK = FF // 4
UNITS = 12
UNIT = 2304
SHARE = UNIT // 2
PIECE = SHARE // 3
SLOTS = 15
WHEN = (
    (2, 6, 11, 17, 21, 25, 34, 52),
    (4, 8, 13, 17, 22, 28, 37, 58),
    (6, 12, 16, 20, 24, 29, 40, 50),
    (8, 12, 17, 21, 25, 35, 46, 61),
    (14, 18, 22, 26, 31, 37, 44, 63),
    (15, 19, 24, 28, 33, 40, 48, 69),
)
HALVES = (PIECE // 2, PIECE // 4, PIECE // 8)
STAGES = 8
FLAT = (PIECE // 2, PIECE // 4, PIECE // 4, PIECE // 4, PIECE // 4, PIECE // 4, PIECE // 2)
TALL = (PIECE // 2, PIECE // 4, PIECE // 8, PIECE // 8, PIECE // 8, PIECE // 4, PIECE // 2)
FLAT_LAND = sum(FLAT[:4])
LAND_ROWS = 2 * FLAT_LAND + sum(TALL[:4])


def mm(a, b):
    return lax.dot_general(a, b, (((1,), (0,)), ((), ())), preferred_element_type=F32)


def mm_nt(a, b):
    return lax.dot_general(a, b, (((1,), (1,)), ((), ())), preferred_element_type=F32)


def mm_tn(a, b):
    return lax.dot_general(a, b, (((0,), (0,)), ((), ())), preferred_element_type=F32)


def rsqrt_mean(values):
    return lax.rsqrt(jnp.mean(values * values, axis=-1, keepdims=True) + NORM_EPS)


PARTS = [(pair, block) for pair in range(HEADS // 2) for block in range(2)]


def lanes(pair, part=0):
    return pl.ds(part * DIM + pair * 2 * HEAD_DIM, 2 * HEAD_DIM)


def rows(start, size):
    return pl.ds(pl.multiple_of(start, 16), size)


class Links:
    def __init__(self, s):
        self.s = s
        self.c = lax.axis_index("section")
        self.dp = lax.axis_index("dp")
        local = lax.rem(self.dp, GROUP)
        x = lax.rem(local, 2)
        y = lax.rem(lax.div(local, 2), 2)
        z = lax.div(local, 4)
        p = lax.rem(z, 2)
        q = lax.div(z, 2)
        c = self.c
        self.middle = (z == 1) | (z == 2)
        self.end = (z == 0) | (z == 3)
        self.to_core = (1 - c, self.dp)
        step_x, step_y = 1 - 2 * x, 2 - 4 * y
        self.to_x = (c, self.dp + step_x)
        self.to_y = (c, self.dp + step_y)
        self.to_p = (c, self.dp + 4 - 8 * p)
        self.to_q = (c, self.dp + 8 - 16 * q)
        self.to_m = (c, self.dp + 4 - 8 * q)
        along_x, along_y, along_p = (x, self.to_x), (y, self.to_y), (p, self.to_p)
        one = (x + c * (y - x), (c, self.dp + step_x + c * (step_y - step_x)))
        two = (y + c * (x - y), (c, self.dp + step_y + c * (step_x - step_y)))
        orders = ((along_x, along_y), (along_y, along_x), (along_p, one, two))
        self.pieces = []
        for index, order in enumerate(orders):
            starts = [index * PIECE]
            for (bit, _), size in zip(order, HALVES):
                starts.append(starts[-1] + bit * size)
            self.pieces.append((index, order, starts))

    def meet(self):
        barrier = pltpu.get_barrier_semaphore()
        for target in (self.to_core, self.to_x, self.to_y, self.to_p, self.to_q):
            pl.semaphore_signal(barrier, inc=1, device_id=target, device_id_type=MESH)

        @pl.when(self.middle)
        def _():
            pl.semaphore_signal(barrier, inc=1, device_id=self.to_m, device_id_type=MESH)

    def met(self):
        barrier = pltpu.get_barrier_semaphore()

        @pl.when(self.middle)
        def _():
            pl.semaphore_wait(barrier, 6)

        @pl.when(self.end)
        def _():
            pl.semaphore_wait(barrier, 5)

    def landing(self, index, step):
        table = FLAT if index < 2 else TALL
        return pl.ds(index * FLAT_LAND + sum(table[:step]), table[step])

    def send(self, u, piece, step):
        index, order, starts = piece
        s = self.s
        table = FLAT if index < 2 else TALL
        halvings = len(order)
        if step < halvings:
            bit, target = order[step]
            src = s.part.at[u, rows(starts[step] + (1 - bit) * table[step], table[step])]
        elif step < 4:
            target = self.to_p if step == 2 else self.to_m if index < 2 else self.to_q
            src = s.part.at[u, rows(starts[halvings], table[step])]
        else:
            back = min(6 - step, halvings)
            target = order[back][1] if back < halvings else self.to_p
            src = s.done.at[u, rows(starts[min(back + 1, halvings)], table[step])]
        pltpu.make_async_remote_copy(
            src_ref=src,
            dst_ref=s.land.at[u, self.landing(index, step)] if step < 4 else src,
            send_sem=s.sent.at[u],
            recv_sem=s.recv.at[u, step],
            device_id=target,
            device_id_type=MESH,
        ).start()

    def wait(self, u, step, size, sent=False):
        some = self.s.own.at[u, pl.ds(0, size)]
        copy = pltpu.make_async_remote_copy(
            src_ref=some,
            dst_ref=some,
            send_sem=self.s.sent.at[u],
            recv_sem=self.s.recv.at[u, step],
            device_id=self.to_core,
            device_id_type=MESH,
        )
        copy.wait_send() if sent else copy.wait_recv()

    def add(self, u, piece, step):
        index, order, starts = piece
        s = self.s
        table = FLAT if index < 2 else TALL
        here = rows(starts[min(step + 1, len(order))], table[step])
        total = s.part[u, here] + s.land[u, self.landing(index, step)]
        if step < 3:
            s.part[u, here] = total
        else:
            s.done[u, here] = total

    def core_copy(self, u):
        return pltpu.make_async_remote_copy(
            src_ref=self.s.own.at[u, rows((1 - self.c) * SHARE, SHARE)],
            dst_ref=self.s.part.at[u],
            send_sem=self.s.core_sent,
            recv_sem=self.s.core_recv.at[u],
            device_id=self.to_core,
            device_id_type=MESH,
        )

    def result(self, k):
        return self.s.grads_out.at[k, rows(self.c * SHARE, SHARE)]

    def result_local(self, u, k):
        return pltpu.make_async_copy(self.s.done.at[u], self.result(k), self.s.out_sent)

    def result_copy(self, u, k):
        return pltpu.make_async_remote_copy(
            src_ref=self.s.done.at[u],
            dst_ref=self.result(k),
            send_sem=self.s.out_sent,
            recv_sem=self.s.out_recv,
            device_id=self.to_core,
            device_id_type=MESH,
        )

    def stage(self, step, u, k, layer):
        s = self.s
        flat, tall = self.pieces[:2], self.pieces[2]
        both, everything = 2 * FLAT[2] + TALL[2], self.pieces
        if step == 0:
            self.core_copy(u).wait_recv()
            s.part[u] = s.part[u] + s.own[u, rows(self.c * SHARE, SHARE)]
            for piece in everything:
                self.send(u, piece, 0)
        elif step == 1:
            self.wait(u, 0, 3 * FLAT[0])
            for piece in everything:
                self.add(u, piece, 0)
                self.send(u, piece, 1)
        elif step == 2:
            self.wait(u, 1, 3 * FLAT[1])
            for piece in everything:
                self.add(u, piece, 1)
            self.send(u, tall, 2)

            @pl.when(self.end)
            def _():
                for piece in flat:
                    self.send(u, piece, 2)
        elif step == 3:
            pl.when(self.middle)(lambda: self.wait(u, 2, both))
            pl.when(self.end)(lambda: self.wait(u, 2, TALL[2]))
            self.add(u, tall, 2)
            self.send(u, tall, 3)

            @pl.when(self.middle)
            def _():
                for piece in flat:
                    self.add(u, piece, 2)
                    self.send(u, piece, 3)
        elif step == 4:
            pl.when(self.middle)(lambda: self.wait(u, 3, both))
            pl.when(self.end)(lambda: self.wait(u, 3, TALL[3]))
            self.add(u, tall, 3)
            self.send(u, tall, 4)

            @pl.when(self.middle)
            def _():
                for piece in flat:
                    self.add(u, piece, 3)
                    self.send(u, piece, 4)
                    self.send(u, piece, 5)
        elif step == 5:
            pl.when(self.middle)(lambda: self.wait(u, 4, TALL[4]))
            pl.when(self.end)(lambda: self.wait(u, 4, both))
            self.send(u, tall, 5)

            @pl.when(self.end)
            def _():
                for piece in flat:
                    self.send(u, piece, 5)
        elif step == 6:
            self.wait(u, 5, 3 * FLAT[5])
            for piece in everything:
                self.send(u, piece, 6)
        elif step == 7:
            self.wait(u, 6, 3 * FLAT[6])
            pl.when(layer == self.c)(lambda: self.result_local(u, k).start())
            pl.when(layer != self.c)(lambda: self.result_copy(u, k).start())
            sent = sum(TALL) + 2 * (FLAT[0] + FLAT[1] + FLAT[5] + FLAT[6])
            pl.when(self.middle)(lambda: self.wait(u, 0, sent + 2 * (FLAT[3] + FLAT[4]), sent=True))
            pl.when(self.end)(lambda: self.wait(u, 0, sent + 2 * FLAT[2], sent=True))

    def settle(self):
        def whole(refs, send_sem, recv_sem):
            return pltpu.make_async_remote_copy(
                src_ref=refs, dst_ref=refs, send_sem=send_sem, recv_sem=recv_sem,
                device_id=self.to_core, device_id_type=MESH,
            )

        s = self.s
        whole(s.part, s.core_sent, s.out_recv).wait_send()
        whole(s.done, s.out_sent, s.out_recv).wait_send()
        whole(s.done.at[pl.ds(0, UNITS // 2)], s.out_sent, s.out_recv).wait_recv()

    def sum_gains(self, step):
        s = self.s
        total = s.gain_sum
        targets = (self.to_core, self.to_x, self.to_y, self.to_p, self.to_q)

        def copy(index):
            return pltpu.make_async_remote_copy(
                src_ref=total.at[index],
                dst_ref=s.gain_land.at[index],
                send_sem=s.gain_send.at[index],
                recv_sem=s.gain_recv.at[index],
                device_id=targets[index],
                device_id_type=MESH,
            )

        if step > 0:
            copy(step - 1).wait()
            total[step] = total[step - 1] + s.gain_land[step - 1]
        if step < 5:
            copy(step).start()


WEIGHTS = ("first_gain", "query", "key", "value", "output", "second_gain", "gate", "up", "down")
EARLY = (("first_gain", 0), ("query", 0), ("key", 0), ("value", 0))
LATE = (("output", 0), ("second_gain", 0)) + tuple((name, half) for half in range(2) for name in ("gate", "up", "down"))
HANDED = EARLY + LATE


def kernel(names, *refs):
    s = types.SimpleNamespace(**dict(zip(names, refs)))
    links = Links(s)
    c = links.c
    links.meet()

    token_copy = pltpu.make_async_copy(s.tokens.at[c], s.tok, s.in_sem.at[0])
    token_copy.start()
    cot_copy = pltpu.make_async_copy(s.cotangent.at[c], s.cot, s.in_sem.at[1])
    cot_copy.start()

    def place(name, half, layer):
        part = pl.ds(half * (FF // 2), FF // 2)
        where = {
            "first_gain": lambda: s.gain1.at[layer],
            "query": lambda: s.wqkv.at[layer, :, pl.ds(0, DIM)],
            "key": lambda: s.wqkv.at[layer, :, pl.ds(DIM, DIM)],
            "value": lambda: s.wqkv.at[layer, :, pl.ds(2 * DIM, DIM)],
            "output": lambda: s.wo.at[layer],
            "second_gain": lambda: s.gain2.at[layer],
            "gate": lambda: s.wg.at[layer, :, part],
            "up": lambda: s.wu.at[layer, :, part],
            "down": lambda: s.wd.at[layer, part, :],
        }
        return where[name]()

    def source(name, half):
        ref = getattr(s, "in_" + name)
        part = pl.ds(half * (FF // 2), FF // 2)
        if name.endswith("gain"):
            return ref
        return ref.at[0, :, part] if name in ("gate", "up") else ref.at[0, part, :] if name == "down" else ref.at[0]

    def weight_local(piece, layer):
        sem = s.w_sem.at[layer, HANDED.index(piece)]
        return pltpu.make_async_copy(source(*piece), place(*piece, layer), sem)

    def weight_copy(piece, layer):
        index = HANDED.index(piece)
        return pltpu.make_async_remote_copy(
            src_ref=place(*piece, layer) if piece in EARLY else source(*piece),
            dst_ref=place(*piece, layer),
            send_sem=s.w_send.at[index],
            recv_sem=s.w_sem.at[layer, index],
            device_id=links.to_core,
            device_id_type=MESH,
        )

    def need(layer, *pieces):
        for piece in pieces:
            weight_local(piece, layer).wait()

    for piece in HANDED:
        weight_local(piece, c).start()

    ids = s.sample_ids[pl.ds(c, 1), :].astype(F32)
    count = [jnp.sum(jnp.where(ids == v, 1.0, 0.0), axis=-1, keepdims=True) for v in range(3)]
    first = jnp.where(
        count[0] == HALF,
        0.0,
        jnp.where(
            count[1] == HALF,
            count[0],
            jnp.where(count[2] == HALF, count[0] + count[1], count[0] + count[1] + count[2]),
        ),
    ).astype(jnp.int32)
    down_iota = lax.broadcasted_iota(jnp.int32, (SEQ, SEQ), 0)
    lane_iota = lax.broadcasted_iota(jnp.int32, (SEQ, SEQ), 1)
    moved = down_iota + first
    moved = jnp.where(moved >= SEQ, moved - SEQ, moved)
    perm = jnp.where(lane_iota == moved, 1.0, 0.0)
    ids_down = jnp.sum(perm[HALF:] * ids, axis=-1, keepdims=True)
    s.perm[...] = perm.astype(BF)
    moved = lane_iota + first
    moved = jnp.where(moved >= SEQ, moved - SEQ, moved)
    s.back[...] = jnp.where(down_iota == moved, 1.0, 0.0).astype(BF)
    ids_lane = mm(jnp.broadcast_to(ids, (16, SEQ)).astype(BF), s.back[:, HALF:])[:1]
    s.mask[...] = jnp.where(ids_down == ids_lane, 0.0, MASKED)

    token_copy.wait()
    s.x[0] = mm(s.perm[...], s.tok[...]).astype(BF)
    cot_copy.wait()
    s.dy[...] = mm(s.perm[...], s.cot[...]).astype(BF)

    need(c, *EARLY)
    links.met()
    for piece in EARLY:
        weight_copy(piece, c).start()

    head0 = lax.broadcasted_iota(jnp.int32, (HALF, 128), 1) < HEAD_DIM

    def of_head(values, h):
        return jnp.where(head0 if h == 0 else ~head0, values, jnp.zeros_like(values))

    def output_row(layer, src, out, sems):
        @pl.when(layer == c)
        def _():
            pltpu.make_async_copy(src, out.at[c], sems.at[0]).start()

        @pl.when(layer != c)
        def _():
            pltpu.make_async_remote_copy(
                src_ref=src, dst_ref=out.at[c], send_sem=sems.at[1], recv_sem=sems.at[2],
                device_id=links.to_core, device_id_type=MESH,
            ).start()

    def output_settle(src, out, sems):
        pltpu.make_async_copy(src, out.at[c], sems.at[0]).wait()
        pltpu.make_async_remote_copy(
            src_ref=src, dst_ref=out.at[c], send_sem=sems.at[1], recv_sem=sems.at[2],
            device_id=links.to_core, device_id_type=MESH,
        ).wait()

    def forward(layer):
        x = s.x[layer].astype(F32)
        r = rsqrt_mean(x)
        s.r1[layer] = r
        pl.when(layer != c)(lambda: need(layer, *EARLY))
        a = (x * r * s.gain1[layer]).astype(BF)
        s.a[layer] = a
        for lo, hi in ((0, 512), (512, 1024), (1024, 1152)):
            part = mm(a, s.wqkv[layer, :, lo:hi])
            if lo == 0:
                s.qkv[layer, :, :DIM] = (part[:, :DIM] * HEAD_DIM ** (-0.5)).astype(BF)
                s.qkv[layer, :, DIM:hi] = part[:, DIM:].astype(BF)
            else:
                s.qkv[layer, :, lo:hi] = part.astype(BF)

        @pl.when(layer == 0)
        def _():
            for piece in LATE:
                weight_copy(piece, c).start()

        for pair, block in PARTS:
            at = pl.ds(block * HALF, HALF)
            q, k, v = [s.qkv[layer, at, lanes(pair, part)] for part in range(3)]
            outs = []
            for h in range(2):
                score = mm_nt(q, of_head(k, h))
                if block == 1:
                    score = score + s.mask[...]
                expo = jnp.exp(score - jnp.max(score, axis=-1, keepdims=True)).astype(BF)
                s.e[layer, pair * 4 + block * 2 + h] = expo
                outs.append(mm(expo, jnp.where(head0 if h == 0 else ~head0, v, jnp.ones_like(v))))
            inverse = 1.0 / pltpu.roll(jnp.where(head0, outs[1], outs[0]), HEAD_DIM, 1)
            s.inverse[layer, pair * 2 + block] = inverse
            s.o[layer, at, lanes(pair)] = (jnp.where(head0, outs[0], outs[1]) * inverse).astype(BF)

        need(layer, *LATE[:2])
        x1 = x + mm(s.o[layer], s.wo[layer])
        s.x1[layer] = x1
        r = rsqrt_mean(x1)
        s.r2[layer] = r
        s.b[layer] = (x1 * r * s.gain2[layer]).astype(BF)

    def hidden(layer, j):
        at = pl.ds(j * CHUNK, CHUNK)
        b = s.b[layer]
        g = mm(b, s.wg[layer, :, at])
        u = mm(b, s.wu[layer, :, at])
        sig = 1.0 / (1.0 + jnp.exp(-g))
        return at, g, u, sig

    def unroll(layer, low, out, dst, sems):
        out[layer] = mm(s.back[...], low[...]).astype(BF)
        output_row(layer, out.at[layer], dst, sems)

    @pl.loop(0, 2)
    def _(layer):
        forward(layer)

        @pl.when(layer == 0)
        def _():
            s.acc[...] = s.x1[0]

            for j in range(4):
                if j % 2 == 0:
                    need(0, *LATE[2 + 3 * (j // 2) : 5 + 3 * (j // 2)])
                at, g, u, sig = hidden(0, j)
                f = (g * sig * u).astype(BF)
                s.acc[...] += mm(f, s.wd[0, at, :])

            s.x[1] = s.acc[...].astype(BF)

    def put(u, start, values):
        size, width = values.shape
        for lo in range(0, width, 128):
            s.own[u, pl.ds(start, size), :] = values[:, lo : lo + 128].astype(BF)
            start += size
        return start

    def put_gain(layer, which, values):
        for i in range(DIM // 128):
            s.gain_sum[0, pl.ds(layer * 8 + which * 4 + i, 1), :] = values[:, i * 128 : (i + 1) * 128]

    def slot(turn, index):
        found = []
        for k in range(6):
            for step in range(STAGES):
                before, place = divmod(WHEN[k][step], SLOTS)
                if place == index and before < 2:
                    found.append((-step, -before, k))
        for step, before, k in sorted(found):
            if before == 0:
                links.stage(-step, 6 * turn + k, k, 1 - turn)
            else:
                pl.when(turn == 1)(functools.partial(links.stage, -step, k, k, 1))

    def after_compute():
        found = []
        for turn in range(2):
            for k in range(6):
                for step in range(STAGES):
                    place = turn * SLOTS + WHEN[k][step]
                    if place >= 2 * SLOTS:
                        found.append((place, -step, 6 * turn + k))
        return [(-step, u) for _, step, u in sorted(found)]

    def made(u):
        links.core_copy(u).start()

    need(1, *LATE[2:])
    s.gain_sum[0] = jnp.zeros((16, 128), F32)

    @pl.loop(0, 2)
    def _(turn):
        layer = 1 - turn
        base = turn * 6
        s.bt[...] = s.b[layer].T
        s.db[...] = jnp.zeros((SEQ, DIM), F32)

        for j in range(4):
            at, g, u, sig = hidden(layer, j)
            silu = g * sig
            f = (silu * u).astype(BF)
            dy = s.dy[...]
            df = mm_nt(dy, s.wd[layer, at, :])
            dg = (df * u * sig * (1.0 + g * (1.0 - sig))).astype(BF)
            du = (df * silu).astype(BF)
            s.f[:, at] = f
            nxt = put(base + j, 0, mm_tn(f, dy))
            nxt = put(base + j, nxt, mm(s.bt[...], dg))
            put(base + j, nxt, mm(s.bt[...], du))
            made(base + j)
            slot(turn, 2 * j)
            s.db[...] += mm_nt(dg, s.wg[layer, :, at]) + mm_nt(du, s.wu[layer, :, at])
            slot(turn, 2 * j + 1)

        @pl.when(layer == 1)
        def _():
            s.y[...] = (s.x1[1] + mm(s.f[...], s.wd[1])).astype(BF)

        db = s.db[...]
        r = s.r2[layer]
        normed = s.x1[layer] * r
        put_gain(layer, 1, jnp.sum(db * normed, axis=0, keepdims=True))
        part = db * s.gain2[layer]
        dx1 = s.dy[...].astype(F32) + r * (part - normed * jnp.mean(part * normed, axis=-1, keepdims=True))
        s.dx1[...] = dx1
        low = dx1.astype(BF)
        nxt = put(base + 4, 0, mm_tn(s.o[layer], low))
        s.do[...] = mm_nt(low, s.wo[layer]).astype(BF)
        slot(turn, 8)

        for pair, block in PARTS:
            at = pl.ds(block * HALF, HALF)
            q, k, v = [s.qkv[layer, at, lanes(pair, part)] for part in range(3)]
            do = s.do[at, lanes(pair)].astype(F32) * s.inverse[layer, pair * 2 + block]
            inner = do * s.o[layer, at, lanes(pair)].astype(F32)
            do = do.astype(BF)
            q_t, do_t = q.T, do.T
            dq, dk_t, dv_t = None, [], []
            for h in range(2):
                mine = slice(h * HEAD_DIM, (h + 1) * HEAD_DIM)
                expo = s.e[layer, pair * 4 + block * 2 + h]
                dv_t.append(mm(do_t[mine], expo))
                dp = mm_nt(do, of_head(v, h))
                ds = expo.astype(F32) * (dp - jnp.sum(of_head(inner, h), axis=-1, keepdims=True))
                ds = ds.astype(BF)
                term = mm(ds, of_head(k, h))
                dk_t.append(mm(q_t[mine], ds))
                dq = term if h == 0 else dq + term
            s.dqkv[at, lanes(pair, 0)] = (dq * HEAD_DIM ** (-0.5)).astype(BF)
            s.dqkv[at, lanes(pair, 1)] = jnp.concatenate(dk_t, 0).astype(BF).T
            s.dqkv[at, lanes(pair, 2)] = jnp.concatenate(dv_t, 0).astype(BF).T
            if block == 1:
                slot(turn, 9 + pair)

        s.at[...] = s.a[layer].T
        put(base + 4, nxt, mm(s.at[...], s.dqkv[:, :DIM]))
        made(base + 4)
        slot(turn, 12)
        nxt = put(base + 5, 0, mm(s.at[...], s.dqkv[:, DIM : 2 * DIM]))
        put(base + 5, nxt, mm(s.at[...], s.dqkv[:, 2 * DIM :]))
        made(base + 5)
        slot(turn, 13)

        da = mm_nt(s.dqkv[...], s.wqkv[layer])
        r = s.r1[layer]
        normed = s.x[layer].astype(F32) * r
        put_gain(layer, 0, jnp.sum(da * normed, axis=0, keepdims=True))
        part = da * s.gain1[layer]
        dx = s.dx1[...] + r * (part - normed * jnp.mean(part * normed, axis=-1, keepdims=True))
        low = dx.astype(BF)
        s.dy[...] = low
        s.dx[layer] = low
        slot(turn, 14)

    left = after_compute()
    beside = {2 + 2 * i: functools.partial(unroll, *row) for i, row in enumerate((
        (0, s.dx.at[0], s.dx_row, s.dx_out, s.dx_sem),
        (1, s.dx.at[1], s.dx_row, s.dx_out, s.dx_sem),
        (0, s.x.at[1], s.y_row, s.rows_out, s.y_sem),
        (1, s.y, s.y_row, s.rows_out, s.y_sem),
    ))}
    gap = max((len(left) - 4) // 5, 1)
    for index, (step, u) in enumerate(left):
        if index % gap == 0 and index // gap < 6:
            links.sum_gains(index // gap)
        links.stage(step, u, u % 6, 1 - u // 6)
        if index in beside:
            beside[index]()

    s.gains_out[...] = s.gain_sum[5, pl.ds(pl.multiple_of(c * 8, 8), 8), :]

    links.settle()

    for piece in HANDED:
        weight_copy(piece, c).wait_send()
    output_settle(s.y_row.at[0], s.rows_out, s.y_sem)
    output_settle(s.dx_row.at[0], s.dx_out, s.dx_sem)


def spread_kernel(*refs):
    s = types.SimpleNamespace(**dict(zip(SPREAD_NAMES, refs)))

    def store(index, src, dst):
        return pltpu.make_async_copy(src, dst, s.out_sem.at[index])

    stores = [store(0, s.rows_in, s.rows_out.at[0])]
    stores[0].start()

    @pl.loop(0, 2)
    def _(row):
        s.dx_wide[row] = s.dx_in[row].astype(F32)

    stores.append(store(7, s.dx_wide, s.dx_out.at[0]))
    stores[-1].start()

    def panels(u, first, size, wide, dst):
        for p in range(wide):
            dst[:, p * 128 : (p + 1) * 128] = s.units[u, pl.ds((first + p) * size, size), :].astype(F32)

    squares = ((4, 0, s.output), (4, 3, s.query), (5, 0, s.key), (5, 3, s.value))
    for index, (u, first, out) in enumerate(squares):
        panels(u, first, DIM, 3, s.square.at[index])
        stores.append(store(1 + index, s.square.at[index], out.at[0]))
        stores[-1].start()
    for p in range(3):
        s.vectors[0:1, p * 128 : (p + 1) * 128] = s.gains_in[p : p + 1, :]
        s.vectors[8:9, p * 128 : (p + 1) * 128] = s.gains_in[4 + p : 5 + p, :]
    stores.append(store(5, s.vectors.at[pl.ds(0, 1)], s.first))
    stores.append(store(6, s.vectors.at[pl.ds(8, 1)], s.second))
    stores[-2].start()
    stores[-1].start()
    def chunk_stores(u):
        at = pl.ds(pl.multiple_of(u * CHUNK, CHUNK), CHUNK)
        return (
            store(8 + u, s.down_wide.at[u], s.down.at[0, at, :]),
            store(12 + u, s.gate_wide.at[u], s.gate.at[0, :, at]),
            store(16 + u, s.up_wide.at[u], s.up.at[0, :, at]),
        )

    @pl.loop(0, 4)
    def _(u):
        panels(u, 0, CHUNK, 3, s.down_wide.at[u])
        panels(u, 2, DIM, 2, s.gate_wide.at[u])
        panels(u, 4, DIM, 2, s.up_wide.at[u])
        for one in chunk_stores(u):
            one.start()

    for one in stores:
        one.wait()

    @pl.loop(0, 4)
    def _(u):
        for one in chunk_stores(u):
            one.wait()


SPREAD_OUTS = {
    "rows_out": ((1, 2, SEQ, DIM), BF),
    "dx_out": ((1, 2, SEQ, DIM), F32),
    "first": ((1, DIM), F32),
    "query": ((1, DIM, DIM), F32),
    "key": ((1, DIM, DIM), F32),
    "value": ((1, DIM, DIM), F32),
    "output": ((1, DIM, DIM), F32),
    "second": ((1, DIM), F32),
    "gate": ((1, DIM, FF), F32),
    "up": ((1, DIM, FF), F32),
    "down": ((1, FF, DIM), F32),
}
SPREAD_SCRATCH = {
    "dx_wide": pltpu.VMEM((2, SEQ, DIM), F32),
    "square": pltpu.VMEM((4, DIM, DIM), F32),
    "vectors": pltpu.VMEM((16, DIM), F32),
    "down_wide": pltpu.VMEM((4, CHUNK, DIM), F32),
    "gate_wide": pltpu.VMEM((4, DIM, CHUNK), F32),
    "up_wide": pltpu.VMEM((4, DIM, CHUNK), F32),
    "out_sem": pltpu.SemaphoreType.DMA((20,)),
}
SPREAD_NAMES = ["units", "rows_in", "dx_in", "gains_in", *SPREAD_OUTS, *SPREAD_SCRATCH]


def spread(units, rows_in, dx_in, gains):
    anywhere = pl.BlockSpec(memory_space=pl.ANY)
    return pl.pallas_call(
        spread_kernel,
        in_specs=[pl.BlockSpec(memory_space=pltpu.VMEM)] * 4,
        out_specs=[anywhere] * len(SPREAD_OUTS),
        out_shape=[jax.ShapeDtypeStruct(*shape) for shape in SPREAD_OUTS.values()],
        scratch_shapes=list(SPREAD_SCRATCH.values()),
        compiler_params=pltpu.CompilerParams(vmem_limit_bytes=40 * 2**20),
    )(units, rows_in, dx_in, gains)


def layers(tokens, sample_ids, cotangent, *weights):
    anywhere = pl.BlockSpec(memory_space=pl.ANY)
    vmem = pl.BlockSpec(memory_space=pltpu.VMEM)
    inputs = ["tokens", "cotangent"] + ["in_" + name for name in WEIGHTS] + ["sample_ids"]
    outputs = {
        "grads_out": pltpu.VMEM((UNITS // 2, UNIT, 128), BF),
        "rows_out": pltpu.VMEM((2, SEQ, DIM), BF),
        "dx_out": pltpu.VMEM((2, SEQ, DIM), BF),
        "gains_out": pltpu.VMEM((8, 128), F32),
    }
    dma = pltpu.SemaphoreType.DMA
    scratch = {
        "tok": pltpu.VMEM((SEQ, DIM), BF),
        "cot": pltpu.VMEM((SEQ, DIM), BF),
        "gain1": pltpu.VMEM((2, 1, DIM), F32),
        "gain2": pltpu.VMEM((2, 1, DIM), F32),
        "wqkv": pltpu.VMEM((2, DIM, 3 * DIM), BF),
        "wo": pltpu.VMEM((2, DIM, DIM), BF),
        "wg": pltpu.VMEM((2, DIM, FF), BF),
        "wu": pltpu.VMEM((2, DIM, FF), BF),
        "wd": pltpu.VMEM((2, FF, DIM), BF),
        "perm": pltpu.VMEM((SEQ, SEQ), BF),
        "back": pltpu.VMEM((SEQ, SEQ), BF),
        "mask": pltpu.VMEM((HALF, HALF), F32),
        "x": pltpu.VMEM((2, SEQ, DIM), BF),
        "a": pltpu.VMEM((2, SEQ, DIM), BF),
        "qkv": pltpu.VMEM((2, SEQ, 3 * DIM), BF),
        "e": pltpu.VMEM((2, 2 * HEADS, HALF, HALF), BF),
        "inverse": pltpu.VMEM((2, HEADS, HALF, 128), F32),
        "f": pltpu.VMEM((SEQ, FF), BF),
        "o": pltpu.VMEM((2, SEQ, DIM), BF),
        "x1": pltpu.VMEM((2, SEQ, DIM), F32),
        "b": pltpu.VMEM((2, SEQ, DIM), BF),
        "r1": pltpu.VMEM((2, SEQ, 1), F32),
        "r2": pltpu.VMEM((2, SEQ, 1), F32),
        "acc": pltpu.VMEM((SEQ, DIM), F32),
        "bt": pltpu.VMEM((DIM, SEQ), BF),
        "at": pltpu.VMEM((DIM, SEQ), BF),
        "db": pltpu.VMEM((SEQ, DIM), F32),
        "dy": pltpu.VMEM((SEQ, DIM), BF),
        "dx1": pltpu.VMEM((SEQ, DIM), F32),
        "dx": pltpu.VMEM((2, SEQ, DIM), BF),
        "y": pltpu.VMEM((SEQ, DIM), BF),
        "do": pltpu.VMEM((SEQ, DIM), BF),
        "dqkv": pltpu.VMEM((SEQ, 3 * DIM), BF),
        "y_row": pltpu.VMEM((2, SEQ, DIM), BF),
        "dx_row": pltpu.VMEM((2, SEQ, DIM), BF),
        "own": pltpu.VMEM((UNITS, UNIT, 128), BF),
        "part": pltpu.VMEM((UNITS, SHARE, 128), BF),
        "land": pltpu.VMEM((UNITS, LAND_ROWS, 128), BF),
        "done": pltpu.VMEM((UNITS, SHARE, 128), BF),
        "gain_sum": pltpu.VMEM((6, 16, 128), F32),
        "gain_land": pltpu.VMEM((5, 16, 128), F32),
        "in_sem": dma((2,)),
        "w_sem": dma((2, len(HANDED))),
        "w_send": dma((len(HANDED),)),
        "sent": dma((UNITS,)),
        "recv": dma((UNITS, 7)),
        "core_sent": dma,
        "core_recv": dma((UNITS,)),
        "out_sent": dma,
        "out_recv": dma,
        "gain_send": dma((5,)),
        "gain_recv": dma((5,)),
        "y_sem": dma((3,)),
        "dx_sem": dma((3,)),
    }
    names = inputs + list(outputs) + list(scratch)
    return pl.pallas_call(
        functools.partial(kernel, names),
        out_shape=list(outputs.values()),
        in_specs=[anywhere] * (len(inputs) - 1) + [vmem],
        out_specs=[anywhere, anywhere, anywhere, vmem],
        scratch_shapes=list(scratch.values()),
        compiler_params=pltpu.CompilerParams(
            collective_id=0, has_side_effects=True, vmem_limit_bytes=52 * 2**20
        ),
        cost_estimate=pl.CostEstimate(flops=15 * 10**9, bytes_accessed=10**7, transcendentals=4 * 10**6),
    )(tokens, cotangent, *weights, sample_ids)


def solution(mesh):
    count = mesh.shape["dp"]

    def per_device(tokens, sample_ids, cotangent, *weights):
        units, rows_out, dx_out, gains = layers(tokens, sample_ids, cotangent, *weights)
        outs = spread(units, rows_out, dx_out, gains)
        if count > GROUP:
            members = [[g * GROUP + i for g in range(count // GROUP)] for i in range(GROUP)]
            outs = list(outs[:2]) + list(lax.psum(tuple(outs[2:]), "dp", axis_index_groups=members))
        return tuple(outs)

    matrix = P("section", None, None)
    vector = P("section", None)
    rows4 = P("section", "dp", None, None)
    grads = (vector, matrix, matrix, matrix, matrix, vector, matrix, matrix, matrix)
    return jax.shard_map(
        per_device,
        mesh=mesh,
        in_specs=(P("dp", None, None), P("dp", None), P("dp", None, None)) + grads,
        out_specs=(rows4, rows4) + grads,
        check_vma=False,
    )
```

```python
import functools
import types

import jax
import jax.numpy as jnp
from jax import lax
from jax.experimental import pallas as pl
from jax.experimental.pallas import tpu as pltpu
from jax.sharding import PartitionSpec as P

MESH = pl.DeviceIdType.MESH
BF = jnp.bfloat16
F32 = jnp.float32
HEADS = 6
HEAD_DIM = 64
NORM_EPS = 1e-05
MASKED = -1e30
GROUP = 16

SEQ = 512
DIM = 384
FF = 1024
HALF = SEQ // 2
CHUNK = FF // 4
UNITS = 12
UNIT = 2304
SHARE = UNIT // 2
PIECE = SHARE // 3
SLOTS = 15
WHEN = (
    (2, 6, 11, 17, 21, 25, 34),
    (4, 8, 13, 17, 22, 28, 37),
    (6, 12, 16, 20, 24, 29, 40),
    (8, 12, 17, 21, 25, 35, 46),
    (14, 18, 22, 26, 31, 37, 44),
    (15, 19, 24, 28, 33, 40, 48),
)
HALVES = (PIECE // 2, PIECE // 4, PIECE // 8)
STAGES = 7
FLAT = (PIECE // 2, PIECE // 4, PIECE // 4, PIECE // 4, PIECE // 4, PIECE // 4, PIECE // 2)
TALL = (PIECE // 2, PIECE // 4, PIECE // 8, PIECE // 8, PIECE // 8, PIECE // 4, PIECE // 2)
FLAT_LAND = sum(FLAT[:4])
LAND_ROWS = 2 * FLAT_LAND + sum(TALL[:4])


def mm(a, b):
    return lax.dot_general(a, b, (((1,), (0,)), ((), ())), preferred_element_type=F32)


def mm_nt(a, b):
    return lax.dot_general(a, b, (((1,), (1,)), ((), ())), preferred_element_type=F32)


def mm_tn(a, b):
    return lax.dot_general(a, b, (((0,), (0,)), ((), ())), preferred_element_type=F32)


def rsqrt_mean(values):
    return lax.rsqrt(jnp.mean(values * values, axis=-1, keepdims=True) + NORM_EPS)


PARTS = [(pair, block) for pair in range(HEADS // 2) for block in range(2)]


def lanes(pair, part=0):
    return pl.ds(part * DIM + pair * 2 * HEAD_DIM, 2 * HEAD_DIM)


def rows(start, size):
    return pl.ds(pl.multiple_of(start, 16), size)


class Links:
    def __init__(self, s):
        self.s = s
        self.c = lax.axis_index("section")
        self.dp = lax.axis_index("dp")
        local = lax.rem(self.dp, GROUP)
        x = lax.rem(local, 2)
        y = lax.rem(lax.div(local, 2), 2)
        z = lax.div(local, 4)
        p = lax.rem(z, 2)
        q = lax.div(z, 2)
        c = self.c
        self.half = h = lax.rem(c + x + y + z, 2)
        self.middle = (z == 1) | (z == 2)
        self.end = (z == 0) | (z == 3)
        self.to_core = (1 - c, self.dp)
        step_x, step_y = 1 - 2 * x, 2 - 4 * y
        self.to_x = (1 - c, self.dp + step_x)
        self.to_y = (1 - c, self.dp + step_y)
        self.to_p = (1 - c, self.dp + 4 - 8 * p)
        self.to_q = (c, self.dp + 8 - 16 * q)
        self.to_m = (1 - c, self.dp + 4 - 8 * q)
        along_x, along_y, along_p = (x, self.to_x), (y, self.to_y), (p, self.to_p)
        one = (x + h * (y - x), (1 - c, self.dp + step_x + h * (step_y - step_x)))
        two = (y + h * (x - y), (1 - c, self.dp + step_y + h * (step_x - step_y)))
        orders = ((along_x, along_y), (along_y, along_x), (along_p, one, two))
        self.pieces = []
        for index, order in enumerate(orders):
            starts = [index * PIECE]
            for (bit, _), size in zip(order, HALVES):
                starts.append(starts[-1] + bit * size)
            self.pieces.append((index, order, starts))

    def meet(self):
        barrier = pltpu.get_barrier_semaphore()
        others = [(1 - self.c, target[1]) for target in (self.to_x, self.to_y, self.to_p)]
        for target in (self.to_core, self.to_x, self.to_y, self.to_p, self.to_q, *others):
            pl.semaphore_signal(barrier, inc=1, device_id=target, device_id_type=MESH)

        @pl.when(self.middle)
        def _():
            pl.semaphore_signal(barrier, inc=1, device_id=self.to_m, device_id_type=MESH)

    def met(self):
        barrier = pltpu.get_barrier_semaphore()

        @pl.when(self.middle)
        def _():
            pl.semaphore_wait(barrier, 9)

        @pl.when(self.end)
        def _():
            pl.semaphore_wait(barrier, 8)

    def landing(self, index, step):
        table = FLAT if index < 2 else TALL
        return pl.ds(index * FLAT_LAND + sum(table[:step]), table[step])

    def send(self, u, piece, step):
        index, order, starts = piece
        s = self.s
        table = FLAT if index < 2 else TALL
        halvings = len(order)
        if step < halvings:
            bit, target = order[step]
            src = s.part.at[u, rows(starts[step] + (1 - bit) * table[step], table[step])]
        elif step < 4:
            target = self.to_p if step == 2 else self.to_m if index < 2 else self.to_q
            src = s.part.at[u, rows(starts[halvings], table[step])]
        else:
            back = min(6 - step, halvings)
            target = order[back][1] if back < halvings else self.to_p
            src = s.done.at[u, rows(starts[min(back + 1, halvings)], table[step])]
        pltpu.make_async_remote_copy(
            src_ref=src,
            dst_ref=s.land.at[u, self.landing(index, step)] if step < 4 else src,
            send_sem=s.sent,
            recv_sem=s.recv.at[u, step],
            device_id=target,
            device_id_type=MESH,
        ).start()

    def finish(self, u, k, layer, piece):
        _, order, starts = piece
        s = self.s
        src = s.done.at[u, rows(starts[1], HALVES[0])]
        dst = s.grads_out.at[k, rows(self.half * SHARE + starts[1], HALVES[0])]

        def hand(chip, sem):
            pltpu.make_async_remote_copy(
                src_ref=src, dst_ref=dst, send_sem=sem, recv_sem=s.out_recv,
                device_id=(layer, chip), device_id_type=MESH,
            ).start()

        hand(order[0][1][1], s.sent)
        pl.when(layer == self.c)(lambda: pltpu.make_async_copy(src, dst, s.out_sent).start())
        pl.when(layer != self.c)(lambda: hand(self.dp, s.out_sent))

    def wait(self, u, step, size):
        some = self.s.own.at[u, pl.ds(0, size)]
        pltpu.make_async_remote_copy(
            src_ref=some,
            dst_ref=some,
            send_sem=self.s.sent,
            recv_sem=self.s.recv.at[u, step],
            device_id=self.to_core,
            device_id_type=MESH,
        ).wait_recv()

    def add(self, u, piece, step):
        index, order, starts = piece
        s = self.s
        table = FLAT if index < 2 else TALL
        here = rows(starts[min(step + 1, len(order))], table[step])
        total = s.part[u, here] + s.land[u, self.landing(index, step)]
        if step < 3:
            s.part[u, here] = total
        else:
            s.done[u, here] = total

    def core_copy(self, u):
        return pltpu.make_async_remote_copy(
            src_ref=self.s.own.at[u, rows((1 - self.half) * SHARE, SHARE)],
            dst_ref=self.s.part.at[u],
            send_sem=self.s.core_sent,
            recv_sem=self.s.core_recv.at[u],
            device_id=self.to_core,
            device_id_type=MESH,
        )

    def stage(self, step, u, k, layer):
        s = self.s
        flat, tall = self.pieces[:2], self.pieces[2]
        both, everything = 2 * FLAT[2] + TALL[2], self.pieces
        if step == 0:
            self.core_copy(u).wait_recv()
            s.part[u] = s.part[u] + s.own[u, rows(self.half * SHARE, SHARE)]
            for piece in everything:
                self.send(u, piece, 0)
        elif step == 1:
            self.wait(u, 0, 3 * FLAT[0])
            for piece in everything:
                self.add(u, piece, 0)
                self.send(u, piece, 1)
        elif step == 2:
            self.wait(u, 1, 3 * FLAT[1])
            for piece in everything:
                self.add(u, piece, 1)
            self.send(u, tall, 2)

            @pl.when(self.end)
            def _():
                for piece in flat:
                    self.send(u, piece, 2)
        elif step == 3:
            pl.when(self.middle)(lambda: self.wait(u, 2, both))
            pl.when(self.end)(lambda: self.wait(u, 2, TALL[2]))
            self.add(u, tall, 2)
            self.send(u, tall, 3)

            @pl.when(self.middle)
            def _():
                for piece in flat:
                    self.add(u, piece, 2)
                    self.send(u, piece, 3)
        elif step == 4:
            pl.when(self.middle)(lambda: self.wait(u, 3, both))
            pl.when(self.end)(lambda: self.wait(u, 3, TALL[3]))
            self.add(u, tall, 3)
            self.send(u, tall, 4)

            @pl.when(self.middle)
            def _():
                for piece in flat:
                    self.add(u, piece, 3)
                    self.send(u, piece, 4)
                    self.send(u, piece, 5)
        elif step == 5:
            pl.when(self.middle)(lambda: self.wait(u, 4, TALL[4]))
            pl.when(self.end)(lambda: self.wait(u, 4, both))
            self.send(u, tall, 5)

            @pl.when(self.end)
            def _():
                for piece in flat:
                    self.send(u, piece, 5)
        elif step == 6:
            self.wait(u, 5, 3 * FLAT[5])
            for piece in everything:
                self.finish(u, k, layer, piece)

    def settle(self):
        def whole(units, size, send_sem):
            some = self.s.own.at[pl.ds(0, units), pl.ds(0, size)]
            return pltpu.make_async_remote_copy(
                src_ref=some, dst_ref=some, send_sem=send_sem, recv_sem=self.s.out_recv,
                device_id=self.to_core, device_id_type=MESH,
            )

        s = self.s
        half = 3 * HALVES[0]
        whole(UNITS, SHARE, s.core_sent).wait_send()
        whole(UNITS, half, s.out_sent).wait_send()
        sent = sum(TALL) + 2 * (FLAT[0] + FLAT[1] + FLAT[5] + FLAT[6])
        pl.when(self.middle)(lambda: whole(UNITS, sent + 2 * (FLAT[3] + FLAT[4]), s.sent).wait_send())
        pl.when(self.end)(lambda: whole(UNITS, sent + 2 * FLAT[2], s.sent).wait_send())
        whole(UNITS // 2, 3 * half, s.out_sent).wait_recv()

    def sum_gains(self, step):
        s = self.s
        total = s.gain_sum
        targets = (self.to_core, self.to_x, self.to_y, self.to_p, self.to_q)

        def copy(index):
            return pltpu.make_async_remote_copy(
                src_ref=total.at[index],
                dst_ref=s.gain_land.at[index],
                send_sem=s.gain_send.at[index],
                recv_sem=s.gain_recv.at[index],
                device_id=targets[index],
                device_id_type=MESH,
            )

        if step > 0:
            copy(step - 1).wait()
            total[step] = total[step - 1] + s.gain_land[step - 1]
        if step < 5:
            copy(step).start()


WEIGHTS = ("first_gain", "query", "key", "value", "output", "second_gain", "gate", "up", "down")
EARLY = (("first_gain", 0), ("query", 0), ("key", 0), ("value", 0))
LATE = (("output", 0), ("second_gain", 0)) + tuple((name, half) for half in range(2) for name in ("gate", "up", "down"))
HANDED = EARLY + LATE


def kernel(names, *refs):
    s = types.SimpleNamespace(**dict(zip(names, refs)))
    links = Links(s)
    c = links.c
    links.meet()

    token_copy = pltpu.make_async_copy(s.tokens.at[c], s.tok, s.in_sem.at[0])
    token_copy.start()
    cot_copy = pltpu.make_async_copy(s.cotangent.at[c], s.cot, s.in_sem.at[1])
    cot_copy.start()

    def place(name, half, layer):
        part = pl.ds(half * (FF // 2), FF // 2)
        where = {
            "first_gain": lambda: s.gain1.at[layer],
            "query": lambda: s.wqkv.at[layer, :, pl.ds(0, DIM)],
            "key": lambda: s.wqkv.at[layer, :, pl.ds(DIM, DIM)],
            "value": lambda: s.wqkv.at[layer, :, pl.ds(2 * DIM, DIM)],
            "output": lambda: s.wo.at[layer],
            "second_gain": lambda: s.gain2.at[layer],
            "gate": lambda: s.wg.at[layer, :, part],
            "up": lambda: s.wu.at[layer, :, part],
            "down": lambda: s.wd.at[layer, part, :],
        }
        return where[name]()

    def source(name, half):
        ref = getattr(s, "in_" + name)
        part = pl.ds(half * (FF // 2), FF // 2)
        if name.endswith("gain"):
            return ref
        return ref.at[0, :, part] if name in ("gate", "up") else ref.at[0, part, :] if name == "down" else ref.at[0]

    def weight_local(piece, layer):
        sem = s.w_sem.at[layer, HANDED.index(piece)]
        return pltpu.make_async_copy(source(*piece), place(*piece, layer), sem)

    def weight_copy(piece, layer):
        index = HANDED.index(piece)
        return pltpu.make_async_remote_copy(
            src_ref=place(*piece, layer) if piece in EARLY else source(*piece),
            dst_ref=place(*piece, layer),
            send_sem=s.w_send.at[index],
            recv_sem=s.w_sem.at[layer, index],
            device_id=links.to_core,
            device_id_type=MESH,
        )

    def need(layer, *pieces):
        for piece in pieces:
            weight_local(piece, layer).wait()

    for piece in HANDED:
        weight_local(piece, c).start()

    need(c, *EARLY)
    links.met()
    for piece in EARLY:
        weight_copy(piece, c).start()

    ids = s.sample_ids[pl.ds(c, 1), :].astype(F32)
    count = [jnp.sum(jnp.where(ids == v, 1.0, 0.0), axis=-1, keepdims=True) for v in range(3)]
    first = jnp.where(
        count[0] == HALF,
        0.0,
        jnp.where(
            count[1] == HALF,
            count[0],
            jnp.where(count[2] == HALF, count[0] + count[1], count[0] + count[1] + count[2]),
        ),
    ).astype(jnp.int32)
    down_iota = lax.broadcasted_iota(jnp.int32, (SEQ, SEQ), 0)
    lane_iota = lax.broadcasted_iota(jnp.int32, (SEQ, SEQ), 1)
    moved = down_iota + first
    moved = jnp.where(moved >= SEQ, moved - SEQ, moved)
    perm = jnp.where(lane_iota == moved, 1.0, 0.0)
    ids_down = jnp.sum(perm[HALF:] * ids, axis=-1, keepdims=True)
    s.perm[...] = perm.astype(BF)
    moved = lane_iota + first
    moved = jnp.where(moved >= SEQ, moved - SEQ, moved)
    s.back[...] = jnp.where(down_iota == moved, 1.0, 0.0).astype(BF)
    ids_lane = mm(jnp.broadcast_to(ids, (16, SEQ)).astype(BF), s.back[:, HALF:])[:1]
    s.mask[...] = jnp.where(ids_down == ids_lane, 0.0, MASKED)

    token_copy.wait()
    s.x[0] = mm(s.perm[...], s.tok[...]).astype(BF)
    for piece in LATE:
        weight_copy(piece, c).start()
    cot_copy.wait()
    s.dy[...] = mm(s.perm[...], s.cot[...]).astype(BF)


    head0 = lax.broadcasted_iota(jnp.int32, (HALF, 128), 1) < HEAD_DIM

    def of_head(values, h):
        return jnp.where(head0 if h == 0 else ~head0, values, jnp.zeros_like(values))

    def output_row(layer, src, out, sems):
        @pl.when(layer == c)
        def _():
            pltpu.make_async_copy(src, out.at[c], sems.at[0]).start()

        @pl.when(layer != c)
        def _():
            pltpu.make_async_remote_copy(
                src_ref=src, dst_ref=out.at[c], send_sem=sems.at[1], recv_sem=sems.at[2],
                device_id=links.to_core, device_id_type=MESH,
            ).start()

    def output_settle(src, out, sems):
        pltpu.make_async_copy(src, out.at[c], sems.at[0]).wait()
        pltpu.make_async_remote_copy(
            src_ref=src, dst_ref=out.at[c], send_sem=sems.at[1], recv_sem=sems.at[2],
            device_id=links.to_core, device_id_type=MESH,
        ).wait()

    def forward(layer):
        x = s.x[layer].astype(F32)
        r = rsqrt_mean(x)
        s.r1[layer] = r
        pl.when(layer != c)(lambda: need(layer, *EARLY[:3]))
        a = (x * r * s.gain1[layer]).astype(BF)
        s.a[layer] = a
        for lo, hi in ((0, 512), (512, 1024), (1024, 1152)):
            if lo == 512:
                pl.when(layer != c)(lambda: need(layer, EARLY[3]))
            part = mm(a, s.wqkv[layer, :, lo:hi])
            if lo == 0:
                s.qkv[layer, :, :DIM] = (part[:, :DIM] * HEAD_DIM ** (-0.5)).astype(BF)
                s.qkv[layer, :, DIM:hi] = part[:, DIM:].astype(BF)
            else:
                s.qkv[layer, :, lo:hi] = part.astype(BF)

        for pair, block in PARTS:
            at = pl.ds(block * HALF, HALF)
            q, k = [s.qkv[layer, at, lanes(pair, part)] for part in range(2)]
            for h in range(2):
                score = mm_nt(q, of_head(k, h))
                s.score[pair * 4 + block * 2 + h] = score + s.mask[...] if block == 1 else score
        for head in range(2 * HEADS):
            score = s.score[head]
            s.e[layer, head] = jnp.exp(score - jnp.max(score, axis=-1, keepdims=True)).astype(BF)
        for pair, block in PARTS:
            at = pl.ds(block * HALF, HALF)
            v = s.qkv[layer, at, lanes(pair, 2)]
            outs = [
                mm(s.e[layer, pair * 4 + block * 2 + h], jnp.where(head0 if h == 0 else ~head0, v, jnp.ones_like(v)))
                for h in range(2)
            ]
            inverse = 1.0 / pltpu.roll(jnp.where(head0, outs[1], outs[0]), HEAD_DIM, 1)
            s.inverse[layer, pair * 2 + block] = inverse
            s.o[layer, at, lanes(pair)] = (jnp.where(head0, outs[0], outs[1]) * inverse).astype(BF)

        need(layer, *LATE[:2])
        x1 = x + mm(s.o[layer], s.wo[layer])
        s.x1[layer] = x1
        r = rsqrt_mean(x1)
        s.r2[layer] = r
        s.b[layer] = (x1 * r * s.gain2[layer]).astype(BF)

    def hidden(layer, j):
        at = pl.ds(j * CHUNK, CHUNK)
        b = s.b[layer]
        g = mm(b, s.wg[layer, :, at])
        u = mm(b, s.wu[layer, :, at])
        sig = 1.0 / (1.0 + jnp.exp(-g))
        return at, g, u, sig

    def unroll(layer, low, out, dst, sems):
        out[layer] = mm(s.back[...], low[...]).astype(BF)
        output_row(layer, out.at[layer], dst, sems)

    @pl.loop(0, 2)
    def _(layer):
        forward(layer)

        @pl.when(layer == 0)
        def _():
            s.acc[...] = s.x1[0]

            for j in range(4):
                if j % 2 == 0:
                    need(0, *LATE[2 + 3 * (j // 2) : 5 + 3 * (j // 2)])
                at, g, u, sig = hidden(0, j)
                f = (g * sig * u).astype(BF)
                s.acc[...] += mm(f, s.wd[0, at, :])

            s.x[1] = s.acc[...].astype(BF)

    def put(u, start, values):
        size, width = values.shape
        for lo in range(0, width, 128):
            s.own[u, pl.ds(start, size), :] = values[:, lo : lo + 128].astype(BF)
            start += size
        return start

    def put_gain(layer, which, values):
        for i in range(DIM // 128):
            s.gain_sum[0, pl.ds(layer * 8 + which * 4 + i, 1), :] = values[:, i * 128 : (i + 1) * 128]

    def slot(turn, index):
        found = []
        for k in range(6):
            for step in range(STAGES):
                before, place = divmod(WHEN[k][step], SLOTS)
                if place == index and before < 2:
                    found.append((-step, -before, k))
        for step, before, k in sorted(found):
            if before == 0:
                links.stage(-step, 6 * turn + k, k, 1 - turn)
            else:
                pl.when(turn == 1)(functools.partial(links.stage, -step, k, k, 1))

    def after_compute():
        found = []
        for turn in range(2):
            for k in range(6):
                for step in range(STAGES):
                    place = turn * SLOTS + WHEN[k][step]
                    if place >= 2 * SLOTS:
                        found.append((place, -step, 6 * turn + k))
        return [(-step, u) for _, step, u in sorted(found)]

    def made(u):
        links.core_copy(u).start()

    need(1, *LATE[2:])
    s.gain_sum[0] = jnp.zeros((16, 128), F32)

    @pl.loop(0, 2)
    def _(turn):
        layer = 1 - turn
        base = turn * 6
        s.bt[...] = s.b[layer].T
        s.db[...] = jnp.zeros((SEQ, DIM), F32)

        for j in range(4):
            at, g, u, sig = hidden(layer, j)
            silu = g * sig
            f = (silu * u).astype(BF)
            dy = s.dy[...]
            df = mm_nt(dy, s.wd[layer, at, :])
            dg = (df * u * sig * (1.0 + g * (1.0 - sig))).astype(BF)
            du = (df * silu).astype(BF)
            s.f[:, at] = f
            nxt = put(base + j, 0, mm_tn(f, dy))
            nxt = put(base + j, nxt, mm(s.bt[...], dg))
            put(base + j, nxt, mm(s.bt[...], du))
            made(base + j)
            slot(turn, 2 * j)
            s.db[...] += mm_nt(dg, s.wg[layer, :, at]) + mm_nt(du, s.wu[layer, :, at])
            slot(turn, 2 * j + 1)

        @pl.when(layer == 1)
        def _():
            s.y[...] = (s.x1[1] + mm(s.f[...], s.wd[1])).astype(BF)

        db = s.db[...]
        r = s.r2[layer]
        normed = s.x1[layer] * r
        put_gain(layer, 1, jnp.sum(db * normed, axis=0, keepdims=True))
        part = db * s.gain2[layer]
        dx1 = s.dy[...].astype(F32) + r * (part - normed * jnp.mean(part * normed, axis=-1, keepdims=True))
        s.dx1[...] = dx1
        low = dx1.astype(BF)
        nxt = put(base + 4, 0, mm_tn(s.o[layer], low))
        s.do[...] = mm_nt(low, s.wo[layer]).astype(BF)
        slot(turn, 8)

        for pair, block in PARTS:
            at = pl.ds(block * HALF, HALF)
            q, k, v = [s.qkv[layer, at, lanes(pair, part)] for part in range(3)]
            do = s.do[at, lanes(pair)].astype(F32) * s.inverse[layer, pair * 2 + block]
            inner = do * s.o[layer, at, lanes(pair)].astype(F32)
            do = do.astype(BF)
            q_t, do_t = q.T, do.T
            dq, dk_t, dv_t = None, [], []
            for h in range(2):
                mine = slice(h * HEAD_DIM, (h + 1) * HEAD_DIM)
                expo = s.e[layer, pair * 4 + block * 2 + h]
                dv_t.append(mm(do_t[mine], expo))
                dp = mm_nt(do, of_head(v, h))
                ds = expo.astype(F32) * (dp - jnp.sum(of_head(inner, h), axis=-1, keepdims=True))
                ds = ds.astype(BF)
                term = mm(ds, of_head(k, h))
                dk_t.append(mm(q_t[mine], ds))
                dq = term if h == 0 else dq + term
            s.dqkv[at, lanes(pair, 0)] = (dq * HEAD_DIM ** (-0.5)).astype(BF)
            s.dqkv[at, lanes(pair, 1)] = jnp.concatenate(dk_t, 0).astype(BF).T
            s.dqkv[at, lanes(pair, 2)] = jnp.concatenate(dv_t, 0).astype(BF).T
            if block == 1:
                slot(turn, 9 + pair)

        s.at[...] = s.a[layer].T
        put(base + 4, nxt, mm(s.at[...], s.dqkv[:, :DIM]))
        made(base + 4)
        slot(turn, 12)
        nxt = put(base + 5, 0, mm(s.at[...], s.dqkv[:, DIM : 2 * DIM]))
        put(base + 5, nxt, mm(s.at[...], s.dqkv[:, 2 * DIM :]))
        made(base + 5)
        slot(turn, 13)

        da = mm_nt(s.dqkv[...], s.wqkv[layer])
        r = s.r1[layer]
        normed = s.x[layer].astype(F32) * r
        put_gain(layer, 0, jnp.sum(da * normed, axis=0, keepdims=True))
        part = da * s.gain1[layer]
        dx = s.dx1[...] + r * (part - normed * jnp.mean(part * normed, axis=-1, keepdims=True))
        low = dx.astype(BF)
        s.dy[...] = low
        s.dx[layer] = low
        slot(turn, 14)

    left = after_compute()
    beside = {2 + 2 * i: functools.partial(unroll, *row) for i, row in enumerate((
        (0, s.dx.at[0], s.dx_row, s.dx_out, s.dx_sem),
        (1, s.dx.at[1], s.dx_row, s.dx_out, s.dx_sem),
        (0, s.x.at[1], s.y_row, s.rows_out, s.y_sem),
        (1, s.y, s.y_row, s.rows_out, s.y_sem),
    ))}
    gap = max((len(left) - 4) // 5, 1)
    for index, (step, u) in enumerate(left):
        if index % gap == 0 and index // gap < 6:
            links.sum_gains(index // gap)
        links.stage(step, u, u % 6, 1 - u // 6)
        if index in beside:
            beside[index]()

    s.gains_out[...] = s.gain_sum[5, pl.ds(pl.multiple_of(c * 8, 8), 8), :]

    links.settle()

    for piece in HANDED:
        weight_copy(piece, c).wait_send()
    output_settle(s.y_row.at[0], s.rows_out, s.y_sem)
    output_settle(s.dx_row.at[0], s.dx_out, s.dx_sem)


def spread_kernel(*refs):
    s = types.SimpleNamespace(**dict(zip(SPREAD_NAMES, refs)))

    def store(index, src, dst):
        return pltpu.make_async_copy(src, dst, s.out_sem.at[index])

    stores = [store(0, s.rows_in, s.rows_out.at[0])]
    stores[0].start()

    @pl.loop(0, 2)
    def _(row):
        s.dx_wide[row] = s.dx_in[row].astype(F32)

    stores.append(store(7, s.dx_wide, s.dx_out.at[0]))
    stores[-1].start()

    def panels(u, first, size, wide, dst):
        for p in range(wide):
            dst[:, p * 128 : (p + 1) * 128] = s.units[u, pl.ds((first + p) * size, size), :].astype(F32)

    squares = ((4, 0, s.output), (4, 3, s.query), (5, 0, s.key), (5, 3, s.value))
    for index, (u, first, out) in enumerate(squares):
        panels(u, first, DIM, 3, s.square.at[index])
        stores.append(store(1 + index, s.square.at[index], out.at[0]))
        stores[-1].start()
    for p in range(3):
        s.vectors[0:1, p * 128 : (p + 1) * 128] = s.gains_in[p : p + 1, :]
        s.vectors[8:9, p * 128 : (p + 1) * 128] = s.gains_in[4 + p : 5 + p, :]
    stores.append(store(5, s.vectors.at[pl.ds(0, 1)], s.first))
    stores.append(store(6, s.vectors.at[pl.ds(8, 1)], s.second))
    stores[-2].start()
    stores[-1].start()
    def chunk_stores(u):
        at = pl.ds(pl.multiple_of(u * CHUNK, CHUNK), CHUNK)
        return (
            store(8 + u, s.down_wide.at[u], s.down.at[0, at, :]),
            store(12 + u, s.gate_wide.at[u], s.gate.at[0, :, at]),
            store(16 + u, s.up_wide.at[u], s.up.at[0, :, at]),
        )

    @pl.loop(0, 4)
    def _(u):
        panels(u, 0, CHUNK, 3, s.down_wide.at[u])
        panels(u, 2, DIM, 2, s.gate_wide.at[u])
        panels(u, 4, DIM, 2, s.up_wide.at[u])
        for one in chunk_stores(u):
            one.start()

    for one in stores:
        one.wait()

    @pl.loop(0, 4)
    def _(u):
        for one in chunk_stores(u):
            one.wait()


SPREAD_OUTS = {
    "rows_out": ((1, 2, SEQ, DIM), BF),
    "dx_out": ((1, 2, SEQ, DIM), F32),
    "first": ((1, DIM), F32),
    "query": ((1, DIM, DIM), F32),
    "key": ((1, DIM, DIM), F32),
    "value": ((1, DIM, DIM), F32),
    "output": ((1, DIM, DIM), F32),
    "second": ((1, DIM), F32),
    "gate": ((1, DIM, FF), F32),
    "up": ((1, DIM, FF), F32),
    "down": ((1, FF, DIM), F32),
}
SPREAD_SCRATCH = {
    "dx_wide": pltpu.VMEM((2, SEQ, DIM), F32),
    "square": pltpu.VMEM((4, DIM, DIM), F32),
    "vectors": pltpu.VMEM((16, DIM), F32),
    "down_wide": pltpu.VMEM((4, CHUNK, DIM), F32),
    "gate_wide": pltpu.VMEM((4, DIM, CHUNK), F32),
    "up_wide": pltpu.VMEM((4, DIM, CHUNK), F32),
    "out_sem": pltpu.SemaphoreType.DMA((20,)),
}
SPREAD_NAMES = ["units", "rows_in", "dx_in", "gains_in", *SPREAD_OUTS, *SPREAD_SCRATCH]


def spread(units, rows_in, dx_in, gains):
    anywhere = pl.BlockSpec(memory_space=pl.ANY)
    return pl.pallas_call(
        spread_kernel,
        in_specs=[pl.BlockSpec(memory_space=pltpu.VMEM)] * 4,
        out_specs=[anywhere] * len(SPREAD_OUTS),
        out_shape=[jax.ShapeDtypeStruct(*shape) for shape in SPREAD_OUTS.values()],
        scratch_shapes=list(SPREAD_SCRATCH.values()),
        compiler_params=pltpu.CompilerParams(vmem_limit_bytes=40 * 2**20),
    )(units, rows_in, dx_in, gains)


def layers(tokens, sample_ids, cotangent, *weights):
    anywhere = pl.BlockSpec(memory_space=pl.ANY)
    vmem = pl.BlockSpec(memory_space=pltpu.VMEM)
    inputs = ["tokens", "cotangent"] + ["in_" + name for name in WEIGHTS] + ["sample_ids"]
    outputs = {
        "grads_out": pltpu.VMEM((UNITS // 2, UNIT, 128), BF),
        "rows_out": pltpu.VMEM((2, SEQ, DIM), BF),
        "dx_out": pltpu.VMEM((2, SEQ, DIM), BF),
        "gains_out": pltpu.VMEM((8, 128), F32),
    }
    dma = pltpu.SemaphoreType.DMA
    scratch = {
        "tok": pltpu.VMEM((SEQ, DIM), BF),
        "cot": pltpu.VMEM((SEQ, DIM), BF),
        "gain1": pltpu.VMEM((2, 1, DIM), F32),
        "gain2": pltpu.VMEM((2, 1, DIM), F32),
        "wqkv": pltpu.VMEM((2, DIM, 3 * DIM), BF),
        "wo": pltpu.VMEM((2, DIM, DIM), BF),
        "wg": pltpu.VMEM((2, DIM, FF), BF),
        "wu": pltpu.VMEM((2, DIM, FF), BF),
        "wd": pltpu.VMEM((2, FF, DIM), BF),
        "perm": pltpu.VMEM((SEQ, SEQ), BF),
        "back": pltpu.VMEM((SEQ, SEQ), BF),
        "mask": pltpu.VMEM((HALF, HALF), F32),
        "x": pltpu.VMEM((2, SEQ, DIM), BF),
        "a": pltpu.VMEM((2, SEQ, DIM), BF),
        "qkv": pltpu.VMEM((2, SEQ, 3 * DIM), BF),
        "score": pltpu.VMEM((2 * HEADS, HALF, HALF), F32),
        "e": pltpu.VMEM((2, 2 * HEADS, HALF, HALF), BF),
        "inverse": pltpu.VMEM((2, HEADS, HALF, 128), F32),
        "f": pltpu.VMEM((SEQ, FF), BF),
        "o": pltpu.VMEM((2, SEQ, DIM), BF),
        "x1": pltpu.VMEM((2, SEQ, DIM), F32),
        "b": pltpu.VMEM((2, SEQ, DIM), BF),
        "r1": pltpu.VMEM((2, SEQ, 1), F32),
        "r2": pltpu.VMEM((2, SEQ, 1), F32),
        "acc": pltpu.VMEM((SEQ, DIM), F32),
        "bt": pltpu.VMEM((DIM, SEQ), BF),
        "at": pltpu.VMEM((DIM, SEQ), BF),
        "db": pltpu.VMEM((SEQ, DIM), F32),
        "dy": pltpu.VMEM((SEQ, DIM), BF),
        "dx1": pltpu.VMEM((SEQ, DIM), F32),
        "dx": pltpu.VMEM((2, SEQ, DIM), BF),
        "y": pltpu.VMEM((SEQ, DIM), BF),
        "do": pltpu.VMEM((SEQ, DIM), BF),
        "dqkv": pltpu.VMEM((SEQ, 3 * DIM), BF),
        "y_row": pltpu.VMEM((2, SEQ, DIM), BF),
        "dx_row": pltpu.VMEM((2, SEQ, DIM), BF),
        "own": pltpu.VMEM((UNITS, UNIT, 128), BF),
        "part": pltpu.VMEM((UNITS, SHARE, 128), BF),
        "land": pltpu.VMEM((UNITS, LAND_ROWS, 128), BF),
        "done": pltpu.VMEM((UNITS, SHARE, 128), BF),
        "gain_sum": pltpu.VMEM((6, 16, 128), F32),
        "gain_land": pltpu.VMEM((5, 16, 128), F32),
        "in_sem": dma((2,)),
        "w_sem": dma((2, len(HANDED))),
        "w_send": dma((len(HANDED),)),
        "sent": dma,
        "recv": dma((UNITS, STAGES - 1)),
        "core_sent": dma,
        "core_recv": dma((UNITS,)),
        "out_sent": dma,
        "out_recv": dma,
        "gain_send": dma((5,)),
        "gain_recv": dma((5,)),
        "y_sem": dma((3,)),
        "dx_sem": dma((3,)),
    }
    names = inputs + list(outputs) + list(scratch)
    return pl.pallas_call(
        functools.partial(kernel, names),
        out_shape=list(outputs.values()),
        in_specs=[anywhere] * (len(inputs) - 1) + [vmem],
        out_specs=[anywhere, anywhere, anywhere, vmem],
        scratch_shapes=list(scratch.values()),
        compiler_params=pltpu.CompilerParams(
            collective_id=0, has_side_effects=True, vmem_limit_bytes=54 * 2**20
        ),
        cost_estimate=pl.CostEstimate(flops=15 * 10**9, bytes_accessed=10**7, transcendentals=4 * 10**6),
    )(tokens, cotangent, *weights, sample_ids)


def solution(mesh):
    count = mesh.shape["dp"]

    def per_device(tokens, sample_ids, cotangent, *weights):
        units, rows_out, dx_out, gains = layers(tokens, sample_ids, cotangent, *weights)
        outs = spread(units, rows_out, dx_out, gains)
        if count > GROUP:
            members = [[g * GROUP + i for g in range(count // GROUP)] for i in range(GROUP)]
            outs = list(outs[:2]) + list(lax.psum(tuple(outs[2:]), "dp", axis_index_groups=members))
        return tuple(outs)

    matrix = P("section", None, None)
    vector = P("section", None)
    rows4 = P("section", "dp", None, None)
    grads = (vector, matrix, matrix, matrix, matrix, vector, matrix, matrix, matrix)
    return jax.shard_map(
        per_device,
        mesh=mesh,
        in_specs=(P("dp", None, None), P("dp", None), P("dp", None, None)) + grads,
        out_specs=(rows4, rows4) + grads,
        check_vma=False,
    )
```

```python
import functools
import types

import jax
import jax.numpy as jnp
from jax import lax
from jax.experimental import pallas as pl
from jax.experimental.pallas import tpu as pltpu
from jax.sharding import PartitionSpec as P

MESH = pl.DeviceIdType.MESH
BF = jnp.bfloat16
F32 = jnp.float32
HEADS = 6
HEAD_DIM = 64
NORM_EPS = 1e-05
MASKED = -1e30
GROUP = 16

SEQ = 512
DIM = 384
FF = 1024
HALF = SEQ // 2
CHUNK = FF // 4
UNITS = 12
UNIT = 2304
SHARE = UNIT // 2
PIECE = SHARE // 3
SLOTS = 15
WHEN = (
    (2, 7, 12, 18, 22, 26, 35),
    (4, 9, 14, 18, 23, 29, 38),
    (6, 13, 17, 21, 25, 30, 41),
    (8, 13, 18, 22, 26, 36, 47),
    (14, 19, 23, 27, 32, 38, 45),
    (15, 20, 25, 29, 34, 41, 49),
)
HALVES = (PIECE // 2, PIECE // 4, PIECE // 8)
STAGES = 7
FLAT = (PIECE // 2, PIECE // 4, PIECE // 4, PIECE // 4, PIECE // 4, PIECE // 4, PIECE // 2)
TALL = (PIECE // 2, PIECE // 4, PIECE // 8, PIECE // 8, PIECE // 8, PIECE // 4, PIECE // 2)
FLAT_LAND = sum(FLAT[:4])
LAND_ROWS = 2 * FLAT_LAND + sum(TALL[:4])


def mm(a, b):
    return lax.dot_general(a, b, (((1,), (0,)), ((), ())), preferred_element_type=F32)


def mm_nt(a, b):
    return lax.dot_general(a, b, (((1,), (1,)), ((), ())), preferred_element_type=F32)


def mm_tn(a, b):
    return lax.dot_general(a, b, (((0,), (0,)), ((), ())), preferred_element_type=F32)


def rsqrt_mean(values):
    return lax.rsqrt(jnp.mean(values * values, axis=-1, keepdims=True) + NORM_EPS)


PARTS = [(pair, block) for pair in range(HEADS // 2) for block in range(2)]


def lanes(pair, part=0):
    return pl.ds(part * DIM + pair * 2 * HEAD_DIM, 2 * HEAD_DIM)


def rows(start, size):
    return pl.ds(pl.multiple_of(start, 16), size)


class Links:
    def __init__(self, s):
        self.s = s
        self.c = lax.axis_index("section")
        self.dp = lax.axis_index("dp")
        local = lax.rem(self.dp, GROUP)
        x = lax.rem(local, 2)
        y = lax.rem(lax.div(local, 2), 2)
        z = lax.div(local, 4)
        p = lax.rem(z, 2)
        q = lax.div(z, 2)
        c = self.c
        self.half = h = lax.rem(c + x + y + z, 2)
        self.middle = (z == 1) | (z == 2)
        self.end = (z == 0) | (z == 3)
        self.to_core = (1 - c, self.dp)
        step_x, step_y = 1 - 2 * x, 2 - 4 * y
        self.to_x = (1 - c, self.dp + step_x)
        self.to_y = (1 - c, self.dp + step_y)
        self.to_p = (1 - c, self.dp + 4 - 8 * p)
        self.to_q = (c, self.dp + 8 - 16 * q)
        self.to_m = (1 - c, self.dp + 4 - 8 * q)
        along_x, along_y, along_p = (x, self.to_x), (y, self.to_y), (p, self.to_p)
        one = (x + h * (y - x), (1 - c, self.dp + step_x + h * (step_y - step_x)))
        two = (y + h * (x - y), (1 - c, self.dp + step_y + h * (step_x - step_y)))
        orders = ((along_x, along_y), (along_y, along_x), (along_p, one, two))
        self.pieces = []
        for index, order in enumerate(orders):
            starts = [index * PIECE]
            for (bit, _), size in zip(order, HALVES):
                starts.append(starts[-1] + bit * size)
            self.pieces.append((index, order, starts))

    def meet(self):
        barrier = pltpu.get_barrier_semaphore()
        others = [(1 - self.c, target[1]) for target in (self.to_x, self.to_y, self.to_p)]
        for target in (self.to_core, self.to_x, self.to_y, self.to_p, self.to_q, *others):
            pl.semaphore_signal(barrier, inc=1, device_id=target, device_id_type=MESH)

        @pl.when(self.middle)
        def _():
            pl.semaphore_signal(barrier, inc=1, device_id=self.to_m, device_id_type=MESH)

    def met(self):
        barrier = pltpu.get_barrier_semaphore()

        @pl.when(self.middle)
        def _():
            pl.semaphore_wait(barrier, 9)

        @pl.when(self.end)
        def _():
            pl.semaphore_wait(barrier, 8)

    def landing(self, index, step):
        table = FLAT if index < 2 else TALL
        return pl.ds(index * FLAT_LAND + sum(table[:step]), table[step])

    def send(self, u, piece, step):
        index, order, starts = piece
        s = self.s
        table = FLAT if index < 2 else TALL
        halvings = len(order)
        if step < halvings:
            bit, target = order[step]
            src = s.part.at[u, rows(starts[step] + (1 - bit) * table[step], table[step])]
        elif step < 4:
            target = self.to_p if step == 2 else self.to_m if index < 2 else self.to_q
            src = s.part.at[u, rows(starts[halvings], table[step])]
        else:
            back = min(6 - step, halvings)
            target = order[back][1] if back < halvings else self.to_p
            src = s.done.at[u, rows(starts[min(back + 1, halvings)], table[step])]
        pltpu.make_async_remote_copy(
            src_ref=src,
            dst_ref=s.land.at[u, self.landing(index, step)] if step < 4 else src,
            send_sem=s.sent,
            recv_sem=s.recv.at[u, step],
            device_id=target,
            device_id_type=MESH,
        ).start()

    def finish(self, u, k, layer, piece):
        _, order, starts = piece
        s = self.s
        src = s.done.at[u, rows(starts[1], HALVES[0])]
        dst = s.grads_out.at[k, rows(self.half * SHARE + starts[1], HALVES[0])]

        def hand(chip, sem):
            pltpu.make_async_remote_copy(
                src_ref=src, dst_ref=dst, send_sem=sem, recv_sem=s.out_recv,
                device_id=(layer, chip), device_id_type=MESH,
            ).start()

        hand(order[0][1][1], s.sent)
        pl.when(layer == self.c)(lambda: pltpu.make_async_copy(src, dst, s.out_sent).start())
        pl.when(layer != self.c)(lambda: hand(self.dp, s.out_sent))

    def wait(self, u, step, size):
        some = self.s.own.at[u, pl.ds(0, size)]
        pltpu.make_async_remote_copy(
            src_ref=some,
            dst_ref=some,
            send_sem=self.s.sent,
            recv_sem=self.s.recv.at[u, step],
            device_id=self.to_core,
            device_id_type=MESH,
        ).wait_recv()

    def add(self, u, piece, step):
        index, order, starts = piece
        s = self.s
        table = FLAT if index < 2 else TALL
        here = rows(starts[min(step + 1, len(order))], table[step])
        total = s.part[u, here] + s.land[u, self.landing(index, step)]
        if step < 3:
            s.part[u, here] = total
        else:
            s.done[u, here] = total

    def core_copy(self, u):
        return pltpu.make_async_remote_copy(
            src_ref=self.s.own.at[u, rows((1 - self.half) * SHARE, SHARE)],
            dst_ref=self.s.part.at[u],
            send_sem=self.s.core_sent,
            recv_sem=self.s.core_recv.at[u],
            device_id=self.to_core,
            device_id_type=MESH,
        )

    def stage(self, step, u, k, layer):
        s = self.s
        flat, tall = self.pieces[:2], self.pieces[2]
        both, everything = 2 * FLAT[2] + TALL[2], self.pieces
        if step == 0:
            self.core_copy(u).wait_recv()
            s.part[u] = s.part[u] + s.own[u, rows(self.half * SHARE, SHARE)]
            for piece in everything:
                self.send(u, piece, 0)
        elif step == 1:
            self.wait(u, 0, 3 * FLAT[0])
            for piece in everything:
                self.add(u, piece, 0)
                self.send(u, piece, 1)
        elif step == 2:
            self.wait(u, 1, 3 * FLAT[1])
            for piece in everything:
                self.add(u, piece, 1)
            self.send(u, tall, 2)

            @pl.when(self.end)
            def _():
                for piece in flat:
                    self.send(u, piece, 2)
        elif step == 3:
            pl.when(self.middle)(lambda: self.wait(u, 2, both))
            pl.when(self.end)(lambda: self.wait(u, 2, TALL[2]))
            self.add(u, tall, 2)
            self.send(u, tall, 3)

            @pl.when(self.middle)
            def _():
                for piece in flat:
                    self.add(u, piece, 2)
                    self.send(u, piece, 3)
        elif step == 4:
            pl.when(self.middle)(lambda: self.wait(u, 3, both))
            pl.when(self.end)(lambda: self.wait(u, 3, TALL[3]))
            self.add(u, tall, 3)
            self.send(u, tall, 4)

            @pl.when(self.middle)
            def _():
                for piece in flat:
                    self.add(u, piece, 3)
                    self.send(u, piece, 4)
                    self.send(u, piece, 5)
        elif step == 5:
            pl.when(self.middle)(lambda: self.wait(u, 4, TALL[4]))
            pl.when(self.end)(lambda: self.wait(u, 4, both))
            self.send(u, tall, 5)

            @pl.when(self.end)
            def _():
                for piece in flat:
                    self.send(u, piece, 5)
        elif step == 6:
            self.wait(u, 5, 3 * FLAT[5])
            for piece in everything:
                self.finish(u, k, layer, piece)

    def settle(self):
        def whole(units, size, send_sem):
            some = self.s.own.at[pl.ds(0, units), pl.ds(0, size)]
            return pltpu.make_async_remote_copy(
                src_ref=some, dst_ref=some, send_sem=send_sem, recv_sem=self.s.out_recv,
                device_id=self.to_core, device_id_type=MESH,
            )

        s = self.s
        half = 3 * HALVES[0]
        whole(UNITS, SHARE, s.core_sent).wait_send()
        whole(UNITS, half, s.out_sent).wait_send()
        sent = sum(TALL) + 2 * (FLAT[0] + FLAT[1] + FLAT[5] + FLAT[6])
        pl.when(self.middle)(lambda: whole(UNITS, sent + 2 * (FLAT[3] + FLAT[4]), s.sent).wait_send())
        pl.when(self.end)(lambda: whole(UNITS, sent + 2 * FLAT[2], s.sent).wait_send())
        whole(UNITS // 2, 3 * half, s.out_sent).wait_recv()

    def sum_gains(self, step):
        s = self.s
        total = s.gain_sum
        targets = (self.to_core, self.to_x, self.to_y, self.to_p, self.to_q)

        def copy(index):
            return pltpu.make_async_remote_copy(
                src_ref=total.at[index],
                dst_ref=s.gain_land.at[index],
                send_sem=s.gain_send,
                recv_sem=s.gain_recv.at[index],
                device_id=targets[index],
                device_id_type=MESH,
            )

        if step > 0:
            copy(step - 1).wait()
            total[step] = total[step - 1] + s.gain_land[step - 1]
        if step < 5:
            copy(step).start()


WEIGHTS = ("first_gain", "query", "key", "value", "output", "second_gain", "gate", "up", "down")
HANDED = (
    (("first_gain", 0),),
    (("query", 0), ("key", 0), ("value", 0)),
    (("output", 0),),
    (("second_gain", 0),),
    (("gate", 0), ("up", 0), ("down", 0)),
    (("gate", 1), ("up", 1), ("down", 1)),
)
EARLY, LATE = (0, 1), (2, 3, 4, 5)


def kernel(names, *refs):
    s = types.SimpleNamespace(**dict(zip(names, refs)))
    links = Links(s)
    c = links.c
    links.meet()

    token_copy = pltpu.make_async_copy(s.tokens.at[c], s.tok, s.in_sem.at[0])
    token_copy.start()
    cot_copy = pltpu.make_async_copy(s.cotangent.at[c], s.cot, s.in_sem.at[1])
    cot_copy.start()

    def place(name, half, layer):
        part = pl.ds(half * (FF // 2), FF // 2)
        where = {
            "first_gain": lambda: s.gain1.at[layer],
            "query": lambda: s.wqkv.at[layer, :, pl.ds(0, DIM)],
            "key": lambda: s.wqkv.at[layer, :, pl.ds(DIM, DIM)],
            "value": lambda: s.wqkv.at[layer, :, pl.ds(2 * DIM, DIM)],
            "output": lambda: s.wo.at[layer],
            "second_gain": lambda: s.gain2.at[layer],
            "gate": lambda: s.wg.at[layer, :, part],
            "up": lambda: s.wu.at[layer, :, part],
            "down": lambda: s.wd.at[layer, part, :],
        }
        return where[name]()

    def source(name, half):
        ref = getattr(s, "in_" + name)
        part = pl.ds(half * (FF // 2), FF // 2)
        if name.endswith("gain"):
            return ref
        return ref.at[0, :, part] if name in ("gate", "up") else ref.at[0, part, :] if name == "down" else ref.at[0]

    def weights_local(group, layer):
        for piece in HANDED[group]:
            pltpu.make_async_copy(source(*piece), place(*piece, layer), s.w_sem.at[layer, group]).start()

    def weights_copy(group, layer):
        for piece in HANDED[group]:
            pltpu.make_async_remote_copy(
                src_ref=place(*piece, layer) if group in EARLY else source(*piece),
                dst_ref=place(*piece, layer),
                send_sem=s.w_send.at[group],
                recv_sem=s.w_sem.at[layer, group],
                device_id=links.to_core,
                device_id_type=MESH,
            ).start()

    def group_wait(group, sem):
        some = (s.gain1.at[0], s.wqkv.at[0], s.wo.at[0], s.gain2.at[0], s.own.at[pl.ds(0, 2)], s.own.at[pl.ds(0, 2)])[group]
        pltpu.make_async_copy(some, some, sem).wait()

    def need(layer, *groups):
        for group in groups:
            group_wait(group, s.w_sem.at[layer, group])

    for group in EARLY + LATE:
        weights_local(group, c)

    need(c, *EARLY)
    links.met()
    for group in EARLY:
        weights_copy(group, c)

    ids = s.sample_ids[pl.ds(c, 1), :].astype(F32)
    count = [jnp.sum(jnp.where(ids == v, 1.0, 0.0), axis=-1, keepdims=True) for v in range(3)]
    first = jnp.where(
        count[0] == HALF,
        0.0,
        jnp.where(
            count[1] == HALF,
            count[0],
            jnp.where(count[2] == HALF, count[0] + count[1], count[0] + count[1] + count[2]),
        ),
    ).astype(jnp.int32)
    down_iota = lax.broadcasted_iota(jnp.int32, (SEQ, SEQ), 0)
    lane_iota = lax.broadcasted_iota(jnp.int32, (SEQ, SEQ), 1)
    moved = down_iota + first
    moved = jnp.where(moved >= SEQ, moved - SEQ, moved)
    perm = jnp.where(lane_iota == moved, 1.0, 0.0)
    ids_down = jnp.sum(perm[HALF:] * ids, axis=-1, keepdims=True)
    s.perm[...] = perm.astype(BF)
    moved = lane_iota + first
    moved = jnp.where(moved >= SEQ, moved - SEQ, moved)
    s.back[...] = jnp.where(down_iota == moved, 1.0, 0.0).astype(BF)
    ids_lane = mm(jnp.broadcast_to(ids, (16, SEQ)).astype(BF), s.back[:, HALF:])[:1]
    s.mask[...] = jnp.where(ids_down == ids_lane, 0.0, MASKED)

    token_copy.wait()
    s.x[0] = mm(s.perm[...], s.tok[...]).astype(BF)
    for group in LATE:
        weights_copy(group, c)
    cot_copy.wait()
    s.dy[...] = mm(s.perm[...], s.cot[...]).astype(BF)


    head0 = lax.broadcasted_iota(jnp.int32, (HALF, 128), 1) < HEAD_DIM

    def of_head(values, h):
        return jnp.where(head0 if h == 0 else ~head0, values, jnp.zeros_like(values))

    def output_row(layer, src, out, sems):
        @pl.when(layer == c)
        def _():
            pltpu.make_async_copy(src, out.at[c], sems.at[0]).start()

        @pl.when(layer != c)
        def _():
            pltpu.make_async_remote_copy(
                src_ref=src, dst_ref=out.at[c], send_sem=sems.at[1], recv_sem=sems.at[2],
                device_id=links.to_core, device_id_type=MESH,
            ).start()

    def output_settle(src, out, sems):
        pltpu.make_async_copy(src, out.at[c], sems.at[0]).wait()
        pltpu.make_async_remote_copy(
            src_ref=src, dst_ref=out.at[c], send_sem=sems.at[1], recv_sem=sems.at[2],
            device_id=links.to_core, device_id_type=MESH,
        ).wait()

    def forward(layer):
        x = s.x[layer].astype(F32)
        r = rsqrt_mean(x)
        s.r1[layer] = r
        pl.when(layer != c)(lambda: need(layer, *EARLY))
        a = (x * r * s.gain1[layer]).astype(BF)
        s.a[layer] = a
        for lo, hi in ((0, 512), (512, 1024), (1024, 1152)):
            part = mm(a, s.wqkv[layer, :, lo:hi])
            if lo == 0:
                s.qkv[layer, :, :DIM] = (part[:, :DIM] * HEAD_DIM ** (-0.5)).astype(BF)
                s.qkv[layer, :, DIM:hi] = part[:, DIM:].astype(BF)
            else:
                s.qkv[layer, :, lo:hi] = part.astype(BF)

        for pair, block in PARTS:
            at = pl.ds(block * HALF, HALF)
            q, k = [s.qkv[layer, at, lanes(pair, part)] for part in range(2)]
            for h in range(2):
                score = mm_nt(q, of_head(k, h))
                s.score[pair * 4 + block * 2 + h] = score + s.mask[...] if block == 1 else score
        for head in range(2 * HEADS):
            score = s.score[head]
            s.e[layer, head] = jnp.exp(score - jnp.max(score, axis=-1, keepdims=True)).astype(BF)
        for pair, block in PARTS:
            at = pl.ds(block * HALF, HALF)
            v = s.qkv[layer, at, lanes(pair, 2)]
            outs = [
                mm(s.e[layer, pair * 4 + block * 2 + h], jnp.where(head0 if h == 0 else ~head0, v, jnp.ones_like(v)))
                for h in range(2)
            ]
            inverse = 1.0 / pltpu.roll(jnp.where(head0, outs[1], outs[0]), HEAD_DIM, 1)
            s.inverse[layer, pair * 2 + block] = inverse
            s.o[layer, at, lanes(pair)] = (jnp.where(head0, outs[0], outs[1]) * inverse).astype(BF)

        need(layer, *LATE[:2])
        x1 = x + mm(s.o[layer], s.wo[layer])
        s.x1[layer] = x1
        r = rsqrt_mean(x1)
        s.r2[layer] = r
        s.b[layer] = (x1 * r * s.gain2[layer]).astype(BF)

    def hidden(layer, j):
        at = pl.ds(j * CHUNK, CHUNK)
        b = s.b[layer]
        g = mm(b, s.wg[layer, :, at])
        u = mm(b, s.wu[layer, :, at])
        sig = 1.0 / (1.0 + jnp.exp(-g))
        return at, g, u, sig

    def unroll(layer, low, out, dst, sems):
        out[layer] = mm(s.back[...], low[...]).astype(BF)
        output_row(layer, out.at[layer], dst, sems)

    @pl.loop(0, 2)
    def _(layer):
        forward(layer)

        @pl.when(layer == 0)
        def _():
            s.acc[...] = s.x1[0]

            for j in range(4):
                if j % 2 == 0:
                    need(0, LATE[2 + j // 2])
                at, g, u, sig = hidden(0, j)
                f = (g * sig * u).astype(BF)
                s.acc[...] += mm(f, s.wd[0, at, :])

            s.x[1] = s.acc[...].astype(BF)

    def put(u, start, values):
        size, width = values.shape
        for lo in range(0, width, 128):
            s.own[u, pl.ds(start, size), :] = values[:, lo : lo + 128].astype(BF)
            start += size
        return start

    def put_gain(layer, which, values):
        for i in range(DIM // 128):
            s.gain_sum[0, pl.ds(layer * 8 + which * 4 + i, 1), :] = values[:, i * 128 : (i + 1) * 128]

    def slot(turn, index):
        found = []
        for k in range(6):
            for step in range(STAGES):
                before, place = divmod(WHEN[k][step], SLOTS)
                if place == index and before < 2:
                    found.append((-step, -before, k))
        for step, before, k in sorted(found):
            if before == 0:
                links.stage(-step, 6 * turn + k, k, 1 - turn)
            else:
                pl.when(turn == 1)(functools.partial(links.stage, -step, k, k, 1))

    def after_compute():
        found = []
        for turn in range(2):
            for k in range(6):
                for step in range(STAGES):
                    place = turn * SLOTS + WHEN[k][step]
                    if place >= 2 * SLOTS:
                        found.append((place, -step, 6 * turn + k))
        return [(-step, u) for _, step, u in sorted(found)]

    def made(u):
        links.core_copy(u).start()

    need(1, *LATE[2:])
    s.gain_sum[0] = jnp.zeros((16, 128), F32)

    @pl.loop(0, 2)
    def _(turn):
        layer = 1 - turn
        base = turn * 6
        s.bt[...] = s.b[layer].T
        s.db[...] = jnp.zeros((SEQ, DIM), F32)

        for j in range(4):
            at, g, u, sig = hidden(layer, j)
            silu = g * sig
            f = (silu * u).astype(BF)
            dy = s.dy[...]
            df = mm_nt(dy, s.wd[layer, at, :])
            dg = (df * u * sig * (1.0 + g * (1.0 - sig))).astype(BF)
            du = (df * silu).astype(BF)
            s.f[:, at] = f
            nxt = put(base + j, 0, mm_tn(f, dy))
            nxt = put(base + j, nxt, mm(s.bt[...], dg))
            put(base + j, nxt, mm(s.bt[...], du))
            made(base + j)
            slot(turn, 2 * j)
            s.db[...] += mm_nt(dg, s.wg[layer, :, at]) + mm_nt(du, s.wu[layer, :, at])
            slot(turn, 2 * j + 1)

        @pl.when(layer == 1)
        def _():
            s.y[...] = (s.x1[1] + mm(s.f[...], s.wd[1])).astype(BF)

        db = s.db[...]
        r = s.r2[layer]
        normed = s.x1[layer] * r
        put_gain(layer, 1, jnp.sum(db * normed, axis=0, keepdims=True))
        part = db * s.gain2[layer]
        dx1 = s.dy[...].astype(F32) + r * (part - normed * jnp.mean(part * normed, axis=-1, keepdims=True))
        s.dx1[...] = dx1
        low = dx1.astype(BF)
        nxt = put(base + 4, 0, mm_tn(s.o[layer], low))
        s.do[...] = mm_nt(low, s.wo[layer]).astype(BF)
        slot(turn, 8)

        for pair, block in PARTS:
            at = pl.ds(block * HALF, HALF)
            q, k, v = [s.qkv[layer, at, lanes(pair, part)] for part in range(3)]
            do = s.do[at, lanes(pair)].astype(F32) * s.inverse[layer, pair * 2 + block]
            inner = do * s.o[layer, at, lanes(pair)].astype(F32)
            do = do.astype(BF)
            q_t, do_t = q.T, do.T
            dq, dk_t, dv_t = None, [], []
            for h in range(2):
                mine = slice(h * HEAD_DIM, (h + 1) * HEAD_DIM)
                expo = s.e[layer, pair * 4 + block * 2 + h]
                dv_t.append(mm(do_t[mine], expo))
                dp = mm_nt(do, of_head(v, h))
                ds = expo.astype(F32) * (dp - jnp.sum(of_head(inner, h), axis=-1, keepdims=True))
                ds = ds.astype(BF)
                term = mm(ds, of_head(k, h))
                dk_t.append(mm(q_t[mine], ds))
                dq = term if h == 0 else dq + term
            s.dqkv[at, lanes(pair, 0)] = (dq * HEAD_DIM ** (-0.5)).astype(BF)
            s.dqkv[at, lanes(pair, 1)] = jnp.concatenate(dk_t, 0).astype(BF).T
            s.dqkv[at, lanes(pair, 2)] = jnp.concatenate(dv_t, 0).astype(BF).T
            if block == 1:
                slot(turn, 9 + pair)

        s.at[...] = s.a[layer].T
        put(base + 4, nxt, mm(s.at[...], s.dqkv[:, :DIM]))
        made(base + 4)
        slot(turn, 12)
        nxt = put(base + 5, 0, mm(s.at[...], s.dqkv[:, DIM : 2 * DIM]))
        put(base + 5, nxt, mm(s.at[...], s.dqkv[:, 2 * DIM :]))
        made(base + 5)
        slot(turn, 13)

        da = mm_nt(s.dqkv[...], s.wqkv[layer])
        r = s.r1[layer]
        normed = s.x[layer].astype(F32) * r
        put_gain(layer, 0, jnp.sum(da * normed, axis=0, keepdims=True))
        part = da * s.gain1[layer]
        dx = s.dx1[...] + r * (part - normed * jnp.mean(part * normed, axis=-1, keepdims=True))
        low = dx.astype(BF)
        s.dy[...] = low
        s.dx[layer] = low
        slot(turn, 14)

    left = after_compute()
    beside = {2 + 2 * i: functools.partial(unroll, *row) for i, row in enumerate((
        (0, s.dx.at[0], s.dx_row, s.dx_out, s.dx_sem),
        (1, s.dx.at[1], s.dx_row, s.dx_out, s.dx_sem),
        (0, s.x.at[1], s.y_row, s.rows_out, s.y_sem),
        (1, s.y, s.y_row, s.rows_out, s.y_sem),
    ))}
    gap = max((len(left) - 4) // 5, 1)
    for index, (step, u) in enumerate(left):
        if index % gap == 0 and index // gap < 6:
            links.sum_gains(index // gap)
        links.stage(step, u, u % 6, 1 - u // 6)
        if index in beside:
            beside[index]()

    s.gains_out[...] = s.gain_sum[5, pl.ds(pl.multiple_of(c * 8, 8), 8), :]

    links.settle()

    for group in EARLY + LATE:
        group_wait(group, s.w_send.at[group])
    output_settle(s.y_row.at[0], s.rows_out, s.y_sem)
    output_settle(s.dx_row.at[0], s.dx_out, s.dx_sem)


def spread_kernel(*refs):
    s = types.SimpleNamespace(**dict(zip(SPREAD_NAMES, refs)))

    def store(index, src, dst):
        return pltpu.make_async_copy(src, dst, s.out_sem.at[index])

    stores = [store(0, s.rows_in, s.rows_out.at[0])]
    stores[0].start()

    @pl.loop(0, 2)
    def _(row):
        s.dx_wide[row] = s.dx_in[row].astype(F32)

    stores.append(store(7, s.dx_wide, s.dx_out.at[0]))
    stores[-1].start()

    def panels(u, first, size, wide, dst):
        for p in range(wide):
            dst[:, p * 128 : (p + 1) * 128] = s.units[u, pl.ds((first + p) * size, size), :].astype(F32)

    def chunk_stores(u):
        at = pl.ds(pl.multiple_of(u * CHUNK, CHUNK), CHUNK)
        return (
            store(8 + u, s.down_wide.at[u], s.down.at[0, at, :]),
            store(12 + u, s.gate_wide.at[u], s.gate.at[0, :, at]),
            store(16 + u, s.up_wide.at[u], s.up.at[0, :, at]),
        )

    @pl.loop(0, 4)
    def _(u):
        panels(u, 0, CHUNK, 3, s.down_wide.at[u])
        panels(u, 2, DIM, 2, s.gate_wide.at[u])
        panels(u, 4, DIM, 2, s.up_wide.at[u])
        for one in chunk_stores(u):
            one.start()

    squares = ((4, 0, s.output), (4, 3, s.query), (5, 0, s.key), (5, 3, s.value))
    for index, (u, first, out) in enumerate(squares):
        panels(u, first, DIM, 3, s.square.at[index])
        stores.append(store(1 + index, s.square.at[index], out.at[0]))
        stores[-1].start()
    for p in range(3):
        s.vectors[0:1, p * 128 : (p + 1) * 128] = s.gains_in[p : p + 1, :]
        s.vectors[8:9, p * 128 : (p + 1) * 128] = s.gains_in[4 + p : 5 + p, :]
    stores.append(store(5, s.vectors.at[pl.ds(0, 1)], s.first))
    stores.append(store(6, s.vectors.at[pl.ds(8, 1)], s.second))
    stores[-2].start()
    stores[-1].start()
    for one in stores:
        one.wait()

    @pl.loop(0, 4)
    def _(u):
        for one in chunk_stores(u):
            one.wait()


SPREAD_OUTS = {
    "rows_out": ((1, 2, SEQ, DIM), BF),
    "dx_out": ((1, 2, SEQ, DIM), F32),
    "first": ((1, DIM), F32),
    "query": ((1, DIM, DIM), F32),
    "key": ((1, DIM, DIM), F32),
    "value": ((1, DIM, DIM), F32),
    "output": ((1, DIM, DIM), F32),
    "second": ((1, DIM), F32),
    "gate": ((1, DIM, FF), F32),
    "up": ((1, DIM, FF), F32),
    "down": ((1, FF, DIM), F32),
}
SPREAD_SCRATCH = {
    "dx_wide": pltpu.VMEM((2, SEQ, DIM), F32),
    "square": pltpu.VMEM((4, DIM, DIM), F32),
    "vectors": pltpu.VMEM((16, DIM), F32),
    "down_wide": pltpu.VMEM((4, CHUNK, DIM), F32),
    "gate_wide": pltpu.VMEM((4, DIM, CHUNK), F32),
    "up_wide": pltpu.VMEM((4, DIM, CHUNK), F32),
    "out_sem": pltpu.SemaphoreType.DMA((20,)),
}
SPREAD_NAMES = ["units", "rows_in", "dx_in", "gains_in", *SPREAD_OUTS, *SPREAD_SCRATCH]


def spread(units, rows_in, dx_in, gains):
    anywhere = pl.BlockSpec(memory_space=pl.ANY)
    return pl.pallas_call(
        spread_kernel,
        in_specs=[pl.BlockSpec(memory_space=pltpu.VMEM)] * 4,
        out_specs=[anywhere] * len(SPREAD_OUTS),
        out_shape=[jax.ShapeDtypeStruct(*shape) for shape in SPREAD_OUTS.values()],
        scratch_shapes=list(SPREAD_SCRATCH.values()),
        compiler_params=pltpu.CompilerParams(vmem_limit_bytes=40 * 2**20),
    )(units, rows_in, dx_in, gains)


def layers(tokens, sample_ids, cotangent, *weights):
    anywhere = pl.BlockSpec(memory_space=pl.ANY)
    vmem = pl.BlockSpec(memory_space=pltpu.VMEM)
    inputs = ["tokens", "cotangent"] + ["in_" + name for name in WEIGHTS] + ["sample_ids"]
    outputs = {
        "grads_out": pltpu.VMEM((UNITS // 2, UNIT, 128), BF),
        "rows_out": pltpu.VMEM((2, SEQ, DIM), BF),
        "dx_out": pltpu.VMEM((2, SEQ, DIM), BF),
        "gains_out": pltpu.VMEM((8, 128), F32),
    }
    dma = pltpu.SemaphoreType.DMA
    scratch = {
        "tok": pltpu.VMEM((SEQ, DIM), BF),
        "cot": pltpu.VMEM((SEQ, DIM), BF),
        "gain1": pltpu.VMEM((2, 1, DIM), F32),
        "gain2": pltpu.VMEM((2, 1, DIM), F32),
        "wqkv": pltpu.VMEM((2, DIM, 3 * DIM), BF),
        "wo": pltpu.VMEM((2, DIM, DIM), BF),
        "wg": pltpu.VMEM((2, DIM, FF), BF),
        "wu": pltpu.VMEM((2, DIM, FF), BF),
        "wd": pltpu.VMEM((2, FF, DIM), BF),
        "perm": pltpu.VMEM((SEQ, SEQ), BF),
        "back": pltpu.VMEM((SEQ, SEQ), BF),
        "mask": pltpu.VMEM((HALF, HALF), F32),
        "x": pltpu.VMEM((2, SEQ, DIM), BF),
        "a": pltpu.VMEM((2, SEQ, DIM), BF),
        "qkv": pltpu.VMEM((2, SEQ, 3 * DIM), BF),
        "score": pltpu.VMEM((2 * HEADS, HALF, HALF), F32),
        "e": pltpu.VMEM((2, 2 * HEADS, HALF, HALF), BF),
        "inverse": pltpu.VMEM((2, HEADS, HALF, 128), F32),
        "f": pltpu.VMEM((SEQ, FF), BF),
        "o": pltpu.VMEM((2, SEQ, DIM), BF),
        "x1": pltpu.VMEM((2, SEQ, DIM), F32),
        "b": pltpu.VMEM((2, SEQ, DIM), BF),
        "r1": pltpu.VMEM((2, SEQ, 1), F32),
        "r2": pltpu.VMEM((2, SEQ, 1), F32),
        "acc": pltpu.VMEM((SEQ, DIM), F32),
        "bt": pltpu.VMEM((DIM, SEQ), BF),
        "at": pltpu.VMEM((DIM, SEQ), BF),
        "db": pltpu.VMEM((SEQ, DIM), F32),
        "dy": pltpu.VMEM((SEQ, DIM), BF),
        "dx1": pltpu.VMEM((SEQ, DIM), F32),
        "dx": pltpu.VMEM((2, SEQ, DIM), BF),
        "y": pltpu.VMEM((SEQ, DIM), BF),
        "do": pltpu.VMEM((SEQ, DIM), BF),
        "dqkv": pltpu.VMEM((SEQ, 3 * DIM), BF),
        "y_row": pltpu.VMEM((2, SEQ, DIM), BF),
        "dx_row": pltpu.VMEM((2, SEQ, DIM), BF),
        "own": pltpu.VMEM((UNITS, UNIT, 128), BF),
        "part": pltpu.VMEM((UNITS, SHARE, 128), BF),
        "land": pltpu.VMEM((UNITS, LAND_ROWS, 128), BF),
        "done": pltpu.VMEM((UNITS, SHARE, 128), BF),
        "gain_sum": pltpu.VMEM((6, 16, 128), F32),
        "gain_land": pltpu.VMEM((5, 16, 128), F32),
        "in_sem": dma((2,)),
        "w_sem": dma((2, len(HANDED))),
        "w_send": dma((len(HANDED),)),
        "sent": dma,
        "recv": dma((UNITS, STAGES - 1)),
        "core_sent": dma,
        "core_recv": dma((UNITS,)),
        "out_sent": dma,
        "out_recv": dma,
        "gain_send": dma,
        "gain_recv": dma((5,)),
        "y_sem": dma((3,)),
        "dx_sem": dma((3,)),
    }
    names = inputs + list(outputs) + list(scratch)
    return pl.pallas_call(
        functools.partial(kernel, names),
        out_shape=list(outputs.values()),
        in_specs=[anywhere] * (len(inputs) - 1) + [vmem],
        out_specs=[anywhere, anywhere, anywhere, vmem],
        scratch_shapes=list(scratch.values()),
        compiler_params=pltpu.CompilerParams(
            collective_id=0, has_side_effects=True, vmem_limit_bytes=54 * 2**20
        ),
        cost_estimate=pl.CostEstimate(flops=15 * 10**9, bytes_accessed=10**7, transcendentals=4 * 10**6),
    )(tokens, cotangent, *weights, sample_ids)


def solution(mesh):
    count = mesh.shape["dp"]

    def per_device(tokens, sample_ids, cotangent, *weights):
        units, rows_out, dx_out, gains = layers(tokens, sample_ids, cotangent, *weights)
        outs = spread(units, rows_out, dx_out, gains)
        if count > GROUP:
            members = [[g * GROUP + i for g in range(count // GROUP)] for i in range(GROUP)]
            outs = list(outs[:2]) + list(lax.psum(tuple(outs[2:]), "dp", axis_index_groups=members))
        return tuple(outs)

    matrix = P("section", None, None)
    vector = P("section", None)
    rows4 = P("section", "dp", None, None)
    grads = (vector, matrix, matrix, matrix, matrix, vector, matrix, matrix, matrix)
    return jax.shard_map(
        per_device,
        mesh=mesh,
        in_specs=(P("dp", None, None), P("dp", None), P("dp", None, None)) + grads,
        out_specs=(rows4, rows4) + grads,
        check_vma=False,
    )
```

```python
import functools
import types

import jax
import jax.numpy as jnp
from jax import lax
from jax.experimental import pallas as pl
from jax.experimental.pallas import tpu as pltpu
from jax.sharding import PartitionSpec as P

MESH = pl.DeviceIdType.MESH
BF = jnp.bfloat16
F32 = jnp.float32
HEADS = 6
HEAD_DIM = 64
NORM_EPS = 1e-05
MASKED = -1e30
GROUP = 16

SEQ = 512
DIM = 384
FF = 1024
HALF = SEQ // 2
CHUNK = FF // 4
UNITS = 12
UNIT = 2304
SHARE = UNIT // 2
PIECE = SHARE // 3
SLOTS = 15
WHEN = (
    (2, 7, 12, 18, 22, 26, 35),
    (4, 9, 14, 18, 23, 29, 38),
    (6, 13, 17, 21, 25, 30, 41),
    (8, 13, 18, 22, 26, 36, 47),
    (14, 18, 22, 26, 31, 37, 44),
    (15, 19, 24, 28, 33, 40, 48),
)
HALVES = (PIECE // 2, PIECE // 4, PIECE // 8)
STAGES = 7
FLAT = (PIECE // 2, PIECE // 4, PIECE // 4, PIECE // 4, PIECE // 4, PIECE // 4, PIECE // 2)
TALL = (PIECE // 2, PIECE // 4, PIECE // 8, PIECE // 8, PIECE // 8, PIECE // 4, PIECE // 2)
FLAT_LAND = sum(FLAT[:4])
LAND_ROWS = 2 * FLAT_LAND + sum(TALL[:4])


def mm(a, b):
    return lax.dot_general(a, b, (((1,), (0,)), ((), ())), preferred_element_type=F32)


def mm_nt(a, b):
    return lax.dot_general(a, b, (((1,), (1,)), ((), ())), preferred_element_type=F32)


def mm_tn(a, b):
    return lax.dot_general(a, b, (((0,), (0,)), ((), ())), preferred_element_type=F32)


def rsqrt_mean(values):
    return lax.rsqrt(jnp.mean(values * values, axis=-1, keepdims=True) + NORM_EPS)


PARTS = [(pair, block) for pair in range(HEADS // 2) for block in range(2)]


def lanes(pair, part=0):
    return pl.ds(part * DIM + pair * 2 * HEAD_DIM, 2 * HEAD_DIM)


def rows(start, size):
    return pl.ds(pl.multiple_of(start, 16), size)


class Links:
    def __init__(self, s):
        self.s = s
        self.c = lax.axis_index("section")
        self.dp = lax.axis_index("dp")
        local = lax.rem(self.dp, GROUP)
        x = lax.rem(local, 2)
        y = lax.rem(lax.div(local, 2), 2)
        z = lax.div(local, 4)
        p = lax.rem(z, 2)
        q = lax.div(z, 2)
        c = self.c
        self.half = h = lax.rem(c + x + y + z, 2)
        self.middle = (z == 1) | (z == 2)
        self.end = (z == 0) | (z == 3)
        self.to_core = (1 - c, self.dp)
        step_x, step_y = 1 - 2 * x, 2 - 4 * y
        self.to_x = (1 - c, self.dp + step_x)
        self.to_y = (1 - c, self.dp + step_y)
        self.to_p = (1 - c, self.dp + 4 - 8 * p)
        self.to_q = (c, self.dp + 8 - 16 * q)
        self.to_m = (1 - c, self.dp + 4 - 8 * q)
        along_x, along_y, along_p = (x, self.to_x), (y, self.to_y), (p, self.to_p)
        one = (x + h * (y - x), (1 - c, self.dp + step_x + h * (step_y - step_x)))
        two = (y + h * (x - y), (1 - c, self.dp + step_y + h * (step_x - step_y)))
        orders = ((along_x, along_y), (along_y, along_x), (along_p, one, two))
        self.pieces = []
        for index, order in enumerate(orders):
            starts = [index * PIECE]
            for (bit, _), size in zip(order, HALVES):
                starts.append(starts[-1] + bit * size)
            self.pieces.append((index, order, starts))

    def meet(self):
        barrier = pltpu.get_barrier_semaphore()
        others = [(1 - self.c, target[1]) for target in (self.to_x, self.to_y, self.to_p)]
        for target in (self.to_core, self.to_x, self.to_y, self.to_p, self.to_q, *others):
            pl.semaphore_signal(barrier, inc=1, device_id=target, device_id_type=MESH)

        @pl.when(self.middle)
        def _():
            pl.semaphore_signal(barrier, inc=1, device_id=self.to_m, device_id_type=MESH)

    def met(self):
        barrier = pltpu.get_barrier_semaphore()

        @pl.when(self.middle)
        def _():
            pl.semaphore_wait(barrier, 9)

        @pl.when(self.end)
        def _():
            pl.semaphore_wait(barrier, 8)

    def landing(self, index, step):
        table = FLAT if index < 2 else TALL
        return pl.ds(index * FLAT_LAND + sum(table[:step]), table[step])

    def send(self, u, piece, step):
        index, order, starts = piece
        s = self.s
        table = FLAT if index < 2 else TALL
        halvings = len(order)
        if step < halvings:
            bit, target = order[step]
            src = s.part.at[u, rows(starts[step] + (1 - bit) * table[step], table[step])]
        elif step < 4:
            target = self.to_p if step == 2 else self.to_m if index < 2 else self.to_q
            src = s.part.at[u, rows(starts[halvings], table[step])]
        else:
            back = min(6 - step, halvings)
            target = order[back][1] if back < halvings else self.to_p
            src = s.done.at[u, rows(starts[min(back + 1, halvings)], table[step])]
        pltpu.make_async_remote_copy(
            src_ref=src,
            dst_ref=s.land.at[u, self.landing(index, step)] if step < 4 else src,
            send_sem=s.sent,
            recv_sem=s.recv.at[u, step],
            device_id=target,
            device_id_type=MESH,
        ).start()

    def finish(self, u, k, layer, piece):
        _, order, starts = piece
        s = self.s
        src = s.done.at[u, rows(starts[1], HALVES[0])]
        dst = s.grads_out.at[k, rows(self.half * SHARE + starts[1], HALVES[0])]

        def hand(chip, sem):
            pltpu.make_async_remote_copy(
                src_ref=src, dst_ref=dst, send_sem=sem, recv_sem=s.out_recv,
                device_id=(layer, chip), device_id_type=MESH,
            ).start()

        hand(order[0][1][1], s.sent)
        pl.when(layer == self.c)(lambda: pltpu.make_async_copy(src, dst, s.out_sent).start())
        pl.when(layer != self.c)(lambda: hand(self.dp, s.out_sent))

    def wait(self, u, step, size):
        some = self.s.own.at[u, pl.ds(0, size)]
        pltpu.make_async_remote_copy(
            src_ref=some,
            dst_ref=some,
            send_sem=self.s.sent,
            recv_sem=self.s.recv.at[u, step],
            device_id=self.to_core,
            device_id_type=MESH,
        ).wait_recv()

    def add(self, u, piece, step):
        index, order, starts = piece
        s = self.s
        table = FLAT if index < 2 else TALL
        here = rows(starts[min(step + 1, len(order))], table[step])
        total = s.part[u, here] + s.land[u, self.landing(index, step)]
        if step < 3:
            s.part[u, here] = total
        else:
            s.done[u, here] = total

    def core_copy(self, u):
        return pltpu.make_async_remote_copy(
            src_ref=self.s.own.at[u, rows((1 - self.half) * SHARE, SHARE)],
            dst_ref=self.s.part.at[u],
            send_sem=self.s.core_sent,
            recv_sem=self.s.core_recv.at[u],
            device_id=self.to_core,
            device_id_type=MESH,
        )

    def stage(self, step, u, k, layer):
        s = self.s
        flat, tall = self.pieces[:2], self.pieces[2]
        both, everything = 2 * FLAT[2] + TALL[2], self.pieces
        if step == 0:
            self.core_copy(u).wait_recv()
            s.part[u] = s.part[u] + s.own[u, rows(self.half * SHARE, SHARE)]
            for piece in everything:
                self.send(u, piece, 0)
        elif step == 1:
            self.wait(u, 0, 3 * FLAT[0])
            for piece in everything:
                self.add(u, piece, 0)
                self.send(u, piece, 1)
        elif step == 2:
            self.wait(u, 1, 3 * FLAT[1])
            for piece in everything:
                self.add(u, piece, 1)
            self.send(u, tall, 2)

            @pl.when(self.end)
            def _():
                for piece in flat:
                    self.send(u, piece, 2)
        elif step == 3:
            pl.when(self.middle)(lambda: self.wait(u, 2, both))
            pl.when(self.end)(lambda: self.wait(u, 2, TALL[2]))
            self.add(u, tall, 2)
            self.send(u, tall, 3)

            @pl.when(self.middle)
            def _():
                for piece in flat:
                    self.add(u, piece, 2)
                    self.send(u, piece, 3)
        elif step == 4:
            pl.when(self.middle)(lambda: self.wait(u, 3, both))
            pl.when(self.end)(lambda: self.wait(u, 3, TALL[3]))
            self.add(u, tall, 3)
            self.send(u, tall, 4)

            @pl.when(self.middle)
            def _():
                for piece in flat:
                    self.add(u, piece, 3)
                    self.send(u, piece, 4)
                    self.send(u, piece, 5)
        elif step == 5:
            pl.when(self.middle)(lambda: self.wait(u, 4, TALL[4]))
            pl.when(self.end)(lambda: self.wait(u, 4, both))
            self.send(u, tall, 5)

            @pl.when(self.end)
            def _():
                for piece in flat:
                    self.send(u, piece, 5)
        elif step == 6:
            self.wait(u, 5, 3 * FLAT[5])
            for piece in everything:
                self.finish(u, k, layer, piece)

    def settle(self):
        def whole(units, size, send_sem):
            some = self.s.own.at[pl.ds(0, units), pl.ds(0, size)]
            return pltpu.make_async_remote_copy(
                src_ref=some, dst_ref=some, send_sem=send_sem, recv_sem=self.s.out_recv,
                device_id=self.to_core, device_id_type=MESH,
            )

        s = self.s
        half = 3 * HALVES[0]
        whole(UNITS, SHARE, s.core_sent).wait_send()
        whole(UNITS, half, s.out_sent).wait_send()
        sent = sum(TALL) + 2 * (FLAT[0] + FLAT[1] + FLAT[5] + FLAT[6])
        pl.when(self.middle)(lambda: whole(UNITS, sent + 2 * (FLAT[3] + FLAT[4]), s.sent).wait_send())
        pl.when(self.end)(lambda: whole(UNITS, sent + 2 * FLAT[2], s.sent).wait_send())
        whole(UNITS // 2, 3 * half, s.out_sent).wait_recv()

    def sum_gains(self, step):
        s = self.s
        total = s.gain_sum
        targets = (self.to_core, self.to_x, self.to_y, self.to_p, self.to_q)

        def copy(index):
            return pltpu.make_async_remote_copy(
                src_ref=total.at[index],
                dst_ref=s.gain_land.at[index],
                send_sem=s.gain_send,
                recv_sem=s.gain_recv.at[index],
                device_id=targets[index],
                device_id_type=MESH,
            )

        if step > 0:
            copy(step - 1).wait()
            total[step] = total[step - 1] + s.gain_land[step - 1]
        if step < 5:
            copy(step).start()


WEIGHTS = ("first_gain", "query", "key", "value", "output", "second_gain", "gate", "up", "down")
HANDED = (
    (("first_gain", 0),),
    (("query", 0), ("key", 0), ("value", 0)),
    (("output", 0),),
    (("second_gain", 0),),
    (("gate", 0), ("up", 0), ("down", 0)),
    (("gate", 1), ("up", 1), ("down", 1)),
)
EARLY, LATE = (0, 1), (2, 3, 4, 5)


def kernel(names, *refs):
    s = types.SimpleNamespace(**dict(zip(names, refs)))
    links = Links(s)
    c = links.c
    links.meet()

    token_copy = pltpu.make_async_copy(s.tokens.at[c], s.tok, s.in_sem.at[0])
    token_copy.start()
    cot_copy = pltpu.make_async_copy(s.cotangent.at[c], s.cot, s.in_sem.at[1])
    cot_copy.start()

    def place(name, half, layer):
        part = pl.ds(half * (FF // 2), FF // 2)
        where = {
            "first_gain": lambda: s.gain1.at[layer],
            "query": lambda: s.wqkv.at[layer, :, pl.ds(0, DIM)],
            "key": lambda: s.wqkv.at[layer, :, pl.ds(DIM, DIM)],
            "value": lambda: s.wqkv.at[layer, :, pl.ds(2 * DIM, DIM)],
            "output": lambda: s.wo.at[layer],
            "second_gain": lambda: s.gain2.at[layer],
            "gate": lambda: s.wg.at[layer, :, part],
            "up": lambda: s.wu.at[layer, :, part],
            "down": lambda: s.wd.at[layer, part, :],
        }
        return where[name]()

    def source(name, half):
        ref = getattr(s, "in_" + name)
        part = pl.ds(half * (FF // 2), FF // 2)
        if name.endswith("gain"):
            return ref
        return ref.at[0, :, part] if name in ("gate", "up") else ref.at[0, part, :] if name == "down" else ref.at[0]

    def weights_local(group, layer):
        for piece in HANDED[group]:
            pltpu.make_async_copy(source(*piece), place(*piece, layer), s.w_sem.at[layer, group]).start()

    def weights_copy(group, layer):
        for piece in HANDED[group]:
            pltpu.make_async_remote_copy(
                src_ref=place(*piece, layer) if group in EARLY else source(*piece),
                dst_ref=place(*piece, layer),
                send_sem=s.w_send.at[group],
                recv_sem=s.w_sem.at[layer, group],
                device_id=links.to_core,
                device_id_type=MESH,
            ).start()

    def group_wait(group, sem):
        some = (s.gain1.at[0], s.wqkv.at[0], s.wo.at[0], s.gain2.at[0], s.own.at[pl.ds(0, 2)], s.own.at[pl.ds(0, 2)])[group]
        pltpu.make_async_copy(some, some, sem).wait()

    def need(layer, *groups):
        for group in groups:
            group_wait(group, s.w_sem.at[layer, group])

    for group in EARLY + LATE:
        weights_local(group, c)

    need(c, *EARLY)
    links.met()
    for group in EARLY:
        weights_copy(group, c)

    ids = s.sample_ids[pl.ds(c, 1), :].astype(F32)
    count = [jnp.sum(jnp.where(ids == v, 1.0, 0.0), axis=-1, keepdims=True) for v in range(3)]
    first = jnp.where(
        count[0] == HALF,
        0.0,
        jnp.where(
            count[1] == HALF,
            count[0],
            jnp.where(count[2] == HALF, count[0] + count[1], count[0] + count[1] + count[2]),
        ),
    ).astype(jnp.int32)
    down_iota = lax.broadcasted_iota(jnp.int32, (SEQ, SEQ), 0)
    lane_iota = lax.broadcasted_iota(jnp.int32, (SEQ, SEQ), 1)
    moved = down_iota + first
    moved = jnp.where(moved >= SEQ, moved - SEQ, moved)
    perm = jnp.where(lane_iota == moved, 1.0, 0.0)
    ids_down = jnp.sum(perm[HALF:] * ids, axis=-1, keepdims=True)
    s.perm[...] = perm.astype(BF)
    moved = lane_iota + first
    moved = jnp.where(moved >= SEQ, moved - SEQ, moved)
    s.back[...] = jnp.where(down_iota == moved, 1.0, 0.0).astype(BF)
    ids_lane = mm(jnp.broadcast_to(ids, (16, SEQ)).astype(BF), s.back[:, HALF:])[:1]
    s.mask[...] = jnp.where(ids_down == ids_lane, 0.0, MASKED)

    token_copy.wait()
    s.x[0] = mm(s.perm[...], s.tok[...]).astype(BF)
    for group in LATE:
        weights_copy(group, c)
    cot_copy.wait()
    s.dy[...] = mm(s.perm[...], s.cot[...]).astype(BF)


    head0 = lax.broadcasted_iota(jnp.int32, (HALF, 128), 1) < HEAD_DIM

    def of_head(values, h):
        return jnp.where(head0 if h == 0 else ~head0, values, jnp.zeros_like(values))

    def output_row(layer, src, out, sems):
        @pl.when(layer == c)
        def _():
            pltpu.make_async_copy(src, out.at[c], sems.at[0]).start()

        @pl.when(layer != c)
        def _():
            pltpu.make_async_remote_copy(
                src_ref=src, dst_ref=out.at[c], send_sem=sems.at[1], recv_sem=sems.at[2],
                device_id=links.to_core, device_id_type=MESH,
            ).start()

    def output_settle(src, out, sems):
        pltpu.make_async_copy(src, out.at[c], sems.at[0]).wait()
        pltpu.make_async_remote_copy(
            src_ref=src, dst_ref=out.at[c], send_sem=sems.at[1], recv_sem=sems.at[2],
            device_id=links.to_core, device_id_type=MESH,
        ).wait()

    def forward(layer):
        x = s.x[layer].astype(F32)
        r = rsqrt_mean(x)
        s.r1[layer] = r
        pl.when(layer != c)(lambda: need(layer, *EARLY))
        a = (x * r * s.gain1[layer]).astype(BF)
        s.a[layer] = a
        for lo, hi in ((0, 512), (512, 1024), (1024, 1152)):
            part = mm(a, s.wqkv[layer, :, lo:hi])
            if lo == 0:
                s.qkv[layer, :, :DIM] = (part[:, :DIM] * HEAD_DIM ** (-0.5)).astype(BF)
                s.qkv[layer, :, DIM:hi] = part[:, DIM:].astype(BF)
            else:
                s.qkv[layer, :, lo:hi] = part.astype(BF)

        for pair, block in PARTS:
            at = pl.ds(block * HALF, HALF)
            q, k = [s.qkv[layer, at, lanes(pair, part)] for part in range(2)]
            for h in range(2):
                score = mm_nt(q, of_head(k, h))
                s.score[pair * 4 + block * 2 + h] = score + s.mask[...] if block == 1 else score
        for head in range(2 * HEADS):
            score = s.score[head]
            s.e[layer, head] = jnp.exp(score - jnp.max(score, axis=-1, keepdims=True)).astype(BF)
        for pair, block in PARTS:
            at = pl.ds(block * HALF, HALF)
            v = s.qkv[layer, at, lanes(pair, 2)]
            outs = [
                mm(s.e[layer, pair * 4 + block * 2 + h], jnp.where(head0 if h == 0 else ~head0, v, jnp.ones_like(v)))
                for h in range(2)
            ]
            inverse = 1.0 / pltpu.roll(jnp.where(head0, outs[1], outs[0]), HEAD_DIM, 1)
            s.inverse[layer, pair * 2 + block] = inverse
            s.o[layer, at, lanes(pair)] = (jnp.where(head0, outs[0], outs[1]) * inverse).astype(BF)

        need(layer, *LATE[:2])
        x1 = x + mm(s.o[layer], s.wo[layer])
        s.x1[layer] = x1
        r = rsqrt_mean(x1)
        s.r2[layer] = r
        s.b[layer] = (x1 * r * s.gain2[layer]).astype(BF)

    def hidden(layer, j):
        at = pl.ds(j * CHUNK, CHUNK)
        b = s.b[layer]
        g = mm(b, s.wg[layer, :, at])
        u = mm(b, s.wu[layer, :, at])
        sig = 1.0 / (1.0 + jnp.exp(-g))
        return at, g, u, sig

    def unroll(layer, low, out, dst, sems):
        out[layer] = mm(s.back[...], low[...]).astype(BF)
        output_row(layer, out.at[layer], dst, sems)

    @pl.loop(0, 2)
    def _(layer):
        forward(layer)

        @pl.when(layer == 0)
        def _():
            s.acc[...] = s.x1[0]

            for j in range(4):
                if j % 2 == 0:
                    need(0, LATE[2 + j // 2])
                at, g, u, sig = hidden(0, j)
                f = (g * sig * u).astype(BF)
                s.acc[...] += mm(f, s.wd[0, at, :])

            s.x[1] = s.acc[...].astype(BF)

    def put(u, start, values):
        size, width = values.shape
        for lo in range(0, width, 128):
            s.own[u, pl.ds(start, size), :] = values[:, lo : lo + 128].astype(BF)
            start += size
        return start

    def put_gain(layer, which, values):
        for i in range(DIM // 128):
            s.gain_sum[0, pl.ds(layer * 8 + which * 4 + i, 1), :] = values[:, i * 128 : (i + 1) * 128]

    def slot(turn, index):
        found = []
        for k in range(6):
            for step in range(STAGES):
                before, place = divmod(WHEN[k][step], SLOTS)
                if place == index and before < 2:
                    found.append((-step, -before, k))
        for step, before, k in sorted(found):
            if before == 0:
                links.stage(-step, 6 * turn + k, k, 1 - turn)
            else:
                pl.when(turn == 1)(functools.partial(links.stage, -step, k, k, 1))

    def after_compute():
        found = []
        for turn in range(2):
            for k in range(6):
                for step in range(STAGES):
                    place = turn * SLOTS + WHEN[k][step]
                    if place >= 2 * SLOTS:
                        found.append((place, -step, 6 * turn + k))
        return [(-step, u) for _, step, u in sorted(found)]

    def made(u):
        links.core_copy(u).start()

    need(1, *LATE[2:])
    s.gain_sum[0] = jnp.zeros((16, 128), F32)

    @pl.loop(0, 2)
    def _(turn):
        layer = 1 - turn
        base = turn * 6
        s.bt[...] = s.b[layer].T
        s.db[...] = jnp.zeros((SEQ, DIM), F32)

        for j in range(4):
            at, g, u, sig = hidden(layer, j)
            silu = g * sig
            f = (silu * u).astype(BF)
            dy = s.dy[...]
            df = mm_nt(dy, s.wd[layer, at, :])
            dg = (df * u * sig * (1.0 + g * (1.0 - sig))).astype(BF)
            du = (df * silu).astype(BF)
            s.f[:, at] = f
            nxt = put(base + j, 0, mm_tn(f, dy))
            nxt = put(base + j, nxt, mm(s.bt[...], dg))
            put(base + j, nxt, mm(s.bt[...], du))
            made(base + j)
            slot(turn, 2 * j)
            s.db[...] += mm_nt(dg, s.wg[layer, :, at]) + mm_nt(du, s.wu[layer, :, at])
            slot(turn, 2 * j + 1)

        @pl.when(layer == 1)
        def _():
            s.y[...] = (s.x1[1] + mm(s.f[...], s.wd[1])).astype(BF)

        db = s.db[...]
        r = s.r2[layer]
        normed = s.x1[layer] * r
        put_gain(layer, 1, jnp.sum(db * normed, axis=0, keepdims=True))
        part = db * s.gain2[layer]
        dx1 = s.dy[...].astype(F32) + r * (part - normed * jnp.mean(part * normed, axis=-1, keepdims=True))
        s.dx1[...] = dx1
        low = dx1.astype(BF)
        nxt = put(base + 4, 0, mm_tn(s.o[layer], low))
        s.do[...] = mm_nt(low, s.wo[layer]).astype(BF)
        slot(turn, 8)

        for pair, block in PARTS:
            at = pl.ds(block * HALF, HALF)
            q, k, v = [s.qkv[layer, at, lanes(pair, part)] for part in range(3)]
            do = s.do[at, lanes(pair)].astype(F32) * s.inverse[layer, pair * 2 + block]
            inner = do * s.o[layer, at, lanes(pair)].astype(F32)
            do = do.astype(BF)
            q_t, do_t = q.T, do.T
            dq, dk_t, dv_t = None, [], []
            for h in range(2):
                mine = slice(h * HEAD_DIM, (h + 1) * HEAD_DIM)
                expo = s.e[layer, pair * 4 + block * 2 + h]
                dv_t.append(mm(do_t[mine], expo))
                dp = mm_nt(do, of_head(v, h))
                ds = expo.astype(F32) * (dp - jnp.sum(of_head(inner, h), axis=-1, keepdims=True))
                ds = ds.astype(BF)
                term = mm(ds, of_head(k, h))
                dk_t.append(mm(q_t[mine], ds))
                dq = term if h == 0 else dq + term
            s.dqkv[at, lanes(pair, 0)] = (dq * HEAD_DIM ** (-0.5)).astype(BF)
            s.dqkv[at, lanes(pair, 1)] = jnp.concatenate(dk_t, 0).astype(BF).T
            s.dqkv[at, lanes(pair, 2)] = jnp.concatenate(dv_t, 0).astype(BF).T
            if block == 1:
                slot(turn, 9 + pair)

        s.at[...] = s.a[layer].T
        put(base + 4, nxt, mm(s.at[...], s.dqkv[:, :DIM]))
        made(base + 4)
        slot(turn, 12)
        nxt = put(base + 5, 0, mm(s.at[...], s.dqkv[:, DIM : 2 * DIM]))
        put(base + 5, nxt, mm(s.at[...], s.dqkv[:, 2 * DIM :]))
        made(base + 5)
        slot(turn, 13)

        da = mm_nt(s.dqkv[...], s.wqkv[layer])
        r = s.r1[layer]
        normed = s.x[layer].astype(F32) * r
        put_gain(layer, 0, jnp.sum(da * normed, axis=0, keepdims=True))
        part = da * s.gain1[layer]
        dx = s.dx1[...] + r * (part - normed * jnp.mean(part * normed, axis=-1, keepdims=True))
        low = dx.astype(BF)
        s.dy[...] = low
        s.dx[layer] = low
        slot(turn, 14)

    left = after_compute()
    beside = {2 + 2 * i: functools.partial(unroll, *row) for i, row in enumerate((
        (0, s.dx.at[0], s.dx_row, s.dx_out, s.dx_sem),
        (1, s.dx.at[1], s.dx_row, s.dx_out, s.dx_sem),
        (0, s.x.at[1], s.y_row, s.rows_out, s.y_sem),
        (1, s.y, s.y_row, s.rows_out, s.y_sem),
    ))}
    gap = max((len(left) - 4) // 5, 1)
    for index, (step, u) in enumerate(left):
        if index % gap == 0 and index // gap < 6:
            links.sum_gains(index // gap)
        links.stage(step, u, u % 6, 1 - u // 6)
        if index in beside:
            beside[index]()

    s.gains_out[...] = s.gain_sum[5, pl.ds(pl.multiple_of(c * 8, 8), 8), :]

    links.settle()

    for group in EARLY + LATE:
        group_wait(group, s.w_send.at[group])
    output_settle(s.y_row.at[0], s.rows_out, s.y_sem)
    output_settle(s.dx_row.at[0], s.dx_out, s.dx_sem)


def spread_kernel(*refs):
    s = types.SimpleNamespace(**dict(zip(SPREAD_NAMES, refs)))

    def store(index, src, dst):
        return pltpu.make_async_copy(src, dst, s.out_sem.at[index])

    stores = [store(0, s.rows_in, s.rows_out.at[0])]
    stores[0].start()

    @pl.loop(0, 2)
    def _(row):
        s.dx_wide[row] = s.dx_in[row].astype(F32)

    stores.append(store(7, s.dx_wide, s.dx_out.at[0]))
    stores[-1].start()

    def panels(u, first, size, wide, dst):
        for p in range(wide):
            dst[:, p * 128 : (p + 1) * 128] = s.units[u, pl.ds((first + p) * size, size), :].astype(F32)

    def chunk_stores(u):
        at = pl.ds(pl.multiple_of(u * CHUNK, CHUNK), CHUNK)
        return (
            store(8 + u, s.down_wide.at[u], s.down.at[0, at, :]),
            store(12 + u, s.gate_wide.at[u], s.gate.at[0, :, at]),
            store(16 + u, s.up_wide.at[u], s.up.at[0, :, at]),
        )

    @pl.loop(0, 4)
    def _(u):
        panels(u, 0, CHUNK, 3, s.down_wide.at[u])
        panels(u, 2, DIM, 2, s.gate_wide.at[u])
        panels(u, 4, DIM, 2, s.up_wide.at[u])
        for one in chunk_stores(u):
            one.start()

    squares = ((4, 0, s.output), (4, 3, s.query), (5, 0, s.key), (5, 3, s.value))
    for index, (u, first, out) in enumerate(squares):
        panels(u, first, DIM, 3, s.square.at[index])
        stores.append(store(1 + index, s.square.at[index], out.at[0]))
        stores[-1].start()
    for p in range(3):
        s.vectors[0:1, p * 128 : (p + 1) * 128] = s.gains_in[p : p + 1, :]
        s.vectors[8:9, p * 128 : (p + 1) * 128] = s.gains_in[4 + p : 5 + p, :]
    stores.append(store(5, s.vectors.at[pl.ds(0, 1)], s.first))
    stores.append(store(6, s.vectors.at[pl.ds(8, 1)], s.second))
    stores[-2].start()
    stores[-1].start()
    for one in stores:
        one.wait()

    @pl.loop(0, 4)
    def _(u):
        for one in chunk_stores(u):
            one.wait()


SPREAD_OUTS = {
    "rows_out": ((1, 2, SEQ, DIM), BF),
    "dx_out": ((1, 2, SEQ, DIM), F32),
    "first": ((1, DIM), F32),
    "query": ((1, DIM, DIM), F32),
    "key": ((1, DIM, DIM), F32),
    "value": ((1, DIM, DIM), F32),
    "output": ((1, DIM, DIM), F32),
    "second": ((1, DIM), F32),
    "gate": ((1, DIM, FF), F32),
    "up": ((1, DIM, FF), F32),
    "down": ((1, FF, DIM), F32),
}
SPREAD_SCRATCH = {
    "dx_wide": pltpu.VMEM((2, SEQ, DIM), F32),
    "square": pltpu.VMEM((4, DIM, DIM), F32),
    "vectors": pltpu.VMEM((16, DIM), F32),
    "down_wide": pltpu.VMEM((4, CHUNK, DIM), F32),
    "gate_wide": pltpu.VMEM((4, DIM, CHUNK), F32),
    "up_wide": pltpu.VMEM((4, DIM, CHUNK), F32),
    "out_sem": pltpu.SemaphoreType.DMA((20,)),
}
SPREAD_NAMES = ["units", "rows_in", "dx_in", "gains_in", *SPREAD_OUTS, *SPREAD_SCRATCH]


def spread(units, rows_in, dx_in, gains):
    anywhere = pl.BlockSpec(memory_space=pl.ANY)
    return pl.pallas_call(
        spread_kernel,
        in_specs=[pl.BlockSpec(memory_space=pltpu.VMEM)] * 4,
        out_specs=[anywhere] * len(SPREAD_OUTS),
        out_shape=[jax.ShapeDtypeStruct(*shape) for shape in SPREAD_OUTS.values()],
        scratch_shapes=list(SPREAD_SCRATCH.values()),
        compiler_params=pltpu.CompilerParams(vmem_limit_bytes=40 * 2**20),
    )(units, rows_in, dx_in, gains)


def layers(tokens, sample_ids, cotangent, *weights):
    anywhere = pl.BlockSpec(memory_space=pl.ANY)
    vmem = pl.BlockSpec(memory_space=pltpu.VMEM)
    inputs = ["tokens", "cotangent"] + ["in_" + name for name in WEIGHTS] + ["sample_ids"]
    outputs = {
        "grads_out": pltpu.VMEM((UNITS // 2, UNIT, 128), BF),
        "rows_out": pltpu.VMEM((2, SEQ, DIM), BF),
        "dx_out": pltpu.VMEM((2, SEQ, DIM), BF),
        "gains_out": pltpu.VMEM((8, 128), F32),
    }
    dma = pltpu.SemaphoreType.DMA
    scratch = {
        "tok": pltpu.VMEM((SEQ, DIM), BF),
        "cot": pltpu.VMEM((SEQ, DIM), BF),
        "gain1": pltpu.VMEM((2, 1, DIM), F32),
        "gain2": pltpu.VMEM((2, 1, DIM), F32),
        "wqkv": pltpu.VMEM((2, DIM, 3 * DIM), BF),
        "wo": pltpu.VMEM((2, DIM, DIM), BF),
        "wg": pltpu.VMEM((2, DIM, FF), BF),
        "wu": pltpu.VMEM((2, DIM, FF), BF),
        "wd": pltpu.VMEM((2, FF, DIM), BF),
        "perm": pltpu.VMEM((SEQ, SEQ), BF),
        "back": pltpu.VMEM((SEQ, SEQ), BF),
        "mask": pltpu.VMEM((HALF, HALF), F32),
        "x": pltpu.VMEM((2, SEQ, DIM), BF),
        "a": pltpu.VMEM((2, SEQ, DIM), BF),
        "qkv": pltpu.VMEM((2, SEQ, 3 * DIM), BF),
        "score": pltpu.VMEM((2 * HEADS, HALF, HALF), F32),
        "e": pltpu.VMEM((2, 2 * HEADS, HALF, HALF), BF),
        "inverse": pltpu.VMEM((2, HEADS, HALF, 128), F32),
        "f": pltpu.VMEM((SEQ, FF), BF),
        "o": pltpu.VMEM((2, SEQ, DIM), BF),
        "x1": pltpu.VMEM((2, SEQ, DIM), F32),
        "b": pltpu.VMEM((2, SEQ, DIM), BF),
        "r1": pltpu.VMEM((2, SEQ, 1), F32),
        "r2": pltpu.VMEM((2, SEQ, 1), F32),
        "acc": pltpu.VMEM((SEQ, DIM), F32),
        "bt": pltpu.VMEM((DIM, SEQ), BF),
        "at": pltpu.VMEM((DIM, SEQ), BF),
        "db": pltpu.VMEM((SEQ, DIM), F32),
        "dy": pltpu.VMEM((SEQ, DIM), BF),
        "dx1": pltpu.VMEM((SEQ, DIM), F32),
        "dx": pltpu.VMEM((2, SEQ, DIM), BF),
        "y": pltpu.VMEM((SEQ, DIM), BF),
        "do": pltpu.VMEM((SEQ, DIM), BF),
        "dqkv": pltpu.VMEM((SEQ, 3 * DIM), BF),
        "y_row": pltpu.VMEM((2, SEQ, DIM), BF),
        "dx_row": pltpu.VMEM((2, SEQ, DIM), BF),
        "own": pltpu.VMEM((UNITS, UNIT, 128), BF),
        "part": pltpu.VMEM((UNITS, SHARE, 128), BF),
        "land": pltpu.VMEM((UNITS, LAND_ROWS, 128), BF),
        "done": pltpu.VMEM((UNITS, SHARE, 128), BF),
        "gain_sum": pltpu.VMEM((6, 16, 128), F32),
        "gain_land": pltpu.VMEM((5, 16, 128), F32),
        "in_sem": dma((2,)),
        "w_sem": dma((2, len(HANDED))),
        "w_send": dma((len(HANDED),)),
        "sent": dma,
        "recv": dma((UNITS, STAGES - 1)),
        "core_sent": dma,
        "core_recv": dma((UNITS,)),
        "out_sent": dma,
        "out_recv": dma,
        "gain_send": dma,
        "gain_recv": dma((5,)),
        "y_sem": dma((3,)),
        "dx_sem": dma((3,)),
    }
    names = inputs + list(outputs) + list(scratch)
    return pl.pallas_call(
        functools.partial(kernel, names),
        out_shape=list(outputs.values()),
        in_specs=[anywhere] * (len(inputs) - 1) + [vmem],
        out_specs=[anywhere, anywhere, anywhere, vmem],
        scratch_shapes=list(scratch.values()),
        compiler_params=pltpu.CompilerParams(
            collective_id=0, has_side_effects=True, vmem_limit_bytes=54 * 2**20
        ),
        cost_estimate=pl.CostEstimate(flops=15 * 10**9, bytes_accessed=10**7, transcendentals=4 * 10**6),
    )(tokens, cotangent, *weights, sample_ids)


def solution(mesh):
    count = mesh.shape["dp"]

    def per_device(tokens, sample_ids, cotangent, *weights):
        units, rows_out, dx_out, gains = layers(tokens, sample_ids, cotangent, *weights)
        outs = spread(units, rows_out, dx_out, gains)
        if count > GROUP:
            members = [[g * GROUP + i for g in range(count // GROUP)] for i in range(GROUP)]
            outs = list(outs[:2]) + list(lax.psum(tuple(outs[2:]), "dp", axis_index_groups=members))
        return tuple(outs)

    matrix = P("section", None, None)
    vector = P("section", None)
    rows4 = P("section", "dp", None, None)
    grads = (vector, matrix, matrix, matrix, matrix, vector, matrix, matrix, matrix)
    return jax.shard_map(
        per_device,
        mesh=mesh,
        in_specs=(P("dp", None, None), P("dp", None), P("dp", None, None)) + grads,
        out_specs=(rows4, rows4) + grads,
        check_vma=False,
    )
```

```python
import functools
import types

import jax
import jax.numpy as jnp
from jax import lax
from jax.experimental import pallas as pl
from jax.experimental.pallas import tpu as pltpu
from jax.sharding import PartitionSpec as P

MESH = pl.DeviceIdType.MESH
BF = jnp.bfloat16
F32 = jnp.float32
HEADS = 6
HEAD_DIM = 64
NORM_EPS = 1e-05
MASKED = -1e30
GROUP = 16

SEQ = 512
DIM = 384
FF = 1024
HALF = SEQ // 2
CHUNK = FF // 4
UNITS = 12
UNIT = 2304
SHARE = UNIT // 2
PIECE = SHARE // 3
SLOTS = 15
WHEN = (
    (2, 7, 12, 18, 22, 26, 35),
    (4, 9, 14, 18, 23, 29, 38),
    (6, 13, 17, 21, 25, 30, 41),
    (8, 13, 18, 22, 26, 36, 47),
    (14, 18, 22, 26, 31, 37, 44),
    (15, 19, 24, 28, 33, 40, 48),
)
HALVES = (PIECE // 2, PIECE // 4, PIECE // 8)
STAGES = 7
FLAT = (PIECE // 2, PIECE // 4, PIECE // 4, PIECE // 4, PIECE // 4, PIECE // 4, PIECE // 2)
TALL = (PIECE // 2, PIECE // 4, PIECE // 8, PIECE // 8, PIECE // 8, PIECE // 4, PIECE // 2)
FLAT_LAND = sum(FLAT[:4])
LAND_ROWS = 2 * FLAT_LAND + sum(TALL[:4])


def mm(a, b):
    return lax.dot_general(a, b, (((1,), (0,)), ((), ())), preferred_element_type=F32)


def mm_nt(a, b):
    return lax.dot_general(a, b, (((1,), (1,)), ((), ())), preferred_element_type=F32)


def mm_tn(a, b):
    return lax.dot_general(a, b, (((0,), (0,)), ((), ())), preferred_element_type=F32)


def rsqrt_mean(values):
    return lax.rsqrt(jnp.mean(values * values, axis=-1, keepdims=True) + NORM_EPS)


PARTS = [(pair, block) for pair in range(HEADS // 2) for block in range(2)]


def lanes(pair, part=0):
    return pl.ds(part * DIM + pair * 2 * HEAD_DIM, 2 * HEAD_DIM)


def rows(start, size):
    return pl.ds(pl.multiple_of(start, 16), size)


class Links:
    def __init__(self, s):
        self.s = s
        self.c = lax.axis_index("section")
        self.dp = lax.axis_index("dp")
        local = lax.rem(self.dp, GROUP)
        x = lax.rem(local, 2)
        y = lax.rem(lax.div(local, 2), 2)
        z = lax.div(local, 4)
        p = lax.rem(z, 2)
        q = lax.div(z, 2)
        c = self.c
        self.half = h = lax.rem(c + x + y + z, 2)
        self.middle = (z == 1) | (z == 2)
        self.end = (z == 0) | (z == 3)
        self.to_core = (1 - c, self.dp)
        step_x, step_y = 1 - 2 * x, 2 - 4 * y
        self.to_x = (1 - c, self.dp + step_x)
        self.to_y = (1 - c, self.dp + step_y)
        self.to_p = (1 - c, self.dp + 4 - 8 * p)
        self.to_q = (c, self.dp + 8 - 16 * q)
        self.to_m = (1 - c, self.dp + 4 - 8 * q)
        along_x, along_y, along_p = (x, self.to_x), (y, self.to_y), (p, self.to_p)
        one = (x + h * (y - x), (1 - c, self.dp + step_x + h * (step_y - step_x)))
        two = (y + h * (x - y), (1 - c, self.dp + step_y + h * (step_x - step_y)))
        orders = ((along_x, along_y), (along_y, along_x), (along_p, one, two))
        self.pieces = []
        for index, order in enumerate(orders):
            starts = [index * PIECE]
            for (bit, _), size in zip(order, HALVES):
                starts.append(starts[-1] + bit * size)
            self.pieces.append((index, order, starts))

    def meet(self):
        barrier = pltpu.get_barrier_semaphore()
        others = [(1 - self.c, target[1]) for target in (self.to_x, self.to_y, self.to_p)]
        for target in (self.to_core, self.to_x, self.to_y, self.to_p, self.to_q, *others):
            pl.semaphore_signal(barrier, inc=1, device_id=target, device_id_type=MESH)

        @pl.when(self.middle)
        def _():
            pl.semaphore_signal(barrier, inc=1, device_id=self.to_m, device_id_type=MESH)

    def met(self):
        barrier = pltpu.get_barrier_semaphore()

        @pl.when(self.middle)
        def _():
            pl.semaphore_wait(barrier, 9)

        @pl.when(self.end)
        def _():
            pl.semaphore_wait(barrier, 8)

    def landing(self, index, step):
        table = FLAT if index < 2 else TALL
        return pl.ds(index * FLAT_LAND + sum(table[:step]), table[step])

    def send(self, u, piece, step):
        index, order, starts = piece
        s = self.s
        table = FLAT if index < 2 else TALL
        halvings = len(order)
        if step < halvings:
            bit, target = order[step]
            src = s.part.at[u, rows(starts[step] + (1 - bit) * table[step], table[step])]
        elif step < 4:
            target = self.to_p if step == 2 else self.to_m if index < 2 else self.to_q
            src = s.part.at[u, rows(starts[halvings], table[step])]
        else:
            back = min(6 - step, halvings)
            target = order[back][1] if back < halvings else self.to_p
            src = s.done.at[u, rows(starts[min(back + 1, halvings)], table[step])]
        pltpu.make_async_remote_copy(
            src_ref=src,
            dst_ref=s.land.at[u, self.landing(index, step)] if step < 4 else src,
            send_sem=s.sent,
            recv_sem=s.recv.at[u, step],
            device_id=target,
            device_id_type=MESH,
        ).start()

    def finish(self, u, k, layer, piece):
        _, order, starts = piece
        s = self.s
        src = s.done.at[u, rows(starts[1], HALVES[0])]
        dst = s.grads_out.at[k, rows(self.half * SHARE + starts[1], HALVES[0])]

        def hand(chip, sem):
            pltpu.make_async_remote_copy(
                src_ref=src, dst_ref=dst, send_sem=sem, recv_sem=s.out_recv,
                device_id=(layer, chip), device_id_type=MESH,
            ).start()

        hand(order[0][1][1], s.sent)
        pl.when(layer == self.c)(lambda: pltpu.make_async_copy(src, dst, s.out_sent).start())
        pl.when(layer != self.c)(lambda: hand(self.dp, s.out_sent))

    def wait(self, u, step, size):
        some = self.s.own.at[u, pl.ds(0, size)]
        pltpu.make_async_remote_copy(
            src_ref=some,
            dst_ref=some,
            send_sem=self.s.sent,
            recv_sem=self.s.recv.at[u, step],
            device_id=self.to_core,
            device_id_type=MESH,
        ).wait_recv()

    def add(self, u, piece, step):
        index, order, starts = piece
        s = self.s
        table = FLAT if index < 2 else TALL
        here = rows(starts[min(step + 1, len(order))], table[step])
        total = s.part[u, here] + s.land[u, self.landing(index, step)]
        if step < 3:
            s.part[u, here] = total
        else:
            s.done[u, here] = total

    def core_copy(self, u):
        return pltpu.make_async_remote_copy(
            src_ref=self.s.own.at[u, rows((1 - self.half) * SHARE, SHARE)],
            dst_ref=self.s.part.at[u],
            send_sem=self.s.core_sent,
            recv_sem=self.s.core_recv.at[u],
            device_id=self.to_core,
            device_id_type=MESH,
        )

    def stage(self, step, u, k, layer):
        s = self.s
        flat, tall = self.pieces[:2], self.pieces[2]
        both, everything = 2 * FLAT[2] + TALL[2], self.pieces
        if step == 0:
            self.core_copy(u).wait_recv()
            for piece in everything:
                begin = piece[0] * PIECE
                here = pl.ds(begin, PIECE)
                s.part[u, here] = s.part[u, here] + s.own[u, rows(self.half * SHARE + begin, PIECE)]
                self.send(u, piece, 0)
        elif step == 1:
            self.wait(u, 0, 3 * FLAT[0])
            for piece in everything:
                self.add(u, piece, 0)
                self.send(u, piece, 1)
        elif step == 2:
            self.wait(u, 1, 3 * FLAT[1])
            self.add(u, tall, 1)
            self.send(u, tall, 2)
            for piece in flat:
                self.add(u, piece, 1)
                pl.when(self.end)(functools.partial(self.send, u, piece, 2))
        elif step == 3:
            pl.when(self.middle)(lambda: self.wait(u, 2, both))
            pl.when(self.end)(lambda: self.wait(u, 2, TALL[2]))
            self.add(u, tall, 2)
            self.send(u, tall, 3)

            @pl.when(self.middle)
            def _():
                for piece in flat:
                    self.add(u, piece, 2)
                    self.send(u, piece, 3)
        elif step == 4:
            pl.when(self.middle)(lambda: self.wait(u, 3, both))
            pl.when(self.end)(lambda: self.wait(u, 3, TALL[3]))
            self.add(u, tall, 3)
            self.send(u, tall, 4)

            @pl.when(self.middle)
            def _():
                for piece in flat:
                    self.add(u, piece, 3)
                    self.send(u, piece, 4)
                    self.send(u, piece, 5)
        elif step == 5:
            pl.when(self.middle)(lambda: self.wait(u, 4, TALL[4]))
            pl.when(self.end)(lambda: self.wait(u, 4, both))
            self.send(u, tall, 5)

            @pl.when(self.end)
            def _():
                for piece in flat:
                    self.send(u, piece, 5)
        elif step == 6:
            self.wait(u, 5, 3 * FLAT[5])
            for piece in everything:
                self.finish(u, k, layer, piece)

    def settle(self):
        def whole(units, size, send_sem):
            some = self.s.own.at[pl.ds(0, units), pl.ds(0, size)]
            return pltpu.make_async_remote_copy(
                src_ref=some, dst_ref=some, send_sem=send_sem, recv_sem=self.s.out_recv,
                device_id=self.to_core, device_id_type=MESH,
            )

        s = self.s
        half = 3 * HALVES[0]
        whole(UNITS, SHARE, s.core_sent).wait_send()
        whole(UNITS, half, s.out_sent).wait_send()
        sent = sum(TALL) + 2 * (FLAT[0] + FLAT[1] + FLAT[5] + FLAT[6])
        pl.when(self.middle)(lambda: whole(UNITS, sent + 2 * (FLAT[3] + FLAT[4]), s.sent).wait_send())
        pl.when(self.end)(lambda: whole(UNITS, sent + 2 * FLAT[2], s.sent).wait_send())
        whole(UNITS // 2, 3 * half, s.out_sent).wait_recv()

    def sum_gains(self, step):
        s = self.s
        total = s.gain_sum
        targets = (self.to_core, self.to_x, self.to_y, self.to_p, self.to_q)

        def copy(index):
            return pltpu.make_async_remote_copy(
                src_ref=total.at[index],
                dst_ref=s.gain_land.at[index],
                send_sem=s.gain_send,
                recv_sem=s.gain_recv.at[index],
                device_id=targets[index],
                device_id_type=MESH,
            )

        if step > 0:
            copy(step - 1).wait()
            total[step] = total[step - 1] + s.gain_land[step - 1]
        if step < 5:
            copy(step).start()


WEIGHTS = ("first_gain", "query", "key", "value", "output", "second_gain", "gate", "up", "down")
HANDED = (
    (("first_gain", 0),),
    (("query", 0), ("key", 0), ("value", 0)),
    (("output", 0),),
    (("second_gain", 0),),
    (("gate", 0), ("up", 0), ("down", 0)),
    (("gate", 1), ("up", 1), ("down", 1)),
)
EARLY, LATE = (0, 1), (2, 3, 4, 5)


def kernel(names, *refs):
    s = types.SimpleNamespace(**dict(zip(names, refs)))
    links = Links(s)
    c = links.c
    links.meet()

    token_copy = pltpu.make_async_copy(s.tokens.at[c], s.tok, s.in_sem.at[0])
    token_copy.start()
    cot_copy = pltpu.make_async_copy(s.cotangent.at[c], s.cot, s.in_sem.at[1])
    cot_copy.start()

    def place(name, half, layer):
        part = pl.ds(half * (FF // 2), FF // 2)
        where = {
            "first_gain": lambda: s.gain1.at[layer],
            "query": lambda: s.wqkv.at[layer, :, pl.ds(0, DIM)],
            "key": lambda: s.wqkv.at[layer, :, pl.ds(DIM, DIM)],
            "value": lambda: s.wqkv.at[layer, :, pl.ds(2 * DIM, DIM)],
            "output": lambda: s.wo.at[layer],
            "second_gain": lambda: s.gain2.at[layer],
            "gate": lambda: s.wg.at[layer, :, part],
            "up": lambda: s.wu.at[layer, :, part],
            "down": lambda: s.wd.at[layer, part, :],
        }
        return where[name]()

    def source(name, half):
        ref = getattr(s, "in_" + name)
        part = pl.ds(half * (FF // 2), FF // 2)
        if name.endswith("gain"):
            return ref
        return ref.at[0, :, part] if name in ("gate", "up") else ref.at[0, part, :] if name == "down" else ref.at[0]

    def weights_local(group, layer):
        for piece in HANDED[group]:
            pltpu.make_async_copy(source(*piece), place(*piece, layer), s.w_sem.at[layer, group]).start()

    def weights_copy(group, layer):
        for piece in HANDED[group]:
            pltpu.make_async_remote_copy(
                src_ref=place(*piece, layer) if group in EARLY else source(*piece),
                dst_ref=place(*piece, layer),
                send_sem=s.w_send.at[group],
                recv_sem=s.w_sem.at[layer, group],
                device_id=links.to_core,
                device_id_type=MESH,
            ).start()

    def group_wait(group, sem):
        some = (s.gain1.at[0], s.wqkv.at[0], s.wo.at[0], s.gain2.at[0], s.own.at[pl.ds(0, 2)], s.own.at[pl.ds(0, 2)])[group]
        pltpu.make_async_copy(some, some, sem).wait()

    def need(layer, *groups):
        for group in groups:
            group_wait(group, s.w_sem.at[layer, group])

    for group in EARLY + LATE:
        weights_local(group, c)

    need(c, *EARLY)
    links.met()
    for group in EARLY:
        weights_copy(group, c)

    ids = s.sample_ids[pl.ds(c, 1), :].astype(F32)
    count = [jnp.sum(jnp.where(ids == v, 1.0, 0.0), axis=-1, keepdims=True) for v in range(3)]
    first = jnp.where(
        count[0] == HALF,
        0.0,
        jnp.where(
            count[1] == HALF,
            count[0],
            jnp.where(count[2] == HALF, count[0] + count[1], count[0] + count[1] + count[2]),
        ),
    ).astype(jnp.int32)
    down_iota = lax.broadcasted_iota(jnp.int32, (SEQ, SEQ), 0)
    lane_iota = lax.broadcasted_iota(jnp.int32, (SEQ, SEQ), 1)
    moved = down_iota + first
    moved = jnp.where(moved >= SEQ, moved - SEQ, moved)
    perm = jnp.where(lane_iota == moved, 1.0, 0.0)
    ids_down = jnp.sum(perm[HALF:] * ids, axis=-1, keepdims=True)
    s.perm[...] = perm.astype(BF)
    moved = lane_iota + first
    moved = jnp.where(moved >= SEQ, moved - SEQ, moved)
    s.back[...] = jnp.where(down_iota == moved, 1.0, 0.0).astype(BF)
    ids_lane = mm(jnp.broadcast_to(ids, (16, SEQ)).astype(BF), s.back[:, HALF:])[:1]
    s.mask[...] = jnp.where(ids_down == ids_lane, 0.0, MASKED)

    token_copy.wait()
    s.x[0] = mm(s.perm[...], s.tok[...]).astype(BF)
    for group in LATE:
        weights_copy(group, c)
    cot_copy.wait()
    s.dy[...] = mm(s.perm[...], s.cot[...]).astype(BF)


    head0 = lax.broadcasted_iota(jnp.int32, (HALF, 128), 1) < HEAD_DIM

    def of_head(values, h):
        return jnp.where(head0 if h == 0 else ~head0, values, jnp.zeros_like(values))

    def output_row(layer, src, out, sems):
        @pl.when(layer == c)
        def _():
            pltpu.make_async_copy(src, out.at[c], sems.at[0]).start()

        @pl.when(layer != c)
        def _():
            pltpu.make_async_remote_copy(
                src_ref=src, dst_ref=out.at[c], send_sem=sems.at[1], recv_sem=sems.at[2],
                device_id=links.to_core, device_id_type=MESH,
            ).start()

    def output_settle(src, out, sems):
        pltpu.make_async_copy(src, out.at[c], sems.at[0]).wait()
        pltpu.make_async_remote_copy(
            src_ref=src, dst_ref=out.at[c], send_sem=sems.at[1], recv_sem=sems.at[2],
            device_id=links.to_core, device_id_type=MESH,
        ).wait()

    def forward(layer):
        x = s.x[layer].astype(F32)
        r = rsqrt_mean(x)
        s.r1[layer] = r
        pl.when(layer != c)(lambda: need(layer, *EARLY))
        a = (x * r * s.gain1[layer]).astype(BF)
        s.a[layer] = a
        for lo, hi in ((0, 512), (512, 1024), (1024, 1152)):
            part = mm(a, s.wqkv[layer, :, lo:hi])
            if lo == 0:
                s.qkv[layer, :, :DIM] = (part[:, :DIM] * HEAD_DIM ** (-0.5)).astype(BF)
                s.qkv[layer, :, DIM:hi] = part[:, DIM:].astype(BF)
            else:
                s.qkv[layer, :, lo:hi] = part.astype(BF)

        for pair, block in PARTS:
            at = pl.ds(block * HALF, HALF)
            q, k = [s.qkv[layer, at, lanes(pair, part)] for part in range(2)]
            for h in range(2):
                score = mm_nt(q, of_head(k, h))
                s.score[pair * 4 + block * 2 + h] = score + s.mask[...] if block == 1 else score
        for head in range(2 * HEADS):
            score = s.score[head]
            s.e[layer, head] = jnp.exp(score - jnp.max(score, axis=-1, keepdims=True)).astype(BF)
        for pair, block in PARTS:
            at = pl.ds(block * HALF, HALF)
            v = s.qkv[layer, at, lanes(pair, 2)]
            outs = [
                mm(s.e[layer, pair * 4 + block * 2 + h], jnp.where(head0 if h == 0 else ~head0, v, jnp.ones_like(v)))
                for h in range(2)
            ]
            inverse = 1.0 / pltpu.roll(jnp.where(head0, outs[1], outs[0]), HEAD_DIM, 1)
            s.inverse[layer, pair * 2 + block] = inverse
            s.o[layer, at, lanes(pair)] = (jnp.where(head0, outs[0], outs[1]) * inverse).astype(BF)

        need(layer, *LATE[:2])
        x1 = x + mm(s.o[layer], s.wo[layer])
        s.x1[layer] = x1
        r = rsqrt_mean(x1)
        s.r2[layer] = r
        s.b[layer] = (x1 * r * s.gain2[layer]).astype(BF)

    def hidden(layer, j):
        at = pl.ds(j * CHUNK, CHUNK)
        b = s.b[layer]
        g = mm(b, s.wg[layer, :, at])
        u = mm(b, s.wu[layer, :, at])
        sig = 1.0 / (1.0 + jnp.exp(-g))
        return at, g, u, sig

    def unroll(layer, low, out, dst, sems):
        out[layer] = mm(s.back[...], low[...]).astype(BF)
        output_row(layer, out.at[layer], dst, sems)

    @pl.loop(0, 2)
    def _(layer):
        forward(layer)

        @pl.when(layer == 0)
        def _():
            s.acc[...] = s.x1[0]

            for j in range(4):
                if j % 2 == 0:
                    need(0, LATE[2 + j // 2])
                at, g, u, sig = hidden(0, j)
                f = (g * sig * u).astype(BF)
                s.acc[...] += mm(f, s.wd[0, at, :])

            s.x[1] = s.acc[...].astype(BF)

    def put(u, start, values):
        size, width = values.shape
        for lo in range(0, width, 128):
            s.own[u, pl.ds(start, size), :] = values[:, lo : lo + 128].astype(BF)
            start += size
        return start

    def put_gain(layer, which, values):
        for i in range(DIM // 128):
            s.gain_sum[0, pl.ds(layer * 8 + which * 4 + i, 1), :] = values[:, i * 128 : (i + 1) * 128]

    def slot(turn, index):
        found = []
        for k in range(6):
            for step in range(STAGES):
                before, place = divmod(WHEN[k][step], SLOTS)
                if place == index and before < 2:
                    found.append((-step, -before, k))
        for step, before, k in sorted(found):
            if before == 0:
                links.stage(-step, 6 * turn + k, k, 1 - turn)
            else:
                pl.when(turn == 1)(functools.partial(links.stage, -step, k, k, 1))

    def after_compute():
        found = []
        for turn in range(2):
            for k in range(6):
                for step in range(STAGES):
                    place = turn * SLOTS + WHEN[k][step]
                    if place >= 2 * SLOTS:
                        found.append((place, -step, 6 * turn + k))
        return [(-step, u) for _, step, u in sorted(found)]

    def made(u):
        links.core_copy(u).start()

    need(1, *LATE[2:])
    s.gain_sum[0] = jnp.zeros((16, 128), F32)

    @pl.loop(0, 2)
    def _(turn):
        layer = 1 - turn
        base = turn * 6
        s.bt[...] = s.b[layer].T
        s.db[...] = jnp.zeros((SEQ, DIM), F32)

        for j in range(4):
            at, g, u, sig = hidden(layer, j)
            silu = g * sig
            f = (silu * u).astype(BF)
            dy = s.dy[...]
            df = mm_nt(dy, s.wd[layer, at, :])
            dg = (df * u * sig * (1.0 + g * (1.0 - sig))).astype(BF)
            du = (df * silu).astype(BF)
            s.f[:, at] = f
            nxt = put(base + j, 0, mm_tn(f, dy))
            nxt = put(base + j, nxt, mm(s.bt[...], dg))
            put(base + j, nxt, mm(s.bt[...], du))
            made(base + j)
            slot(turn, 2 * j)
            s.db[...] += mm_nt(dg, s.wg[layer, :, at]) + mm_nt(du, s.wu[layer, :, at])
            slot(turn, 2 * j + 1)

        @pl.when(layer == 1)
        def _():
            s.y[...] = (s.x1[1] + mm(s.f[...], s.wd[1])).astype(BF)

        db = s.db[...]
        r = s.r2[layer]
        normed = s.x1[layer] * r
        put_gain(layer, 1, jnp.sum(db * normed, axis=0, keepdims=True))
        part = db * s.gain2[layer]
        dx1 = s.dy[...].astype(F32) + r * (part - normed * jnp.mean(part * normed, axis=-1, keepdims=True))
        s.dx1[...] = dx1
        low = dx1.astype(BF)
        nxt = put(base + 4, 0, mm_tn(s.o[layer], low))
        s.do[...] = mm_nt(low, s.wo[layer]).astype(BF)
        slot(turn, 8)

        for pair, block in PARTS:
            at = pl.ds(block * HALF, HALF)
            q, k, v = [s.qkv[layer, at, lanes(pair, part)] for part in range(3)]
            do = s.do[at, lanes(pair)].astype(F32) * s.inverse[layer, pair * 2 + block]
            inner = do * s.o[layer, at, lanes(pair)].astype(F32)
            do = do.astype(BF)
            q_t, do_t = q.T, do.T
            dq, dk_t, dv_t = None, [], []
            for h in range(2):
                mine = slice(h * HEAD_DIM, (h + 1) * HEAD_DIM)
                expo = s.e[layer, pair * 4 + block * 2 + h]
                dv_t.append(mm(do_t[mine], expo))
                dp = mm_nt(do, of_head(v, h))
                ds = expo.astype(F32) * (dp - jnp.sum(of_head(inner, h), axis=-1, keepdims=True))
                ds = ds.astype(BF)
                term = mm(ds, of_head(k, h))
                dk_t.append(mm(q_t[mine], ds))
                dq = term if h == 0 else dq + term
            s.dqkv[at, lanes(pair, 0)] = (dq * HEAD_DIM ** (-0.5)).astype(BF)
            s.dqkv[at, lanes(pair, 1)] = jnp.concatenate(dk_t, 0).astype(BF).T
            s.dqkv[at, lanes(pair, 2)] = jnp.concatenate(dv_t, 0).astype(BF).T
            if block == 1:
                slot(turn, 9 + pair)

        s.at[...] = s.a[layer].T
        put(base + 4, nxt, mm(s.at[...], s.dqkv[:, :DIM]))
        made(base + 4)
        slot(turn, 12)
        nxt = put(base + 5, 0, mm(s.at[...], s.dqkv[:, DIM : 2 * DIM]))
        put(base + 5, nxt, mm(s.at[...], s.dqkv[:, 2 * DIM :]))
        made(base + 5)
        slot(turn, 13)

        da = mm_nt(s.dqkv[...], s.wqkv[layer])
        r = s.r1[layer]
        normed = s.x[layer].astype(F32) * r
        put_gain(layer, 0, jnp.sum(da * normed, axis=0, keepdims=True))
        part = da * s.gain1[layer]
        dx = s.dx1[...] + r * (part - normed * jnp.mean(part * normed, axis=-1, keepdims=True))
        low = dx.astype(BF)
        s.dy[...] = low
        s.dx[layer] = low
        slot(turn, 14)

    left = after_compute()
    beside = {2 + 2 * i: functools.partial(unroll, *row) for i, row in enumerate((
        (0, s.dx.at[0], s.dx_row, s.dx_out, s.dx_sem),
        (1, s.dx.at[1], s.dx_row, s.dx_out, s.dx_sem),
        (0, s.x.at[1], s.y_row, s.rows_out, s.y_sem),
        (1, s.y, s.y_row, s.rows_out, s.y_sem),
    ))}
    gap = max((len(left) - 4) // 5, 1)
    for index, (step, u) in enumerate(left):
        if index % gap == 0 and index // gap < 6:
            links.sum_gains(index // gap)
        links.stage(step, u, u % 6, 1 - u // 6)
        if index in beside:
            beside[index]()

    s.gains_out[...] = s.gain_sum[5, pl.ds(pl.multiple_of(c * 8, 8), 8), :]

    links.settle()

    for group in EARLY + LATE:
        group_wait(group, s.w_send.at[group])
    output_settle(s.y_row.at[0], s.rows_out, s.y_sem)
    output_settle(s.dx_row.at[0], s.dx_out, s.dx_sem)


def spread_kernel(*refs):
    s = types.SimpleNamespace(**dict(zip(SPREAD_NAMES, refs)))

    def store(index, src, dst):
        return pltpu.make_async_copy(src, dst, s.out_sem.at[index])

    stores = [store(0, s.rows_in, s.rows_out.at[0])]
    stores[0].start()

    @pl.loop(0, 2)
    def _(row):
        s.dx_wide[row] = s.dx_in[row].astype(F32)

    stores.append(store(7, s.dx_wide, s.dx_out.at[0]))
    stores[-1].start()

    def panels(u, first, size, wide, dst):
        for p in range(wide):
            dst[:, p * 128 : (p + 1) * 128] = s.units[u, pl.ds((first + p) * size, size), :].astype(F32)

    def chunk_stores(u):
        at = pl.ds(pl.multiple_of(u * CHUNK, CHUNK), CHUNK)
        return (
            store(8 + u, s.down_wide.at[u], s.down.at[0, at, :]),
            store(12 + u, s.gate_wide.at[u], s.gate.at[0, :, at]),
            store(16 + u, s.up_wide.at[u], s.up.at[0, :, at]),
        )

    @pl.loop(0, 4)
    def _(u):
        panels(u, 0, CHUNK, 3, s.down_wide.at[u])
        panels(u, 2, DIM, 2, s.gate_wide.at[u])
        panels(u, 4, DIM, 2, s.up_wide.at[u])
        for one in chunk_stores(u):
            one.start()

    squares = ((4, 0, s.output), (4, 3, s.query), (5, 0, s.key), (5, 3, s.value))
    for index, (u, first, out) in enumerate(squares):
        panels(u, first, DIM, 3, s.square.at[index])
        stores.append(store(1 + index, s.square.at[index], out.at[0]))
        stores[-1].start()
    for p in range(3):
        s.vectors[0:1, p * 128 : (p + 1) * 128] = s.gains_in[p : p + 1, :]
        s.vectors[8:9, p * 128 : (p + 1) * 128] = s.gains_in[4 + p : 5 + p, :]
    stores.append(store(5, s.vectors.at[pl.ds(0, 1)], s.first))
    stores.append(store(6, s.vectors.at[pl.ds(8, 1)], s.second))
    stores[-2].start()
    stores[-1].start()
    for one in stores:
        one.wait()

    @pl.loop(0, 4)
    def _(u):
        for one in chunk_stores(u):
            one.wait()


SPREAD_OUTS = {
    "rows_out": ((1, 2, SEQ, DIM), BF),
    "dx_out": ((1, 2, SEQ, DIM), F32),
    "first": ((1, DIM), F32),
    "query": ((1, DIM, DIM), F32),
    "key": ((1, DIM, DIM), F32),
    "value": ((1, DIM, DIM), F32),
    "output": ((1, DIM, DIM), F32),
    "second": ((1, DIM), F32),
    "gate": ((1, DIM, FF), F32),
    "up": ((1, DIM, FF), F32),
    "down": ((1, FF, DIM), F32),
}
SPREAD_SCRATCH = {
    "dx_wide": pltpu.VMEM((2, SEQ, DIM), F32),
    "square": pltpu.VMEM((4, DIM, DIM), F32),
    "vectors": pltpu.VMEM((16, DIM), F32),
    "down_wide": pltpu.VMEM((4, CHUNK, DIM), F32),
    "gate_wide": pltpu.VMEM((4, DIM, CHUNK), F32),
    "up_wide": pltpu.VMEM((4, DIM, CHUNK), F32),
    "out_sem": pltpu.SemaphoreType.DMA((20,)),
}
SPREAD_NAMES = ["units", "rows_in", "dx_in", "gains_in", *SPREAD_OUTS, *SPREAD_SCRATCH]


def spread(units, rows_in, dx_in, gains):
    anywhere = pl.BlockSpec(memory_space=pl.ANY)
    return pl.pallas_call(
        spread_kernel,
        in_specs=[pl.BlockSpec(memory_space=pltpu.VMEM)] * 4,
        out_specs=[anywhere] * len(SPREAD_OUTS),
        out_shape=[jax.ShapeDtypeStruct(*shape) for shape in SPREAD_OUTS.values()],
        scratch_shapes=list(SPREAD_SCRATCH.values()),
        compiler_params=pltpu.CompilerParams(vmem_limit_bytes=40 * 2**20),
    )(units, rows_in, dx_in, gains)


def layers(tokens, sample_ids, cotangent, *weights):
    anywhere = pl.BlockSpec(memory_space=pl.ANY)
    vmem = pl.BlockSpec(memory_space=pltpu.VMEM)
    inputs = ["tokens", "cotangent"] + ["in_" + name for name in WEIGHTS] + ["sample_ids"]
    outputs = {
        "grads_out": pltpu.VMEM((UNITS // 2, UNIT, 128), BF),
        "rows_out": pltpu.VMEM((2, SEQ, DIM), BF),
        "dx_out": pltpu.VMEM((2, SEQ, DIM), BF),
        "gains_out": pltpu.VMEM((8, 128), F32),
    }
    dma = pltpu.SemaphoreType.DMA
    scratch = {
        "tok": pltpu.VMEM((SEQ, DIM), BF),
        "cot": pltpu.VMEM((SEQ, DIM), BF),
        "gain1": pltpu.VMEM((2, 1, DIM), F32),
        "gain2": pltpu.VMEM((2, 1, DIM), F32),
        "wqkv": pltpu.VMEM((2, DIM, 3 * DIM), BF),
        "wo": pltpu.VMEM((2, DIM, DIM), BF),
        "wg": pltpu.VMEM((2, DIM, FF), BF),
        "wu": pltpu.VMEM((2, DIM, FF), BF),
        "wd": pltpu.VMEM((2, FF, DIM), BF),
        "perm": pltpu.VMEM((SEQ, SEQ), BF),
        "back": pltpu.VMEM((SEQ, SEQ), BF),
        "mask": pltpu.VMEM((HALF, HALF), F32),
        "x": pltpu.VMEM((2, SEQ, DIM), BF),
        "a": pltpu.VMEM((2, SEQ, DIM), BF),
        "qkv": pltpu.VMEM((2, SEQ, 3 * DIM), BF),
        "score": pltpu.VMEM((2 * HEADS, HALF, HALF), F32),
        "e": pltpu.VMEM((2, 2 * HEADS, HALF, HALF), BF),
        "inverse": pltpu.VMEM((2, HEADS, HALF, 128), F32),
        "f": pltpu.VMEM((SEQ, FF), BF),
        "o": pltpu.VMEM((2, SEQ, DIM), BF),
        "x1": pltpu.VMEM((2, SEQ, DIM), F32),
        "b": pltpu.VMEM((2, SEQ, DIM), BF),
        "r1": pltpu.VMEM((2, SEQ, 1), F32),
        "r2": pltpu.VMEM((2, SEQ, 1), F32),
        "acc": pltpu.VMEM((SEQ, DIM), F32),
        "bt": pltpu.VMEM((DIM, SEQ), BF),
        "at": pltpu.VMEM((DIM, SEQ), BF),
        "db": pltpu.VMEM((SEQ, DIM), F32),
        "dy": pltpu.VMEM((SEQ, DIM), BF),
        "dx1": pltpu.VMEM((SEQ, DIM), F32),
        "dx": pltpu.VMEM((2, SEQ, DIM), BF),
        "y": pltpu.VMEM((SEQ, DIM), BF),
        "do": pltpu.VMEM((SEQ, DIM), BF),
        "dqkv": pltpu.VMEM((SEQ, 3 * DIM), BF),
        "y_row": pltpu.VMEM((2, SEQ, DIM), BF),
        "dx_row": pltpu.VMEM((2, SEQ, DIM), BF),
        "own": pltpu.VMEM((UNITS, UNIT, 128), BF),
        "part": pltpu.VMEM((UNITS, SHARE, 128), BF),
        "land": pltpu.VMEM((UNITS, LAND_ROWS, 128), BF),
        "done": pltpu.VMEM((UNITS, SHARE, 128), BF),
        "gain_sum": pltpu.VMEM((6, 16, 128), F32),
        "gain_land": pltpu.VMEM((5, 16, 128), F32),
        "in_sem": dma((2,)),
        "w_sem": dma((2, len(HANDED))),
        "w_send": dma((len(HANDED),)),
        "sent": dma,
        "recv": dma((UNITS, STAGES - 1)),
        "core_sent": dma,
        "core_recv": dma((UNITS,)),
        "out_sent": dma,
        "out_recv": dma,
        "gain_send": dma,
        "gain_recv": dma((5,)),
        "y_sem": dma((3,)),
        "dx_sem": dma((3,)),
    }
    names = inputs + list(outputs) + list(scratch)
    return pl.pallas_call(
        functools.partial(kernel, names),
        out_shape=list(outputs.values()),
        in_specs=[anywhere] * (len(inputs) - 1) + [vmem],
        out_specs=[anywhere, anywhere, anywhere, vmem],
        scratch_shapes=list(scratch.values()),
        compiler_params=pltpu.CompilerParams(
            collective_id=0, has_side_effects=True, vmem_limit_bytes=54 * 2**20
        ),
        cost_estimate=pl.CostEstimate(flops=15 * 10**9, bytes_accessed=10**7, transcendentals=4 * 10**6),
    )(tokens, cotangent, *weights, sample_ids)


def solution(mesh):
    count = mesh.shape["dp"]

    def per_device(tokens, sample_ids, cotangent, *weights):
        units, rows_out, dx_out, gains = layers(tokens, sample_ids, cotangent, *weights)
        outs = spread(units, rows_out, dx_out, gains)
        if count > GROUP:
            members = [[g * GROUP + i for g in range(count // GROUP)] for i in range(GROUP)]
            outs = list(outs[:2]) + list(lax.psum(tuple(outs[2:]), "dp", axis_index_groups=members))
        return tuple(outs)

    matrix = P("section", None, None)
    vector = P("section", None)
    rows4 = P("section", "dp", None, None)
    grads = (vector, matrix, matrix, matrix, matrix, vector, matrix, matrix, matrix)
    return jax.shard_map(
        per_device,
        mesh=mesh,
        in_specs=(P("dp", None, None), P("dp", None), P("dp", None, None)) + grads,
        out_specs=(rows4, rows4) + grads,
        check_vma=False,
    )
```
